32 devices in a mesh: groups: 2 (over y), batch: 4 (over z), proto: 2 (over x), sub: 2 (over core).
Axes of the slice: x: 2, y: 2, z: 4, core: 2. Of those that a mesh axis runs over, the one named last changes fastest.
Arguments:
- embeddings: bfloat16 [8192, 512], P(('groups', 'batch', 'proto', 'sub')), parts along dimension 0, may hold values from -48 to 48, as said below
- prototypes: bfloat16 [65536, 512], P(('groups', 'proto', 'sub')), parts along dimension 0, may hold values from -48 to 48, as said below
- crop_image: int32 [8192], P(('groups', 'batch')), parts along dimension 0, may hold values from 0 to 511, as said below
- crop_view: int32 [8192], P(('groups', 'batch')), parts along dimension 0, may hold values from 0 to 1, as said below
Outputs:
- crop_loss: float32 [8192], P(('groups', 'batch')), parts along dimension 0
- proto_grad: float32 [512, 65536], P('batch', ('groups', 'proto', 'sub')), parts along dimension 1
The draws below stay inside these ranges and needn't reach their ends.
There are 2 independent parts, one for each index of `groups`. The reference program is written for one: setup_inputs(seed, part) draws one part's arguments, and reference() takes and returns one part's arrays. A program takes and returns all parts, laid end to end along the dimension named above; each array names one. Nothing has to cross between parts.
Inputs may be any that keep to these rules, and one draw needn't show every extreme that they name: `embeddings`: row scales differ widely from row to row. `prototypes`: row scales differ widely from row to row. `crop_image`: every image has exactly 8 crops, all among the 1024 rows of one index b of batch, and those rows hold exactly the images b * 128 to b * 128 + 127. `crop_view`: every image has exactly 2 global crops.
All inputs are finite; a program needn't handle non-finite values.
Results may differ from the reference program's by a relative error of at most 0.0043.
Values may be sent and summed in bfloat16 or wider, within the bound.
No kernel may reach another device: no remote copies, remote signals or barrier semaphores. Data moves between devices by JAX's collectives and lax.ppermute only.
A program may use at most 256 MiB of HBM per device.

```python
import math
import jax
import jax.numpy as jnp
from jax import lax

D = 512
K = 32768
TOK_DEV = 1024
CROPS = 8
GLOBALS = 2
ITERS = 3
IMG_DEV = 128
TOKENS = 4096
IMAGES = 512
N_BATCH = 4


def crop_slots(key):
    blocks = TOKENS // TOK_DEV
    keys = jax.random.split(key, blocks)
    return jax.vmap(lambda single: jax.random.permutation(single, TOK_DEV))(keys).astype(jnp.int32)


def crop_images(key):
    slots = crop_slots(key)
    starts = jnp.arange(slots.shape[0], dtype=jnp.int32)[:, None] * (TOK_DEV // CROPS)
    return (starts + slots // CROPS).reshape(-1).astype(jnp.int32)


def cluster_centers(key):
    clusters = K // 64
    base = jax.random.normal(jax.random.fold_in(key, 101), (clusters, D), jnp.float32)
    return jnp.clip(base, -3.0, 3.0)


def image_clusters(key):
    clusters = K // 64
    picks = jax.random.randint(jax.random.fold_in(key, 103), (3, IMAGES), 0, clusters)
    return jnp.min(picks, axis=0).astype(jnp.int32)


def proto_clusters(key):
    clusters = K // 64
    return jax.random.randint(jax.random.fold_in(key, 107), (K,), 0, clusters).astype(jnp.int32)


def draw_crop_image(key, part):
    return crop_images(key)


def draw_crop_view(key, part):
    slots = crop_slots(key)
    return (slots % CROPS < GLOBALS).astype(jnp.int32).reshape(-1)


def draw_embeddings(key, part):
    centers = cluster_centers(key)
    owner = image_clusters(key)
    images = crop_images(key)
    key = jax.random.fold_in(key, 11)
    first = jax.random.fold_in(key, 0)
    second = jax.random.fold_in(key, 1)
    fourth = jax.random.fold_in(key, 3)
    scales = jnp.exp(jax.random.uniform(second, (TOKENS, 1), jnp.float32, 0.0, math.log(10.0)))
    pull = jax.random.uniform(fourth, (TOKENS, 1), jnp.float32, 0.5, 2.0)
    noise = jnp.clip(jax.random.normal(first, (TOKENS, D), jnp.float32), -3.0, 3.0)
    base = (pull * centers[owner[images]] + noise) / jnp.sqrt(pull * pull + 1.0)
    return (base * scales).astype(jnp.bfloat16)


def draw_prototypes(key, part):
    centers = cluster_centers(key)
    owner = proto_clusters(key)
    key = jax.random.fold_in(key, 23)
    first = jax.random.fold_in(key, 0)
    second = jax.random.fold_in(key, 1)
    fourth = jax.random.fold_in(key, 3)
    scales = jnp.exp(jax.random.uniform(second, (K, 1), jnp.float32, 0.0, math.log(10.0)))
    pull = jax.random.uniform(fourth, (K, 1), jnp.float32, 0.0, 2.0)
    noise = jnp.clip(jax.random.normal(first, (K, D), jnp.float32), -3.0, 3.0)
    base = (pull * centers[owner] + noise) / jnp.sqrt(pull * pull + 1.0)
    return (base * scales).astype(jnp.bfloat16)


def setup_inputs(seed: int = 0, part: int = 0) -> dict:
    arg_keys = jax.random.split(jax.random.key(seed), 5)
    part_keys = jax.random.split(jax.random.fold_in(arg_keys[4], part), 5)
    embeddings = draw_embeddings(jax.random.fold_in(jax.random.fold_in(arg_keys[4], part), 71), part)
    prototypes = draw_prototypes(jax.random.fold_in(jax.random.fold_in(arg_keys[4], part), 71), part)
    crop_image = draw_crop_image(jax.random.fold_in(jax.random.fold_in(arg_keys[4], part), 71), part)
    crop_view = draw_crop_view(jax.random.fold_in(jax.random.fold_in(arg_keys[4], part), 71), part)
    return {"embeddings": embeddings, "prototypes": prototypes, "crop_image": crop_image, "crop_view": crop_view}


sharpen = 0.05
temper = 0.1

def unit_rows(values):
    wide = values.astype(jnp.float32)
    factor = lax.rsqrt(lax.optimization_barrier(jnp.mean(wide * wide, axis=-1, keepdims=True)) + 1e-06) / math.sqrt(values.shape[-1])
    return (wide * factor).astype(jnp.bfloat16)

def reference(embeddings, prototypes, crop_image, crop_view):
    unit_z = unit_rows(embeddings).reshape(N_BATCH, TOK_DEV, D)
    unit_c = unit_rows(prototypes)
    glob = crop_view.astype(jnp.float32).reshape(N_BATCH, TOK_DEV)
    image = crop_image.reshape(N_BATCH, TOK_DEV)
    block_ids = jnp.arange(N_BATCH, dtype=jnp.int32)

    def scores_of(rows):
        return lax.dot_general(rows, unit_c, (((1,), (1,)), ((), ())), preferred_element_type=jnp.float32)

    def sharp_of(rows):
        return jnp.exp(scores_of(rows) / sharpen).astype(jnp.bfloat16)

    def column_pass(row_scale):

        def step(total, block):
            rows, weight, scale = block
            sharp = sharp_of(rows)
            mixed = (weight * scale).astype(jnp.bfloat16)
            return (total + jnp.dot(mixed, sharp, preferred_element_type=jnp.float32), None)
        total, unused = lax.scan(step, jnp.zeros((K,), jnp.float32), (unit_z, glob, row_scale))
        return 1.0 / total

    def row_pass(col_scale):
        narrow = col_scale.astype(jnp.bfloat16)

        def one(rows):
            return jnp.dot(sharp_of(rows), narrow, preferred_element_type=jnp.float32)
        return 1.0 / lax.map(one, unit_z)
    row_scale = jnp.ones((N_BATCH, TOK_DEV), jnp.float32)
    col_scale = jnp.ones((K,), jnp.float32)
    for step_index in range(ITERS):
        col_scale = column_pass(row_scale)
        row_scale = row_pass(col_scale)

    def final(grad, block):
        rows, weight, scale, images, index = block
        scores = scores_of(rows)
        sharp = jnp.exp(scores / sharpen).astype(jnp.bfloat16)
        power = jnp.exp(scores / temper)
        totals = lax.optimization_barrier(jnp.sum(power, axis=1))
        codes = ((weight * scale)[:, None] * sharp.astype(jnp.float32) * col_scale[None, :]).astype(jnp.bfloat16)
        local = (images - index * IMG_DEV).astype(jnp.int32)
        onehot = (local[:, None] == jnp.arange(IMG_DEV, dtype=jnp.int32)[None, :]).astype(jnp.bfloat16)
        image_codes = lax.dot_general(onehot, codes, (((0,), (0,)), ((), ())), preferred_element_type=jnp.float32)
        target = jnp.take(image_codes, local, axis=0) - codes.astype(jnp.float32)
        logs = scores / temper - jnp.log(totals)[:, None] + math.log(K)
        loss = -lax.optimization_barrier(jnp.sum(target * logs, axis=1))
        resid = (((GLOBALS - weight)[:, None] * power / totals[:, None] - target) / temper).astype(jnp.bfloat16)
        grad = grad + lax.dot_general(rows, resid, (((0,), (0,)), ((), ())), preferred_element_type=jnp.float32)
        return (grad, loss)
    grad, losses = lax.scan(final, jnp.zeros((D, K), jnp.float32), (unit_z, glob, row_scale, image, block_ids))
    return (losses.reshape(TOKENS), grad)
```

```python
import functools
import math

import jax
import jax.numpy as jnp
from jax import lax
from jax.experimental import pallas as pl
from jax.experimental.pallas import tpu as pltpu
from jax.sharding import PartitionSpec as P

K = 32768
CROPS = 8
GLOBALS = 2
ITERS = 3
PAD = 16
VMEM_LIMIT = 56 * 1024 * 1024

sharpen = 0.05
temper = 0.1

f32 = jnp.float32
bf16 = jnp.bfloat16


def params():
    return pltpu.CompilerParams(
        dimension_semantics=("arbitrary",), vmem_limit_bytes=VMEM_LIMIT
    )


def whole_spec(array):
    zeros = (0,) * array.ndim
    return pl.BlockSpec(array.shape, lambda *_: zeros)


def whole_out(shape):
    zeros = (0,) * len(shape)
    return pl.BlockSpec(shape, lambda *_: zeros)


def unit(wide):
    factor = lax.rsqrt(jnp.mean(wide * wide, axis=-1, keepdims=True) + 1e-06) / math.sqrt(
        wide.shape[-1]
    )
    return (wide * factor).astype(bf16)


def to_rows(lane_vector, width):
    return jnp.broadcast_to(lane_vector, (128, lane_vector.shape[1])).T[:, :width]


def fold(values):
    return values.reshape(values.shape[0] // 8, 8, values.shape[1]).sum(0)


def cost(flops, nbytes, trans=0):
    return pl.CostEstimate(flops=int(flops), bytes_accessed=int(nbytes), transcendentals=int(trans))


def crops_kernel(ids, emb_ref, image_ref, view_ref, out_ref):
    rows, width = emb_ref.shape
    out_ref[:rows, :] = unit(emb_ref[...].astype(f32))
    images = image_ref[pl.ds(ids[1], 1), :] - ids[0] * ids[3]
    code = (images * 2 + view_ref[pl.ds(ids[1], 1), :]).astype(f32)
    line = jnp.concatenate([code, jnp.zeros((1, width - rows), f32)], axis=1)
    out_ref[rows:, :] = jnp.broadcast_to(line, (PAD, width)).astype(bf16)


def crops(ids, emb, image, view):
    rows, width = emb.shape
    shape = (rows + PAD, width)
    return pl.pallas_call(
        crops_kernel,
        out_shape=jax.ShapeDtypeStruct(shape, bf16),
        grid_spec=pltpu.PrefetchScalarGridSpec(
            num_scalar_prefetch=1,
            grid=(1,),
            in_specs=[whole_spec(emb), whole_spec(image), whole_spec(view)],
            out_specs=whole_out(shape),
        ),
        compiler_params=params(),
        name="unit_crops",
    )(ids, emb, image, view)


def protos_kernel(ids, c_ref, out_ref):
    out_ref[...] = unit(c_ref[...].astype(f32))


def protos(ids, prototypes, parts):
    count, width = prototypes.shape
    tile = min(1024, count // parts)
    per = count // parts // tile
    return pl.pallas_call(
        protos_kernel,
        out_shape=jax.ShapeDtypeStruct((count, width), bf16),
        grid_spec=pltpu.PrefetchScalarGridSpec(
            num_scalar_prefetch=1,
            grid=(count // tile,),
            in_specs=[
                pl.BlockSpec(
                    (tile, width), lambda i, ids: (((i // per) ^ ids[2]) * per + i % per, 0)
                )
            ],
            out_specs=pl.BlockSpec((tile, width), lambda i, ids: (i, 0)),
        ),
        compiler_params=params(),
        cost_estimate=cost(4 * count * width, 4 * count * width),
        name="unit_protos",
    )(ids, prototypes)


def image_masks(code, place, images):
    view = code - 2.0 * jnp.floor(code * 0.5)
    image = (code - view) * 0.5
    row = lax.broadcasted_iota(jnp.int32, (images, code.shape[1]), 0).astype(f32)
    mine = row == image
    glob = mine & (view > 0.5)
    first = jnp.min(jnp.where(glob, place, 1e9), axis=1, keepdims=True)
    one = glob & (place == first)
    two = glob & (place != first)
    return [m.astype(f32) for m in (mine, one, two)]


def block_lines(ids, blocks, rows):
    code = jnp.concatenate([b[rows : rows + 1, :rows].astype(f32) for b in blocks], axis=1)
    lane = lax.broadcasted_iota(jnp.int32, (1, rows), 1)
    place = jnp.concatenate([lane + (j ^ ids[1]) * rows for j in range(len(blocks))], axis=1)
    return code, place.astype(f32)


def power_kernel(n, steps, images, ids, *refs):
    blocks = refs[:n]
    c_ref, power_ref, total_ref, view_ref, glob_ref, other_ref, slice_ref, z_ref, acc_ref = refs[n:]
    rows = blocks[0].shape[0] - PAD
    width = z_ref.shape[1]
    step = pl.program_id(0)

    @pl.when(step == 0)
    def prepare():
        for j in range(n):
            z_ref[j * rows : (j + 1) * rows, :] = blocks[j][:rows, :]
        code, place = block_lines(ids, blocks, rows)
        view_ref[...] = code - 2.0 * jnp.floor(code * 0.5)
        mine, one, two = image_masks(code, place, images)
        picks = jnp.concatenate([one, two], axis=0)
        others = jnp.concatenate([mine, mine], axis=0) - picks
        z = z_ref[...]
        glob_ref[...] = jnp.dot(picks.astype(bf16), z, preferred_element_type=f32).astype(bf16)
        span = other_ref.shape[1]
        feature = lax.broadcasted_iota(jnp.int32, (width, slice_ref.shape[1]), 0)
        column = lax.broadcasted_iota(jnp.int32, (width, slice_ref.shape[1]), 1)
        wanted = (ids[0] ^ (column // span)) * span + column % span
        chosen = jnp.where(feature == wanted, 1.0, 0.0).astype(bf16)
        part = jnp.dot(z, chosen, preferred_element_type=f32).astype(bf16)
        slice_ref[...] = part
        other_ref[...] = jnp.dot(others.astype(bf16), part[:, :span], preferred_element_type=f32)
        acc_ref[...] = jnp.zeros_like(acc_ref)

    chunk = min(128, c_ref.shape[0])
    for j in range(c_ref.shape[0] // chunk):
        at = slice(j * chunk, (j + 1) * chunk)
        scores = lax.dot_general(
            c_ref[at, :], z_ref[...], (((1,), (1,)), ((), ())), preferred_element_type=f32
        )
        power = jnp.exp(scores * (1.0 / temper))
        power_ref[at, :] = power.astype(bf16)
        acc_ref[...] += fold(power)

    @pl.when(step == steps - 1)
    def finish():
        total_ref[...] = jnp.sum(acc_ref[...], axis=0, keepdims=True)


def powers(ids, blocks, unit_c, count, images, span, parts):
    n = len(blocks)
    rows, width = blocks[0].shape[0] - PAD, blocks[0].shape[1]
    crops_all = n * rows
    tile = min(512, count)
    steps = count // tile
    shapes = [
        ((count, crops_all), bf16),
        ((1, crops_all), f32),
        ((1, crops_all), f32),
        ((2 * images, width), bf16),
        ((2 * images, span), f32),
        ((crops_all, parts * span), bf16),
    ]
    return pl.pallas_call(
        functools.partial(power_kernel, n, steps, images),
        out_shape=[jax.ShapeDtypeStruct(s, d) for s, d in shapes],
        grid_spec=pltpu.PrefetchScalarGridSpec(
            num_scalar_prefetch=1,
            grid=(steps,),
            in_specs=[whole_spec(b) for b in blocks]
            + [pl.BlockSpec((tile, width), lambda i, ids: (i, 0))],
            out_specs=[pl.BlockSpec((tile, crops_all), lambda i, ids: (i, 0))]
            + [whole_out(s) for s, _ in shapes[1:]],
            scratch_shapes=[pltpu.VMEM((crops_all, width), bf16), pltpu.VMEM((8, crops_all), f32)],
        ),
        compiler_params=params(),
        cost_estimate=cost(
            2 * crops_all * count * width, 2 * count * (crops_all + width), crops_all * count
        ),
        name="softmax_powers",
    )(ids, *blocks, unit_c)


def sharp_kernel(n, steps, *refs):
    globs = refs[:n]
    c_ref, sharp_ref, row_ref, z_ref, acc_ref = refs[n:]
    step = pl.program_id(0)

    @pl.when(step == 0)
    def prepare():
        rows = globs[0].shape[0]
        for j in range(n):
            z_ref[j * rows : (j + 1) * rows, :] = globs[j][...]
        acc_ref[...] = jnp.zeros_like(acc_ref)

    chunk = min(128, c_ref.shape[0])
    for j in range(c_ref.shape[0] // chunk):
        at = slice(j * chunk, (j + 1) * chunk)
        scores = lax.dot_general(
            c_ref[at, :], z_ref[...], (((1,), (1,)), ((), ())), preferred_element_type=f32
        )
        sharp = jnp.exp(scores * (1.0 / sharpen)).astype(bf16)
        sharp_ref[at, :] = sharp
        wide = sharp.astype(f32)
        col = 1.0 / jnp.sum(wide, axis=1, keepdims=True)
        acc_ref[...] += fold(wide * col.astype(bf16).astype(f32))

    @pl.when(step == steps - 1)
    def finish():
        row_ref[...] = jnp.sum(acc_ref[...], axis=0, keepdims=True)


def sharps(globs, unit_c):
    n = len(globs)
    total = sum(g.shape[0] for g in globs)
    count, width = unit_c.shape
    tile = max(64, min(512, 512 * 1024 // total))
    steps = count // tile
    return pl.pallas_call(
        functools.partial(sharp_kernel, n, steps),
        out_shape=[
            jax.ShapeDtypeStruct((count, total), bf16),
            jax.ShapeDtypeStruct((1, total), f32),
        ],
        grid=(steps,),
        in_specs=[whole_spec(g) for g in globs] + [pl.BlockSpec((tile, width), lambda i: (i, 0))],
        out_specs=[pl.BlockSpec((tile, total), lambda i: (i, 0)), whole_out((1, total))],
        scratch_shapes=[pltpu.VMEM((total, width), bf16), pltpu.VMEM((8, total), f32)],
        compiler_params=params(),
        cost_estimate=cost(
            2 * total * count * width, 2 * count * (total + width), total * count
        ),
        name="sinkhorn_first",
    )(*globs, unit_c)


def scale_pass_kernel(n, steps, final, own, *refs):
    parts = refs[:n]
    if final:
        sharp_ref, c_ref, row_ref, v_ref, mass_ref, w_ref, acc_ref, vacc_ref, macc_ref = refs[n:]
    else:
        sharp_ref, row_ref, w_ref, acc_ref = refs[n:]
    step = pl.program_id(0)

    @pl.when(step == 0)
    def prepare():
        scale = 1.0 / sum(p[...] for p in parts)
        w_ref[...] = to_rows(scale, 128).astype(bf16)
        acc_ref[...] = jnp.zeros_like(acc_ref)
        if final:
            vacc_ref[...] = jnp.zeros_like(vacc_ref)
            macc_ref[...] = jnp.zeros_like(macc_ref)

    total = sharp_ref.shape[1]
    chunk = min(128, sharp_ref.shape[0])
    for j in range(sharp_ref.shape[0] // chunk):
        at = slice(j * chunk, (j + 1) * chunk)
        sharp = sharp_ref[at, :]
        col = 1.0 / jnp.dot(sharp, w_ref[...], preferred_element_type=f32)
        narrow = col.astype(bf16).astype(f32)
        for lane in range(total // 128):
            span = slice(lane * 128, (lane + 1) * 128)
            acc_ref[:, span] += fold(sharp[:, span].astype(f32) * narrow)
        if final:
            for lane in range(own // 128):
                span = slice(lane * 128, (lane + 1) * 128)
                macc_ref[:, span] += fold(sharp[:, span].astype(f32) * col)
            scaled = (c_ref[at, :].astype(f32) * col[:, :1]).astype(bf16)
            vacc_ref[...] += lax.dot_general(
                sharp[:, :own], scaled, (((0,), (0,)), ((), ())), preferred_element_type=f32
            )

    @pl.when(step == steps - 1)
    def finish():
        row_ref[...] = jnp.sum(acc_ref[...], axis=0, keepdims=True)
        if final:
            v_ref[...] = vacc_ref[...]
            mass_ref[...] = jnp.sum(macc_ref[...], axis=0, keepdims=True)


def scale_pass(row_parts, sharp, own, unit_c=None):
    final = unit_c is not None
    count, total = sharp.shape
    tile = max(64, min(512, 512 * 1024 // total))
    steps = count // tile
    n = len(row_parts)
    tiles = pl.BlockSpec((tile, total), lambda i: (i, 0))
    out_shapes = [(1, total)]
    scratch = [pltpu.VMEM((total, 128), bf16), pltpu.VMEM((8, total), f32)]
    args = [*row_parts, sharp]
    in_specs = [whole_spec(p) for p in row_parts] + [tiles]
    if final:
        width = unit_c.shape[1]
        args.append(unit_c)
        in_specs.append(pl.BlockSpec((tile, width), lambda i: (i, 0)))
        out_shapes += [(own, width), (1, own)]
        scratch += [pltpu.VMEM((own, width), f32), pltpu.VMEM((8, own), f32)]
    return pl.pallas_call(
        functools.partial(scale_pass_kernel, n, steps, final, own),
        out_shape=[jax.ShapeDtypeStruct(s, f32) for s in out_shapes],
        grid=(steps,),
        in_specs=in_specs,
        out_specs=[whole_out(s) for s in out_shapes],
        scratch_shapes=scratch,
        compiler_params=params(),
        cost_estimate=cost(4 * total * count, 2 * total * count),
        name="sinkhorn_final" if final else "sinkhorn_pass",
    )(*args)


def push_kernel(n, parts, total_ref, view_ref, *refs):
    powers_in, slices = refs[:n], refs[n : 2 * n]
    outs, z_ref = refs[2 * n : 2 * n + parts], refs[2 * n + parts]
    rows = slices[0].shape[0]
    step = pl.program_id(0)

    @pl.when(step == 0)
    def prepare():
        for j in range(n):
            coef = (GLOBALS - view_ref[j : j + 1, :]) / total_ref[j : j + 1, :] * (1.0 / temper)
            width = slices[0].shape[1]
            tall = to_rows(coef, min(128, width))
            if width > 128:
                tall = jnp.concatenate([tall] * (width // 128), axis=1)
            z_ref[j * rows : (j + 1) * rows, :] = (slices[j][...].astype(f32) * tall).astype(bf16)

    out = jnp.dot(powers_in[0][...], z_ref[:rows, :], preferred_element_type=f32)
    for j in range(1, n):
        out += jnp.dot(
            powers_in[j][...], z_ref[j * rows : (j + 1) * rows, :], preferred_element_type=f32
        )
    span = outs[0].shape[1]
    for part, ref in enumerate(outs):
        ref[...] = out[:, part * span : (part + 1) * span].astype(ref.dtype)


def push(total, view, power_list, slices, parts):
    n = len(power_list)
    count, rows = power_list[0].shape
    width = slices[0].shape[1]
    span = width // parts
    tile = max(64, min(512, 2048 // n, count))
    return pl.pallas_call(
        functools.partial(push_kernel, n, parts),
        out_shape=[jax.ShapeDtypeStruct((count, span), bf16 if k else f32) for k in range(parts)],
        grid=(count // tile,),
        in_specs=[whole_spec(total), whole_spec(view)]
        + [pl.BlockSpec((tile, rows), lambda i: (i, 0)) for _ in power_list]
        + [whole_spec(s) for s in slices],
        out_specs=[pl.BlockSpec((tile, span), lambda i: (i, 0)) for _ in range(parts)],
        scratch_shapes=[pltpu.VMEM((n * rows, width), bf16)],
        compiler_params=params(),
        cost_estimate=cost(2 * n * rows * count * width, 2 * n * rows * count),
        name="gradient_push",
    )(total, view, *power_list, *slices)


def pull_kernel(n, m, ids, *refs):
    before, last, others = refs[:n], refs[n : 2 * n], refs[2 * n : 2 * n + m]
    sharp_ref, push_ref = refs[2 * n + m : 2 * n + m + 2]
    out_ref, w_ref = refs[-2:]
    span = push_ref.shape[1]
    step = pl.program_id(0)

    @pl.when(step == 0)
    def prepare():
        weight = 1.0 / sum(p[...] for p in before)
        scale = (1.0 / temper) / sum(p[...] for p in last)
        tall = to_rows(scale, span)
        rows = others[0].shape[0]
        for j in range(m):
            at = slice(j * rows, (j + 1) * rows)
            w_ref[at, :span] = (others[j][...] * tall[at, :]).astype(bf16)
        w_ref[:, span:] = to_rows(weight, span).astype(bf16)

    both = jnp.dot(sharp_ref[...], w_ref[...], preferred_element_type=f32)
    grad = push_ref[...].astype(f32) - both[:, :span] / both[:, span:]
    out_ref[...] = grad.T


def pull(ids, before, last, others, sharp, pushed, part, parts, carry):
    n, m = len(before), len(others)
    count, total = sharp.shape
    half, span = pushed.shape
    tile = max(128, min(512, 512 * 1024 // total))
    steps = half // tile
    args = [*before, *last, *others, sharp, pushed]
    in_specs = [whole_spec(a) for a in args[: 2 * n + m]] + [
        pl.BlockSpec((tile, total), lambda i, ids: (part * steps + i, 0)),
        pl.BlockSpec((tile, span), lambda i, ids: (i, 0)),
    ]
    aliases = {}
    kernel = functools.partial(pull_kernel, n, m)
    if carry is not None:
        aliases = {len(args) + 1: 0}
        args.append(carry)
        in_specs.append(pl.BlockSpec(memory_space=pl.ANY))
    return pl.pallas_call(
        kernel,
        out_shape=jax.ShapeDtypeStruct((span, count), f32),
        grid_spec=pltpu.PrefetchScalarGridSpec(
            num_scalar_prefetch=1,
            grid=(steps,),
            in_specs=in_specs,
            out_specs=pl.BlockSpec(
                (span, tile), lambda i, ids: (0, (part ^ ids[2]) * steps + i)
            ),
            scratch_shapes=[pltpu.VMEM((total, 2 * span), bf16)],
        ),
        input_output_aliases=aliases,
        compiler_params=params(),
        cost_estimate=cost(4 * total * half * span, 2 * total * half + 6 * half * span),
        name="gradient_pull",
    )(ids, *args)


def loss_kernel(n, m, images, ids, *refs):
    blocks, last = refs[:n], refs[n : n + m]
    v_ref, mass_ref, out_ref, z_ref = refs[n + m :]
    rows = blocks[0].shape[0] - PAD
    for j in range(n):
        z_ref[j * rows : (j + 1) * rows, :] = blocks[j][:rows, :]
    code, place = block_lines(ids, blocks, rows)
    mine, one, two = image_masks(code, place, images)
    own = 2 * images
    others = jnp.concatenate([mine, mine], axis=0) - jnp.concatenate([one, two], axis=0)
    scale = 1.0 / sum(p[:, :own] for p in last)
    tall = to_rows(scale, 128)[:, :1]
    mass = to_rows(mass_ref[...] * scale, 128)[:, :1]
    hits = lax.dot_general(
        (v_ref[...] * tall).astype(bf16),
        z_ref[...],
        (((1,), (1,)), ((), ())),
        preferred_element_type=f32,
    )
    first = jnp.sum(hits * others, axis=0, keepdims=True)
    second = jnp.sum(mass * others, axis=0, keepdims=True)
    out_ref[...] = jnp.concatenate([first, second], axis=0)


def loss_terms(ids, blocks, last, values, mass, images):
    n, m = len(blocks), len(last)
    rows, width = blocks[0].shape[0] - PAD, blocks[0].shape[1]
    args = [*blocks, *last, values, mass]
    shape = (2, n * rows)
    return pl.pallas_call(
        functools.partial(loss_kernel, n, m, images),
        out_shape=jax.ShapeDtypeStruct(shape, f32),
        grid_spec=pltpu.PrefetchScalarGridSpec(
            num_scalar_prefetch=1,
            grid=(1,),
            in_specs=[whole_spec(a) for a in args],
            out_specs=whole_out(shape),
            scratch_shapes=[pltpu.VMEM((n * rows, width), bf16)],
        ),
        compiler_params=params(),
        name="loss_terms",
    )(ids, *args)


def swap(array, axes, sizes, offset):
    size = math.prod(sizes)
    return lax.ppermute(array, axes, [(i, i ^ offset) for i in range(size)])


def reorder(array, axis, offset):
    if offset == 0:
        return array
    pieces = [
        lax.slice_in_dim(array, i ^ offset, (i ^ offset) + 1, axis=axis)
        for i in range(array.shape[axis])
    ]
    return jnp.concatenate(pieces, axis=axis)


def shards(sizes, embeddings, prototypes, crop_image, crop_view):
    n_batch, n_proto, n_sub = sizes
    n = n_proto * n_sub
    parts = 2 if n_batch % 2 == 0 else 1
    rows, width = embeddings.shape
    crops_all = crop_image.shape[0]
    images = crop_image.shape[0] // CROPS
    count = prototypes.shape[0]
    half = count // parts
    span = width // n_batch
    own = GLOBALS * images

    batch = lax.axis_index("batch")
    place = lax.axis_index("proto") * n_sub + lax.axis_index("sub")
    ids = jnp.stack([batch, place, batch % parts, jnp.int32(images)]).astype(jnp.int32)

    mine = crops(ids, embeddings, crop_image.reshape(n, rows), crop_view.reshape(n, rows))
    unit_c = protos(ids, prototypes, parts)

    blocks = []
    for k in range(n_batch):
        block = mine if k == 0 else swap(mine, "batch", (n_batch,), k)
        chips = [block] + [swap(block, "proto", (n_proto,), j) for j in range(1, n_proto)]
        blocks.append(
            [
                chip if s == 0 else swap(chip, "sub", (n_sub,), s)
                for chip in chips
                for s in range(n_sub)
            ]
        )

    found = [powers(ids, b, unit_c, half, images, span, parts) for b in blocks]
    power_list, total_list, view_list, globs, others, slices = [list(x) for x in zip(*found)]

    view = jnp.concatenate(view_list, axis=0)
    total = jnp.concatenate(total_list, axis=0).reshape(n_batch, n_proto, n_sub, rows)
    for s in range(1, n_sub):
        total = total + reorder(swap(total, "sub", (n_sub,), s), 2, s)
    if (n_proto, parts) == (2, 2):
        a = swap(total, "proto", (n_proto,), 1)
        b = swap(total, "batch", (n_batch,), 1)
        c = swap(
            total, ("batch", "proto"), (n_batch, n_proto), n_proto + 1
        )
        total = (
            total
            + reorder(a, 1, 1)
            + reorder(b, 0, 1)
            + reorder(reorder(c, 0, 1), 1, 1)
        )
    else:
        got = [reorder(swap(total, "proto", (n_proto,), j), 1, j) for j in range(1, n_proto)]
        total = total + sum(got)
        if parts == 2:
            total = total + reorder(swap(total, "batch", (n_batch,), 1), 0, 1)
    total = total.reshape(n_batch, crops_all)

    def everywhere(row):
        if n > 4:
            return [lax.psum(row, ("proto", "sub"))]
        return [row] + [swap(row, ("proto", "sub"), (n_proto, n_sub), j) for j in range(1, n)]

    pushed = push(total, view, power_list, slices, parts)
    pieces = [pushed[0]] + [swap(pushed[k], "batch", (n_batch,), k) for k in range(1, parts)]

    sharp, row = sharps(globs, unit_c)
    row_parts = everywhere(row)
    for step_index in range(ITERS - 2):
        (row,) = scale_pass(row_parts, sharp, own)
        row_parts = everywhere(row)
    before = row_parts
    row, values, mass = scale_pass(before, sharp, own, unit_c)
    last = everywhere(row)

    grad = None
    for part in range(parts):
        grad = pull(ids, before, last, others, sharp, pieces[part], part, parts, grad)

    terms = loss_terms(ids, blocks[0], last, values, mass, images)
    terms = terms.reshape(2, n_proto, n_sub, rows)
    for j in range(1, n):
        got = swap(terms, ("proto", "sub"), (n_proto, n_sub), j)
        if j == 1:
            summed = terms
        summed = summed + reorder(reorder(got, 1, j // n_sub), 2, j % n_sub)
    logs = jnp.log(total[0].reshape(n_proto, n_sub, rows)) - math.log(K)
    crop_loss = logs * summed[1] - summed[0] / temper
    for axis, name, size in ((0, "proto", n_proto), (1, "sub", n_sub)):
        index = lax.axis_index(name)
        bit = 1
        while bit < size:
            crop_loss = jnp.where((index & bit) > 0, reorder(crop_loss, axis, bit), crop_loss)
            bit *= 2
    return (crop_loss.reshape(crops_all), grad)


def solution(mesh):
    sizes = tuple(mesh.shape[a] for a in ("batch", "proto", "sub"))
    placed = (
        P(("groups", "batch", "proto", "sub"), None),
        P(("groups", "proto", "sub"), None),
        P(("groups", "batch")),
        P(("groups", "batch")),
    )
    return jax.shard_map(
        functools.partial(shards, sizes),
        mesh=mesh,
        in_specs=placed,
        out_specs=(P(("groups", "batch")), P("batch", ("groups", "proto", "sub"))),
        check_vma=False,
    )
```

```python
import functools
import math

import jax
import jax.numpy as jnp
from jax import lax
from jax.experimental import pallas as pl
from jax.experimental.pallas import tpu as pltpu
from jax.sharding import PartitionSpec as P

K = 32768
CROPS = 8
GLOBALS = 2
ITERS = 3
PAD = 16
LINES = 8
VMEM_LIMIT = 56 * 1024 * 1024

sharpen = 0.05
temper = 0.1

f32 = jnp.float32
bf16 = jnp.bfloat16


def params():
    return pltpu.CompilerParams(
        dimension_semantics=("arbitrary",), vmem_limit_bytes=VMEM_LIMIT
    )


def whole_spec(array):
    zeros = (0,) * array.ndim
    return pl.BlockSpec(array.shape, lambda *_: zeros)


def whole_out(shape):
    zeros = (0,) * len(shape)
    return pl.BlockSpec(shape, lambda *_: zeros)


def unit(wide):
    factor = lax.rsqrt(jnp.mean(wide * wide, axis=-1, keepdims=True) + 1e-06) / math.sqrt(
        wide.shape[-1]
    )
    return (wide * factor).astype(bf16)


def to_rows(lane_vector, width):
    return jnp.broadcast_to(lane_vector, (128, lane_vector.shape[1])).T[:, :width]


def fold(values):
    return values.reshape(values.shape[0] // 8, 8, values.shape[1]).sum(0)


def cost(flops, nbytes, trans=0):
    return pl.CostEstimate(flops=int(flops), bytes_accessed=int(nbytes), transcendentals=int(trans))


def crops_kernel(ids, emb_ref, image_ref, view_ref, out_ref):
    rows, width = emb_ref.shape
    out_ref[:rows, :] = unit(emb_ref[...].astype(f32))
    code = ((image_ref[...] - ids[0] * ids[3]) * 2 + view_ref[...]).astype(f32)
    code = jnp.concatenate([code, jnp.zeros((code.shape[0], width - code.shape[1]), f32)], axis=1)
    code = jnp.concatenate([code, jnp.zeros((PAD - code.shape[0], width), f32)], axis=0)
    out_ref[rows:, :] = code.astype(bf16)


def crops(ids, emb, image, view):
    rows, width = emb.shape
    shape = (rows + PAD, width)
    return pl.pallas_call(
        crops_kernel,
        out_shape=jax.ShapeDtypeStruct(shape, bf16),
        grid_spec=pltpu.PrefetchScalarGridSpec(
            num_scalar_prefetch=1,
            grid=(1,),
            in_specs=[whole_spec(emb), whole_spec(image), whole_spec(view)],
            out_specs=whole_out(shape),
        ),
        compiler_params=params(),
        name="unit_crops",
    )(ids, emb, image, view)


def protos_kernel(ids, c_ref, out_ref):
    out_ref[...] = unit(c_ref[...].astype(f32))


def protos(ids, prototypes, parts):
    count, width = prototypes.shape
    tile = min(2048, count // parts)
    per = count // parts // tile
    return pl.pallas_call(
        protos_kernel,
        out_shape=jax.ShapeDtypeStruct((count, width), bf16),
        grid_spec=pltpu.PrefetchScalarGridSpec(
            num_scalar_prefetch=1,
            grid=(count // tile,),
            in_specs=[
                pl.BlockSpec(
                    (tile, width), lambda i, ids: (((i // per) ^ ids[2]) * per + i % per, 0)
                )
            ],
            out_specs=pl.BlockSpec((tile, width), lambda i, ids: (i, 0)),
        ),
        compiler_params=params(),
        cost_estimate=cost(4 * count * width, 4 * count * width),
        name="unit_protos",
    )(ids, prototypes)


def image_masks(code, images):
    view = code - 2.0 * jnp.floor(code * 0.5)
    image = (code - view) * 0.5
    shape = (images, code.shape[1])
    row = lax.broadcasted_iota(jnp.int32, shape, 0).astype(f32)
    place = lax.broadcasted_iota(jnp.int32, shape, 1).astype(f32)
    mine = row == image
    glob = mine & (view > 0.5)
    first = jnp.min(jnp.where(glob, place, 1e9), axis=1, keepdims=True)
    one = glob & (place == first)
    two = glob & (place != first)
    return [m.astype(f32) for m in (mine, one, two)]


def code_line(lines):
    lines = lines.astype(f32)
    return jnp.concatenate([lines[j : j + 1, :] for j in range(LINES)], axis=1)


def load_blocks(ids, blocks, rows, z_ref, code_ref, sems):
    m, n = len(blocks), len(blocks[0])
    lanes = code_ref.shape[2]
    copies = []
    for k in range(m):
        for j in range(n):
            at = pl.multiple_of(k * n * rows + (j ^ ids[1]) * rows, rows)
            copies.append((blocks[k][j].at[pl.ds(0, rows), :], z_ref.at[pl.ds(at, rows), :]))
        copies.append((blocks[k][0].at[pl.ds(rows, PAD), pl.ds(0, lanes)], code_ref.at[k]))
    copies = [
        pltpu.make_async_copy(a, b, sems.at[i]) for i, (a, b) in enumerate(copies)
    ]
    for c in copies:
        c.start()
    for c in copies:
        c.wait()


def power_kernel(m, n, steps, images, ids, *refs):
    blocks = [refs[k * n : (k + 1) * n] for k in range(m)]
    refs = refs[m * n :]
    c_ref, power_ref, total_ref, view_ref, glob_ref, other_ref, slice_ref = refs[:7]
    z_ref, code_ref, acc_ref, sems = refs[7:]
    rows = blocks[0][0].shape[0] - PAD
    each = n * rows
    own = GLOBALS * images
    width = z_ref.shape[1]
    step = pl.program_id(0)

    @pl.when(step == 0)
    def prepare():
        load_blocks(ids, blocks, rows, z_ref, code_ref, sems)
        span = other_ref.shape[1]
        feature = lax.broadcasted_iota(jnp.int32, (width, slice_ref.shape[1]), 0)
        column = lax.broadcasted_iota(jnp.int32, (width, slice_ref.shape[1]), 1)
        wanted = (ids[0] ^ (column // span)) * span + column % span
        chosen = jnp.where(feature == wanted, 1.0, 0.0).astype(bf16)
        for k in range(m):
            at, to = slice(k * each, (k + 1) * each), slice(k * own, (k + 1) * own)
            code = code_line(code_ref[k])
            view_ref[:, at] = code - 2.0 * jnp.floor(code * 0.5)
            mine, one, two = image_masks(code, images)
            picks = jnp.concatenate([one, two], axis=0)
            rest = jnp.concatenate([mine, mine], axis=0) - picks
            z = z_ref[at, :]
            glob_ref[to, :] = jnp.dot(
                picks.astype(bf16), z, preferred_element_type=f32
            ).astype(bf16)
            part = jnp.dot(z, chosen, preferred_element_type=f32).astype(bf16)
            slice_ref[at, :] = part
            other_ref[to, :] = jnp.dot(
                rest.astype(bf16), part[:, :span], preferred_element_type=f32
            )
        acc_ref[...] = jnp.zeros_like(acc_ref)

    scores = lax.dot_general(
        c_ref[...], z_ref[...], (((1,), (1,)), ((), ())), preferred_element_type=f32
    )
    power = jnp.exp(scores * (1.0 / temper))
    power_ref[...] = power.astype(bf16)
    acc_ref[...] += fold(power)

    @pl.when(step == steps - 1)
    def finish():
        total_ref[...] = jnp.sum(acc_ref[...], axis=0, keepdims=True)


def powers(ids, blocks, unit_c, count, images, span, parts):
    m, n = len(blocks), len(blocks[0])
    rows, width = blocks[0][0].shape[0] - PAD, blocks[0][0].shape[1]
    crops_all = m * n * rows
    own = m * GLOBALS * images
    tile = min(512, count)
    steps = count // tile
    shapes = [
        ((count, crops_all), bf16),
        ((1, crops_all), f32),
        ((1, crops_all), f32),
        ((own, width), bf16),
        ((own, span), f32),
        ((crops_all, parts * span), bf16),
    ]
    return pl.pallas_call(
        functools.partial(power_kernel, m, n, steps, images),
        out_shape=[jax.ShapeDtypeStruct(s, d) for s, d in shapes],
        grid_spec=pltpu.PrefetchScalarGridSpec(
            num_scalar_prefetch=1,
            grid=(steps,),
            in_specs=[pl.BlockSpec(memory_space=pltpu.HBM)] * (m * n)
            + [pl.BlockSpec((tile, width), lambda i, ids: (i, 0))],
            out_specs=[pl.BlockSpec((tile, crops_all), lambda i, ids: (i, 0))]
            + [whole_out(s) for s, _ in shapes[1:]],
            scratch_shapes=[
                pltpu.VMEM((crops_all, width), bf16),
                pltpu.VMEM((m, PAD, n * rows // LINES), bf16),
                pltpu.VMEM((8, crops_all), f32),
                pltpu.SemaphoreType.DMA((m * n + m,)),
            ],
        ),
        compiler_params=params(),
        cost_estimate=cost(
            2 * crops_all * count * width, 2 * count * (crops_all + width), crops_all * count
        ),
        name="softmax_powers",
    )(ids, *[b for block in blocks for b in block], unit_c)


def flip(row, block):
    pieces = [row[:, j * block : (j + 1) * block] for j in range(row.shape[1] // block)]
    return jnp.concatenate([pieces[j ^ 1] for j in range(len(pieces))], axis=1)


def row_sum(refs, flips, block):
    return sum(flip(r[...], block) if turn else r[...] for r, turn in zip(refs, flips))


def sharp_of(c, z):
    scores = lax.dot_general(c, z, (((1,), (1,)), ((), ())), preferred_element_type=f32)
    return jnp.exp(scores * (1.0 / sharpen)).astype(bf16)


def sharp_kernel(n, steps, *refs):
    globs = refs[:n]
    c_ref, sharp_ref, row_ref, z_ref, acc_ref = refs[n:]
    step = pl.program_id(0)

    @pl.when(step == 0)
    def prepare():
        rows = globs[0].shape[0]
        for j in range(n):
            z_ref[j * rows : (j + 1) * rows, :] = globs[j][...]
        acc_ref[...] = jnp.zeros_like(acc_ref)

    chunk = min(512, c_ref.shape[0])
    for j in range(c_ref.shape[0] // chunk):
        at = slice(j * chunk, (j + 1) * chunk)
        sharp = sharp_of(c_ref[at, :], z_ref[...])
        sharp_ref[at, :] = sharp
        wide = sharp.astype(f32)
        col = 1.0 / jnp.sum(wide, axis=1, keepdims=True)
        acc_ref[...] += fold(wide * col.astype(bf16).astype(f32))

    @pl.when(step == steps - 1)
    def finish():
        row_ref[...] = jnp.sum(acc_ref[...], axis=0, keepdims=True)


def sharps(globs, unit_c, count):
    n = len(globs)
    total = sum(g.shape[0] for g in globs)
    width = unit_c.shape[1]
    tile = min(count, max(64, 1024 * 1024 // total))
    steps = count // tile
    return pl.pallas_call(
        functools.partial(sharp_kernel, n, steps),
        out_shape=[
            jax.ShapeDtypeStruct((count, total), bf16),
            jax.ShapeDtypeStruct((1, total), f32),
        ],
        grid=(steps,),
        in_specs=[whole_spec(g) for g in globs] + [pl.BlockSpec((tile, width), lambda i: (i, 0))],
        out_specs=[pl.BlockSpec((tile, total), lambda i: (i, 0)), whole_out((1, total))],
        scratch_shapes=[pltpu.VMEM((total, width), bf16), pltpu.VMEM((8, total), f32)],
        compiler_params=params(),
        cost_estimate=cost(
            2 * total * count * width, 2 * count * (total + width), total * count
        ),
        name="sinkhorn_first",
    )(*globs, unit_c)


def scale_pass_kernel(flips, steps, final, own, block, *refs):
    n = len(flips)
    parts = refs[:n]
    if final:
        sharp_ref, c_ref, row_ref, v_ref, mass_ref, w_ref, acc_ref, vacc_ref, macc_ref = refs[n:]
    else:
        sharp_ref, row_ref, w_ref, acc_ref = refs[n:]
    step = pl.program_id(0)

    @pl.when(step == 0)
    def prepare():
        scale = 1.0 / row_sum(parts, flips, block)
        w_ref[...] = to_rows(scale, 128).astype(bf16)
        acc_ref[...] = jnp.zeros_like(acc_ref)
        if final:
            vacc_ref[...] = jnp.zeros_like(vacc_ref)
            macc_ref[...] = jnp.zeros_like(macc_ref)

    total = sharp_ref.shape[1]
    chunk = min(256, sharp_ref.shape[0])
    for j in range(sharp_ref.shape[0] // chunk):
        at = slice(j * chunk, (j + 1) * chunk)
        sharp = sharp_ref[at, :]
        col = 1.0 / jnp.dot(sharp, w_ref[...], preferred_element_type=f32)
        narrow = col.astype(bf16).astype(f32)
        for lane in range(total // 128):
            span = slice(lane * 128, (lane + 1) * 128)
            acc_ref[:, span] += fold(sharp[:, span].astype(f32) * narrow)
        if final:
            for lane in range(own // 128):
                span = slice(lane * 128, (lane + 1) * 128)
                macc_ref[:, span] += fold(sharp[:, span].astype(f32) * col)
            scaled = (c_ref[at, :].astype(f32) * col[:, :1]).astype(bf16)
            vacc_ref[...] += lax.dot_general(
                sharp[:, :own], scaled, (((0,), (0,)), ((), ())), preferred_element_type=f32
            )

    @pl.when(step == steps - 1)
    def finish():
        row_ref[...] = jnp.sum(acc_ref[...], axis=0, keepdims=True)
        if final:
            v_ref[...] = vacc_ref[...]
            mass_ref[...] = jnp.sum(macc_ref[...], axis=0, keepdims=True)


def scale_pass(row_parts, flips, sharp, own, block, unit_c=None):
    final = unit_c is not None
    count, total = sharp.shape
    tile = min(count, max(64, 1024 * 1024 // total))
    steps = count // tile
    tiles = pl.BlockSpec((tile, total), lambda i: (i, 0))
    out_shapes = [(1, total)]
    scratch = [pltpu.VMEM((total, 128), bf16), pltpu.VMEM((8, total), f32)]
    args = [*row_parts, sharp]
    in_specs = [whole_spec(p) for p in row_parts] + [tiles]
    if final:
        width = unit_c.shape[1]
        args.append(unit_c)
        in_specs.append(pl.BlockSpec((tile, width), lambda i: (i, 0)))
        out_shapes += [(own, width), (1, own)]
        scratch += [pltpu.VMEM((own, width), f32), pltpu.VMEM((8, own), f32)]
    return pl.pallas_call(
        functools.partial(scale_pass_kernel, flips, steps, final, own, block),
        out_shape=[jax.ShapeDtypeStruct(s, f32) for s in out_shapes],
        grid=(steps,),
        in_specs=in_specs,
        out_specs=[whole_out(s) for s in out_shapes],
        scratch_shapes=scratch,
        compiler_params=params(),
        cost_estimate=cost(4 * total * count, 2 * total * count),
        name="sinkhorn_final" if final else "sinkhorn_pass",
    )(*args)


def push_kernel(n, flips, block, *refs):
    p = len(flips)
    totals, views, powers_in, slices = (
        refs[:p],
        refs[p : p + n],
        refs[p + n : p + 2 * n],
        refs[p + 2 * n : p + 3 * n],
    )
    sum_ref, *outs, z_ref = refs[p + 3 * n :]
    rows = slices[0].shape[0]
    step = pl.program_id(0)

    @pl.when(step == 0)
    def prepare():
        total = row_sum(totals, flips, block)
        sum_ref[...] = total
        width = slices[0].shape[1]
        for j in range(n):
            at = slice(j * rows, (j + 1) * rows)
            coef = (GLOBALS - views[j][...]) / total[:, at] * (1.0 / temper)
            tall = to_rows(coef, min(128, width))
            if width > 128:
                tall = jnp.concatenate([tall] * (width // 128), axis=1)
            z_ref[at, :] = (slices[j][...].astype(f32) * tall).astype(bf16)

    out = jnp.dot(powers_in[0][...], z_ref[:rows, :], preferred_element_type=f32)
    for j in range(1, n):
        out += jnp.dot(
            powers_in[j][...], z_ref[j * rows : (j + 1) * rows, :], preferred_element_type=f32
        )
    span = outs[0].shape[1]
    for part, ref in enumerate(outs):
        ref[...] = out[:, part * span : (part + 1) * span].astype(ref.dtype)


def push(totals, flips, block, views, power_list, slices, parts):
    n = len(power_list)
    count, rows = power_list[0].shape
    width = slices[0].shape[1]
    span = width // parts
    tile = max(64, min(1024, 4096 * 1024 // (n * rows), count))
    row = totals[0].shape
    return pl.pallas_call(
        functools.partial(push_kernel, n, flips, block),
        out_shape=[jax.ShapeDtypeStruct(row, f32)]
        + [jax.ShapeDtypeStruct((count, span), bf16 if k else f32) for k in range(parts)],
        grid=(count // tile,),
        in_specs=[whole_spec(t) for t in totals]
        + [whole_spec(v) for v in views]
        + [pl.BlockSpec((tile, rows), lambda i: (i, 0)) for _ in power_list]
        + [whole_spec(s) for s in slices],
        out_specs=[whole_out(row)]
        + [pl.BlockSpec((tile, span), lambda i: (i, 0)) for _ in range(parts)],
        scratch_shapes=[pltpu.VMEM((n * rows, width), bf16)],
        compiler_params=params(),
        cost_estimate=cost(2 * n * rows * count * width, 2 * n * rows * count),
        name="gradient_push",
    )(*totals, *views, *power_list, *slices)


def pull_kernel(flips, m, block, fresh, ids, *refs):
    n = len(flips)
    before, last, others = refs[:n], refs[n : 2 * n], refs[2 * n : 2 * n + m]
    refs = refs[2 * n + m :]
    if fresh:
        globs, (c_ref, push_ref), (w_ref, z_ref) = refs[:m], refs[m : m + 2], refs[-2:]
        out_ref = refs[-3]
    else:
        (sharp_ref, push_ref), (out_ref, w_ref) = refs[:2], refs[-2:]
    span = push_ref.shape[1]
    step = pl.program_id(0)

    @pl.when(step == 0)
    def prepare():
        weight = 1.0 / row_sum(before, flips, block)
        scale = (1.0 / temper) / row_sum(last, flips, block)
        tall = to_rows(scale, span)
        rows = others[0].shape[0]
        for j in range(m):
            at = slice(j * rows, (j + 1) * rows)
            w_ref[at, :span] = (others[j][...] * tall[at, :]).astype(bf16)
            if fresh:
                z_ref[at, :] = globs[j][...]
        w_ref[:, span:] = to_rows(weight, span).astype(bf16)

    sharp = sharp_of(c_ref[...], z_ref[...]) if fresh else sharp_ref[...]
    both = jnp.dot(sharp, w_ref[...], preferred_element_type=f32)
    grad = push_ref[...].astype(f32) - both[:, :span] / both[:, span:]
    out_ref[...] = grad.T


def pull(ids, before, last, flips, block, others, sharp, globs, unit_c, pushed, part, carry):
    n, m = len(before), len(others)
    fresh = sharp is None
    total = sum(o.shape[0] for o in others)
    count, width = unit_c.shape
    half, span = pushed.shape
    tile = min(half, max(128, 1024 * 1024 // total))
    steps = half // tile
    args = [*before, *last, *others] + (list(globs) if fresh else [])
    in_specs = [whole_spec(a) for a in args]
    if fresh:
        args.append(unit_c)
        in_specs.append(pl.BlockSpec((tile, width), lambda i, ids: (part * steps + i, 0)))
    else:
        args.append(sharp)
        in_specs.append(pl.BlockSpec((tile, total), lambda i, ids: (i, 0)))
    args.append(pushed)
    in_specs.append(pl.BlockSpec((tile, span), lambda i, ids: (i, 0)))
    aliases = {}
    if carry is not None:
        aliases = {len(args) + 1: 0}
        args.append(carry)
        in_specs.append(pl.BlockSpec(memory_space=pl.ANY))
    return pl.pallas_call(
        functools.partial(pull_kernel, flips, m, block, fresh),
        out_shape=jax.ShapeDtypeStruct((span, count), f32),
        grid_spec=pltpu.PrefetchScalarGridSpec(
            num_scalar_prefetch=1,
            grid=(steps,),
            in_specs=in_specs,
            out_specs=pl.BlockSpec(
                (span, tile), lambda i, ids: (0, (part ^ ids[2]) * steps + i)
            ),
            scratch_shapes=[pltpu.VMEM((total, 2 * span), bf16)]
            + ([pltpu.VMEM((total, width), bf16)] if fresh else []),
        ),
        input_output_aliases=aliases,
        compiler_params=params(),
        cost_estimate=cost(
            4 * total * half * span + (2 * total * half * width if fresh else 0),
            2 * total * half + 6 * half * span,
        ),
        name="gradient_pull",
    )(ids, *args)


def loss_kernel(m, n, flips, images, ids, *refs):
    blocks = [refs[k * n : (k + 1) * n] for k in range(m)]
    refs = refs[m * n :]
    p = len(flips)
    last = refs[:p]
    v_ref, mass_ref, out_ref, z_ref, code_ref, sems = refs[p:]
    rows = blocks[0][0].shape[0] - PAD
    each = n * rows
    own = GLOBALS * images
    load_blocks(ids, blocks, rows, z_ref, code_ref, sems)
    scale = 1.0 / row_sum(last, flips, own)[:, : m * own]
    tall = to_rows(scale, 128)[:, :1]
    mass = to_rows(mass_ref[...] * scale, 128)[:, :1]
    values = (v_ref[...] * tall).astype(bf16)
    for k in range(m):
        at, to = slice(k * each, (k + 1) * each), slice(k * own, (k + 1) * own)
        mine, one, two = image_masks(code_line(code_ref[k]), images)
        others = jnp.concatenate([mine, mine], axis=0) - jnp.concatenate([one, two], axis=0)
        hits = lax.dot_general(
            values[to, :], z_ref[at, :], (((1,), (1,)), ((), ())), preferred_element_type=f32
        )
        first = jnp.sum(hits * others, axis=0, keepdims=True)
        second = jnp.sum(mass[to, :] * others, axis=0, keepdims=True)
        out_ref[:, at] = jnp.concatenate([first, second], axis=0)


def loss_terms(ids, blocks, last, flips, values, mass, images):
    m, n = len(blocks), len(blocks[0])
    rows, width = blocks[0][0].shape[0] - PAD, blocks[0][0].shape[1]
    args = [*last, values, mass]
    shape = (2, m * n * rows)
    return pl.pallas_call(
        functools.partial(loss_kernel, m, n, flips, images),
        out_shape=jax.ShapeDtypeStruct(shape, f32),
        grid_spec=pltpu.PrefetchScalarGridSpec(
            num_scalar_prefetch=1,
            grid=(1,),
            in_specs=[pl.BlockSpec(memory_space=pltpu.HBM)] * (m * n)
            + [whole_spec(a) for a in args],
            out_specs=whole_out(shape),
            scratch_shapes=[
                pltpu.VMEM((m * n * rows, width), bf16),
                pltpu.VMEM((m, PAD, n * rows // LINES), bf16),
                pltpu.SemaphoreType.DMA((m * n + m,)),
            ],
        ),
        compiler_params=params(),
        name="loss_terms",
    )(ids, *[b for block in blocks for b in block], *args)


def swap(array, axes, sizes, offset):
    size = math.prod(sizes)
    return lax.ppermute(array, axes, [(i, i ^ offset) for i in range(size)])


def shards(sizes, embeddings, prototypes, crop_image, crop_view):
    n_batch, n_proto, n_sub = sizes
    n = n_proto * n_sub
    parts = 2
    width = embeddings.shape[1]
    crops_all = crop_image.shape[0]
    images = crop_image.shape[0] // CROPS
    count = prototypes.shape[0]
    half = count // parts
    span = width // n_batch
    own = GLOBALS * images

    batch = lax.axis_index("batch")
    place = lax.axis_index("proto") * n_sub + lax.axis_index("sub")
    ids = jnp.stack([batch, place, batch % parts, jnp.int32(images)]).astype(jnp.int32)

    lines = (LINES, crops_all // LINES)
    mine = crops(ids, embeddings, crop_image.reshape(lines), crop_view.reshape(lines))
    unit_c = protos(ids, prototypes, parts)

    blocks = []
    for k in range(n_batch):
        block = mine if k == 0 else swap(mine, "batch", (n_batch,), k)
        chips = [block] + [swap(block, "proto", (n_proto,), j) for j in range(1, n_proto)]
        blocks.append(
            [
                chip if s == 0 else swap(chip, "sub", (n_sub,), s)
                for chip in chips
                for s in range(n_sub)
            ]
        )

    found = [
        powers(ids, blocks[k : k + 2], unit_c, half, images, span, parts)
        for k in range(0, n_batch, 2)
    ]
    power_list, total_list, views, globs, others, slices = [list(x) for x in zip(*found)]

    flips = (False, False, True, True) if n_proto == 2 else (False, True)

    def everywhere(row):
        if n_proto != 2 or n_sub != 2:
            row = lax.psum(row, ("proto", "sub"))
            return [row, swap(row, "batch", (n_batch,), 1)]
        row = row + swap(row, "sub", (n_sub,), 1)
        sizes = (n_batch, n_proto)
        return [row] + [swap(row, ("batch", "proto"), sizes, j) for j in (1, n_proto, n_proto + 1)]

    totals = everywhere(jnp.concatenate(total_list, axis=1))
    total, *pushed = push(totals, flips, crops_all, views, power_list, slices, parts)
    pieces = [pushed[0], swap(pushed[1], "batch", (n_batch,), 1)]

    sharp, row = sharps(globs, unit_c, half)
    row_parts = everywhere(row)
    for step_index in range(ITERS - 2):
        (row,) = scale_pass(row_parts, flips, sharp, parts * own, own)
        row_parts = everywhere(row)
    before = row_parts
    row, values, mass = scale_pass(before, flips, sharp, parts * own, own, unit_c)
    last = everywhere(row)

    grad = None
    for part in range(parts):
        grad = pull(
            ids, before, last, flips, own, others, None if part else sharp, globs, unit_c,
            pieces[part], part, grad,
        )

    terms = loss_terms(ids, blocks[:parts], last, flips, values, mass, images)
    found = everywhere(terms)
    summed = sum(
        t[:, crops_all:] if turn else t[:, :crops_all] for t, turn in zip(found, flips)
    )
    logs = jnp.log(total[0, :crops_all]) - math.log(K)
    crop_loss = logs * summed[1] - summed[0] / temper
    return (crop_loss, grad)


def solution(mesh):
    sizes = tuple(mesh.shape[a] for a in ("batch", "proto", "sub"))
    placed = (
        P(("groups", "batch", "proto", "sub"), None),
        P(("groups", "proto", "sub"), None),
        P(("groups", "batch")),
        P(("groups", "batch")),
    )
    return jax.shard_map(
        functools.partial(shards, sizes),
        mesh=mesh,
        in_specs=placed,
        out_specs=(P(("groups", "batch")), P("batch", ("groups", "proto", "sub"))),
        check_vma=False,
    )
```

```python
import functools
import math

import jax
import jax.numpy as jnp
from jax import lax
from jax.experimental import pallas as pl
from jax.experimental.pallas import tpu as pltpu
from jax.sharding import PartitionSpec as P

K = 32768
CROPS = 8
GLOBALS = 2
ITERS = 3
PAD = 16
LINES = 8
VMEM_LIMIT = 56 * 1024 * 1024

sharpen = 0.05
temper = 0.1

f32 = jnp.float32
bf16 = jnp.bfloat16


def params():
    return pltpu.CompilerParams(
        dimension_semantics=("arbitrary",), vmem_limit_bytes=VMEM_LIMIT
    )


def whole_spec(array):
    zeros = (0,) * array.ndim
    return pl.BlockSpec(array.shape, lambda *_: zeros)


def whole_out(shape):
    zeros = (0,) * len(shape)
    return pl.BlockSpec(shape, lambda *_: zeros)


def unit(wide):
    factor = lax.rsqrt(jnp.mean(wide * wide, axis=-1, keepdims=True) + 1e-06) / math.sqrt(
        wide.shape[-1]
    )
    return (wide * factor).astype(bf16)


def to_rows(lane_vector, width):
    return jnp.broadcast_to(lane_vector, (128, lane_vector.shape[1])).T[:, :width]


def fold(values):
    return values.reshape(values.shape[0] // 8, 8, values.shape[1]).sum(0)


def cost(flops, nbytes, trans=0):
    return pl.CostEstimate(flops=int(flops), bytes_accessed=int(nbytes), transcendentals=int(trans))


def crops_kernel(ids, emb_ref, image_ref, view_ref, out_ref):
    rows, width = emb_ref.shape
    out_ref[:rows, :] = unit(emb_ref[...].astype(f32))
    code = ((image_ref[...] - ids[0] * ids[3]) * 2 + view_ref[...]).astype(f32)
    code = jnp.concatenate([code, jnp.zeros((code.shape[0], width - code.shape[1]), f32)], axis=1)
    code = jnp.concatenate([code, jnp.zeros((PAD - code.shape[0], width), f32)], axis=0)
    out_ref[rows:, :] = code.astype(bf16)


def crops(ids, emb, image, view):
    rows, width = emb.shape
    shape = (rows + PAD, width)
    return pl.pallas_call(
        crops_kernel,
        out_shape=jax.ShapeDtypeStruct(shape, bf16),
        grid_spec=pltpu.PrefetchScalarGridSpec(
            num_scalar_prefetch=1,
            grid=(1,),
            in_specs=[whole_spec(emb), whole_spec(image), whole_spec(view)],
            out_specs=whole_out(shape),
        ),
        compiler_params=params(),
        name="unit_crops",
    )(ids, emb, image, view)


def protos_kernel(ids, c_ref, out_ref):
    out_ref[...] = unit(c_ref[...].astype(f32))


def protos(ids, prototypes, parts):
    count, width = prototypes.shape
    tile = min(2048, count // parts)
    per = count // parts // tile
    return pl.pallas_call(
        protos_kernel,
        out_shape=jax.ShapeDtypeStruct((count, width), bf16),
        grid_spec=pltpu.PrefetchScalarGridSpec(
            num_scalar_prefetch=1,
            grid=(count // tile,),
            in_specs=[
                pl.BlockSpec(
                    (tile, width), lambda i, ids: (((i // per) ^ ids[2]) * per + i % per, 0)
                )
            ],
            out_specs=pl.BlockSpec((tile, width), lambda i, ids: (i, 0)),
        ),
        compiler_params=params(),
        cost_estimate=cost(4 * count * width, 4 * count * width),
        name="unit_protos",
    )(ids, prototypes)


def image_masks(code, images):
    view = code - 2.0 * jnp.floor(code * 0.5)
    image = (code - view) * 0.5
    shape = (images, code.shape[1])
    row = lax.broadcasted_iota(jnp.int32, shape, 0).astype(f32)
    place = lax.broadcasted_iota(jnp.int32, shape, 1).astype(f32)
    mine = row == image
    glob = mine & (view > 0.5)
    first = jnp.min(jnp.where(glob, place, 1e9), axis=1, keepdims=True)
    one = glob & (place == first)
    two = glob & (place != first)
    return [m.astype(f32) for m in (mine, one, two)]


def code_line(lines):
    lines = lines.astype(f32)
    return jnp.concatenate([lines[j : j + 1, :] for j in range(LINES)], axis=1)


def block_copies(ids, blocks, rows, z_ref, code_ref, sems):
    m, n = len(blocks), len(blocks[0])
    lanes = code_ref.shape[2]
    copies = []
    for k in range(m):
        for j in range(n):
            at = pl.multiple_of(k * n * rows + (j ^ ids[1]) * rows, rows)
            copies.append((blocks[k][j].at[pl.ds(0, rows), :], z_ref.at[pl.ds(at, rows), :]))
        copies.append((blocks[k][0].at[pl.ds(rows, PAD), pl.ds(0, lanes)], code_ref.at[k]))
    return [pltpu.make_async_copy(a, b, sems.at[i]) for i, (a, b) in enumerate(copies)]


def load_blocks(*args):
    copies = block_copies(*args)
    for c in copies:
        c.start()
    for c in copies:
        c.wait()


def power_kernel(m, n, early, last, steps, images, ids, *refs):
    blocks = [refs[k * n : (k + 1) * n] for k in range(m)]
    refs = refs[m * n :]
    ready, c_ref, refs = refs[:early], refs[early], refs[early + 1 :]
    power_ref, total_ref, view_ref, other_ref, slice_ref, glob_ref = refs[:6]
    refs = refs[6:]
    if last:
        sharp_ref, row_ref, *refs = refs
        z_ref, code_ref, acc_ref, sems, racc_ref = refs
    else:
        z_ref, code_ref, acc_ref, sems = refs
    rows = blocks[0][0].shape[0] - PAD
    each = n * rows
    own = GLOBALS * images
    width = z_ref.shape[1]
    step = pl.program_id(0)

    @pl.when(step == 0)
    def prepare():
        load_blocks(ids, blocks, rows, z_ref, code_ref, sems)
        span = other_ref.shape[1]
        feature = lax.broadcasted_iota(jnp.int32, (width, slice_ref.shape[1]), 0)
        column = lax.broadcasted_iota(jnp.int32, (width, slice_ref.shape[1]), 1)
        wanted = (ids[0] ^ (column // span)) * span + column % span
        chosen = jnp.where(feature == wanted, 1.0, 0.0).astype(bf16)
        base = 0
        for r in ready:
            glob_ref[base : base + r.shape[0], :] = r[...]
            base += r.shape[0]
        for k in range(m):
            at, to = slice(k * each, (k + 1) * each), slice(k * own, (k + 1) * own)
            code = code_line(code_ref[k])
            view_ref[:, at] = code - 2.0 * jnp.floor(code * 0.5)
            mine, one, two = image_masks(code, images)
            picks = jnp.concatenate([one, two], axis=0)
            rest = jnp.concatenate([mine, mine], axis=0) - picks
            z = z_ref[at, :]
            glob_ref[base + k * own : base + (k + 1) * own, :] = jnp.dot(
                picks.astype(bf16), z, preferred_element_type=f32
            ).astype(bf16)
            part = jnp.dot(z, chosen, preferred_element_type=f32).astype(bf16)
            slice_ref[at, :] = part
            other_ref[to, :] = jnp.dot(
                rest.astype(bf16), part[:, :span], preferred_element_type=f32
            )
        acc_ref[...] = jnp.zeros_like(acc_ref)
        if last:
            racc_ref[...] = jnp.zeros_like(racc_ref)

    scores = lax.dot_general(
        c_ref[...], z_ref[...], (((1,), (1,)), ((), ())), preferred_element_type=f32
    )
    power = jnp.exp(scores * (1.0 / temper))
    power_ref[...] = power.astype(bf16)
    acc_ref[...] += fold(power)
    if last:
        sharp = sharp_of(c_ref[...], glob_ref[...])
        sharp_ref[...] = sharp
        wide = sharp.astype(f32)
        col = 1.0 / jnp.sum(wide, axis=1, keepdims=True)
        racc_ref[...] += fold(wide * col.astype(bf16).astype(f32))

    @pl.when(step == steps - 1)
    def finish():
        total_ref[...] = jnp.sum(acc_ref[...], axis=0, keepdims=True)
        if last:
            row_ref[...] = jnp.sum(racc_ref[...], axis=0, keepdims=True)


def powers(ids, blocks, ready, last, unit_c, count, images, span, parts):
    m, n = len(blocks), len(blocks[0])
    rows, width = blocks[0][0].shape[0] - PAD, blocks[0][0].shape[1]
    crops_all = m * n * rows
    own = m * GLOBALS * images
    globs = own + sum(r.shape[0] for r in ready)
    tile = min(512, count, max(64, 2048 * 1024 // (crops_all + globs) // 64 * 64))
    while count % tile:
        tile -= 64
    steps = count // tile
    shapes = [
        ((count, crops_all), bf16),
        ((1, crops_all), f32),
        ((1, crops_all), f32),
        ((own, span), f32),
        ((crops_all, parts * span), bf16),
        ((globs, width), bf16),
    ]
    out_specs = [pl.BlockSpec((tile, crops_all), lambda i, ids: (i, 0))]
    out_specs += [whole_out(s) for s, _ in shapes[1:]]
    scratch = [
        pltpu.VMEM((crops_all, width), bf16),
        pltpu.VMEM((m, PAD, n * rows // LINES), bf16),
        pltpu.VMEM((8, crops_all), f32),
        pltpu.SemaphoreType.DMA((m * n + m,)),
    ]
    if last:
        shapes += [((count, globs), bf16), ((1, globs), f32)]
        out_specs += [
            pl.BlockSpec((tile, globs), lambda i, ids: (i, 0)),
            whole_out((1, globs)),
        ]
        scratch.append(pltpu.VMEM((8, globs), f32))
    columns = crops_all + (globs if last else 0)
    return pl.pallas_call(
        functools.partial(power_kernel, m, n, len(ready), last, steps, images),
        out_shape=[jax.ShapeDtypeStruct(s, d) for s, d in shapes],
        grid_spec=pltpu.PrefetchScalarGridSpec(
            num_scalar_prefetch=1,
            grid=(steps,),
            in_specs=[pl.BlockSpec(memory_space=pltpu.HBM)] * (m * n)
            + [whole_spec(r) for r in ready]
            + [pl.BlockSpec((tile, width), lambda i, ids: (i, 0))],
            out_specs=out_specs,
            scratch_shapes=scratch,
        ),
        compiler_params=params(),
        cost_estimate=cost(
            2 * columns * count * width, 2 * count * (columns + width), columns * count
        ),
        name="softmax_powers",
    )(ids, *[b for block in blocks for b in block], *ready, unit_c)


def flip(row, block):
    pieces = [row[:, j * block : (j + 1) * block] for j in range(row.shape[1] // block)]
    return jnp.concatenate([pieces[j ^ 1] for j in range(len(pieces))], axis=1)


def row_sum(refs, flips, start, size, block):
    parts = [r[:, start : start + size] for r in refs]
    return sum(flip(p, block) if turn else p for p, turn in zip(parts, flips))


def sharp_of(c, z):
    scores = lax.dot_general(c, z, (((1,), (1,)), ((), ())), preferred_element_type=f32)
    return jnp.exp(scores * (1.0 / sharpen)).astype(bf16)


def scale_pass_kernel(flips, start, steps, images, final, ids, *refs):
    p = len(flips)
    parts, sharp_ref, refs = refs[:p], refs[p], refs[p + 1 :]
    if final:
        m, n = final
        c_ref, blocks, refs = refs[0], refs[1 : 1 + m * n], refs[1 + m * n :]
        blocks = [blocks[k * n : (k + 1) * n] for k in range(m)]
        out_ref, w_ref, acc_ref, v_ref, z_ref, code_ref, sems = refs
        rows = blocks[0][0].shape[0] - PAD
    else:
        out_ref, w_ref, acc_ref = refs
    own = GLOBALS * images
    total = sharp_ref.shape[1]
    step = pl.program_id(0)

    @pl.when(step == 0)
    def prepare():
        if final:
            for c in block_copies(ids, blocks, rows, z_ref, code_ref, sems):
                c.start()
            v_ref[...] = jnp.zeros_like(v_ref)
        scale = 1.0 / row_sum(parts, flips, start, total, own)
        w_ref[...] = to_rows(scale, 128).astype(bf16)
        acc_ref[...] = jnp.zeros_like(acc_ref)

    chunk = min(256, sharp_ref.shape[0])
    for j in range(sharp_ref.shape[0] // chunk):
        at = slice(j * chunk, (j + 1) * chunk)
        sharp = sharp_ref[at, :]
        col = 1.0 / jnp.dot(sharp, w_ref[...], preferred_element_type=f32)
        narrow = col.astype(bf16).astype(f32)
        for lane in range(total // 128):
            span = slice(lane * 128, (lane + 1) * 128)
            acc_ref[:, span] += fold(sharp[:, span].astype(f32) * narrow)
        if final:
            scaled = (c_ref[at, :].astype(f32) * col[:, :1]).astype(bf16)
            v_ref[...] += lax.dot_general(
                sharp[:, : m * own], scaled, (((0,), (0,)), ((), ())), preferred_element_type=f32
            )

    @pl.when(step == steps - 1)
    def finish():
        out_ref[:, :total] = jnp.sum(acc_ref[...], axis=0, keepdims=True)
        if final:
            for c in block_copies(ids, blocks, rows, z_ref, code_ref, sems):
                c.wait()
            each = n * rows
            for k in range(m):
                at = slice(k * each, (k + 1) * each)
                mine, one, two = image_masks(code_line(code_ref[k]), images)
                hits = lax.dot_general(
                    v_ref[k * own : (k + 1) * own, :].astype(bf16),
                    z_ref[at, :],
                    (((1,), (1,)), ((), ())),
                    preferred_element_type=f32,
                )
                first = jnp.sum(hits[:images] * (mine - one), axis=0, keepdims=True)
                second = jnp.sum(hits[images:] * (mine - two), axis=0, keepdims=True)
                base = total + k * each
                out_ref[:, base : base + each] = first
                base += m * each
                out_ref[:, base : base + each] = second


def scale_pass(ids, row_parts, flips, start, sharp, images, unit_c=None, blocks=None):
    count, total = sharp.shape
    tile = min(count, max(64, 1024 * 1024 // total))
    steps = count // tile
    size = total
    scratch = [pltpu.VMEM((total, 128), bf16), pltpu.VMEM((8, total), f32)]
    args = [*row_parts, sharp]
    in_specs = [whole_spec(p) for p in row_parts]
    in_specs.append(pl.BlockSpec((tile, total), lambda i, ids: (i, 0)))
    final = None
    if unit_c is not None:
        m, n = final = len(blocks), len(blocks[0])
        rows, width = blocks[0][0].shape[0] - PAD, unit_c.shape[1]
        args += [unit_c] + [b for block in blocks for b in block]
        in_specs.append(pl.BlockSpec((tile, width), lambda i, ids: (i, 0)))
        in_specs += [pl.BlockSpec(memory_space=pltpu.HBM)] * (m * n)
        size += 2 * m * n * rows
        scratch += [
            pltpu.VMEM((m * GLOBALS * images, width), f32),
            pltpu.VMEM((m * n * rows, width), bf16),
            pltpu.VMEM((m, PAD, n * rows // LINES), bf16),
            pltpu.SemaphoreType.DMA((m * n + m,)),
        ]
    return pl.pallas_call(
        functools.partial(scale_pass_kernel, flips, start, steps, images, final),
        out_shape=jax.ShapeDtypeStruct((1, size), f32),
        grid_spec=pltpu.PrefetchScalarGridSpec(
            num_scalar_prefetch=1,
            grid=(steps,),
            in_specs=in_specs,
            out_specs=whole_out((1, size)),
            scratch_shapes=scratch,
        ),
        compiler_params=params(),
        cost_estimate=cost(4 * total * count, 2 * total * count),
        name="sinkhorn_final" if final else "sinkhorn_pass",
    )(ids, *args)


def push_kernel(n, flips, block, *refs):
    p = len(flips)
    totals, views, powers_in, slices = (
        refs[:p],
        refs[p : p + n],
        refs[p + n : p + 2 * n],
        refs[p + 2 * n : p + 3 * n],
    )
    sum_ref, *outs, z_ref = refs[p + 3 * n :]
    bounds = [0]
    for s in slices:
        bounds.append(bounds[-1] + s.shape[0])
    spots = [slice(a, b) for a, b in zip(bounds, bounds[1:])]
    step = pl.program_id(0)

    @pl.when(step == 0)
    def prepare():
        total = row_sum(totals, flips, 0, bounds[-1], block)
        sum_ref[...] = total
        width = slices[0].shape[1]
        for j in range(n):
            at = spots[j]
            coef = (GLOBALS - views[j][...]) / total[:, at] * (1.0 / temper)
            tall = to_rows(coef, min(128, width))
            if width > 128:
                tall = jnp.concatenate([tall] * (width // 128), axis=1)
            z_ref[at, :] = (slices[j][...].astype(f32) * tall).astype(bf16)

    out = jnp.dot(powers_in[0][...], z_ref[spots[0], :], preferred_element_type=f32)
    for j in range(1, n):
        out += jnp.dot(powers_in[j][...], z_ref[spots[j], :], preferred_element_type=f32)
    span = outs[0].shape[1]
    for part, ref in enumerate(outs):
        ref[...] = out[:, part * span : (part + 1) * span].astype(ref.dtype)


def push(totals, flips, block, views, power_list, slices, parts):
    n = len(power_list)
    count = power_list[0].shape[0]
    rows = sum(p.shape[1] for p in power_list)
    width = slices[0].shape[1]
    span = width // parts
    tile = max(64, min(1024, 4096 * 1024 // rows, count))
    row = (1, rows)
    return pl.pallas_call(
        functools.partial(push_kernel, n, flips, block),
        out_shape=[jax.ShapeDtypeStruct(row, f32)]
        + [jax.ShapeDtypeStruct((count, span), bf16 if k else f32) for k in range(parts)],
        grid=(count // tile,),
        in_specs=[whole_spec(t) for t in totals]
        + [whole_spec(v) for v in views]
        + [pl.BlockSpec((tile, p.shape[1]), lambda i: (i, 0)) for p in power_list]
        + [whole_spec(s) for s in slices],
        out_specs=[whole_out(row)]
        + [pl.BlockSpec((tile, span), lambda i: (i, 0)) for _ in range(parts)],
        scratch_shapes=[pltpu.VMEM((rows, width), bf16)],
        compiler_params=params(),
        cost_estimate=cost(2 * rows * count * width, 2 * rows * count),
        name="gradient_push",
    )(*totals, *views, *power_list, *slices)


def pull_kernel(flips, m, block, fresh, ids, *refs):
    n = len(flips)
    before, last, others = refs[:n], refs[n : 2 * n], refs[2 * n : 2 * n + m]
    refs = refs[2 * n + m :]
    if fresh:
        glob_ref, c_ref, push_ref = refs[:3]
    else:
        sharp_ref, push_ref = refs[:2]
    out_ref, w_ref = refs[-2:]
    span = push_ref.shape[1]
    step = pl.program_id(0)

    @pl.when(step == 0)
    def prepare():
        total = w_ref.shape[0]
        weight = 1.0 / row_sum(before, flips, 0, total, block)
        scale = (1.0 / temper) / row_sum(last, flips, 0, total, block)
        tall = to_rows(scale, span)
        base = 0
        for other in others:
            at = slice(base, base + other.shape[0])
            w_ref[at, :span] = (other[...] * tall[at, :]).astype(bf16)
            base += other.shape[0]
        w_ref[:, span:] = to_rows(weight, span).astype(bf16)

    sharp = sharp_of(c_ref[...], glob_ref[...]) if fresh else sharp_ref[...]
    both = jnp.dot(sharp, w_ref[...], preferred_element_type=f32)
    grad = push_ref[...].astype(f32) - both[:, :span] / both[:, span:]
    out_ref[...] = grad.T


def pull(ids, before, last, flips, block, others, sharp, globs, unit_c, pushed, part, carry):
    n, m = len(before), len(others)
    fresh = sharp is None
    total = sum(o.shape[0] for o in others)
    count, width = unit_c.shape
    half, span = pushed.shape
    tile = min(half, max(128, 1024 * 1024 // total))
    steps = half // tile
    args = [*before, *last, *others] + ([globs] if fresh else [])
    in_specs = [whole_spec(a) for a in args]
    if fresh:
        args.append(unit_c)
        in_specs.append(pl.BlockSpec((tile, width), lambda i, ids: (part * steps + i, 0)))
    else:
        args.append(sharp)
        in_specs.append(pl.BlockSpec((tile, total), lambda i, ids: (i, 0)))
    args.append(pushed)
    in_specs.append(pl.BlockSpec((tile, span), lambda i, ids: (i, 0)))
    aliases = {}
    if carry is not None:
        aliases = {len(args) + 1: 0}
        args.append(carry)
        in_specs.append(pl.BlockSpec(memory_space=pl.ANY))
    return pl.pallas_call(
        functools.partial(pull_kernel, flips, m, block, fresh),
        out_shape=jax.ShapeDtypeStruct((span, count), f32),
        grid_spec=pltpu.PrefetchScalarGridSpec(
            num_scalar_prefetch=1,
            grid=(steps,),
            in_specs=in_specs,
            out_specs=pl.BlockSpec(
                (span, tile), lambda i, ids: (0, (part ^ ids[2]) * steps + i)
            ),
            scratch_shapes=[pltpu.VMEM((total, 2 * span), bf16)],
        ),
        input_output_aliases=aliases,
        compiler_params=params(),
        cost_estimate=cost(
            4 * total * half * span + (2 * total * half * width if fresh else 0),
            2 * total * half + 6 * half * span,
        ),
        name="gradient_pull",
    )(ids, *args)


def loss_kernel(flips, images, total_all, block_ref, sum_ref, *refs):
    parts, out_ref = refs[:-1], refs[-1]
    rows = block_ref.shape[0] - PAD
    size = out_ref.shape[1]
    code = code_line(block_ref[rows:, : size // LINES])
    mine, one, two = image_masks(code, images)
    own = GLOBALS * images
    scale = (1.0 / temper) / row_sum(parts, flips, 0, 2 * own, own)[:, :own]
    tall = to_rows(scale, 128)[:, :1]
    pairs = (parts[0].shape[1] - total_all) // 2
    value = 0.0
    for k in range(2):
        product = row_sum(parts, flips, total_all + k * pairs, pairs, size)[:, :size]
        value += product * jnp.sum(mine * tall[k * images : (k + 1) * images], axis=0, keepdims=True)
    view = code - 2.0 * jnp.floor(code * 0.5)
    logs = jnp.log(sum_ref[:, :size]) - math.log(K)
    out_ref[...] = logs * (GLOBALS - view) - value


def losses(block, total, parts, flips, images, total_all, size):
    args = [block, total, *parts]
    return pl.pallas_call(
        functools.partial(loss_kernel, flips, images, total_all),
        out_shape=jax.ShapeDtypeStruct((1, size), f32),
        grid=(1,),
        in_specs=[whole_spec(a) for a in args],
        out_specs=whole_out((1, size)),
        compiler_params=params(),
        name="crop_losses",
    )(*args)


def swap(array, axes, sizes, offset):
    size = math.prod(sizes)
    return lax.ppermute(array, axes, [(i, i ^ offset) for i in range(size)])


def shards(sizes, embeddings, prototypes, crop_image, crop_view):
    n_batch, n_proto, n_sub = sizes
    n = n_proto * n_sub
    parts = 2
    width = embeddings.shape[1]
    crops_all = crop_image.shape[0]
    images = crop_image.shape[0] // CROPS
    count = prototypes.shape[0]
    half = count // parts
    span = width // n_batch
    own = GLOBALS * images

    batch = lax.axis_index("batch")
    place = lax.axis_index("proto") * n_sub + lax.axis_index("sub")
    ids = jnp.stack([batch, place, batch % parts, jnp.int32(images)]).astype(jnp.int32)

    lines = (LINES, crops_all // LINES)
    mine = crops(ids, embeddings, crop_image.reshape(lines), crop_view.reshape(lines))
    unit_c = protos(ids, prototypes, parts)

    def along(array, axis, offset):
        return swap(array, axis, (sizes[("batch", "proto", "sub").index(axis)],), offset)

    def chips(block):
        return [block] + [along(block, "proto", j) for j in range(1, n_proto)]

    def cores(found):
        return [b if k == 0 else along(b, "sub", k) for b in found for k in range(n_sub)]

    moved = {0: mine}
    for k in range(1, n_batch):
        low = k & -k
        moved[k] = along(mine if k == low else moved[k ^ low], "batch", low)
    near = chips(mine)
    near, unit_c = lax.optimization_barrier((near, unit_c))
    near[0] = mine
    blocks = [cores(near)]

    power_list, total_list, views, others, slices = [], [], [], [], []

    def collect(found):
        for kept, new in zip((power_list, total_list, views, others, slices), found):
            kept.append(new)
        return found[5:]

    (globs,) = collect(powers(ids, blocks[:1], [], False, unit_c, half, images, span, parts))
    far = [chips(moved[k]) for k in range(1, n_batch)]
    far, _ = lax.optimization_barrier((far, total_list[0]))
    blocks += [cores(found) for found in far]
    for k in range(1, n_batch, 3):
        found = powers(
            ids, blocks[k : k + 3], [globs], k + 3 >= n_batch, unit_c, half, images, span, parts
        )
        globs, *rest = collect(found)
    sharp, row = rest

    flips = (False, False, True, True) if n_proto == 2 else (False, True)

    def chip_sum(row):
        if n_proto != 2 or n_sub != 2:
            return lax.psum(row, ("proto", "sub"))
        return row + along(row, "sub", 1)

    def everywhere(row):
        if n_proto != 2 or n_sub != 2:
            return [row, along(row, "batch", 1)]
        pair = (n_batch, n_proto)
        return [row] + [swap(row, ("batch", "proto"), pair, j) for j in (1, n_proto, n_proto + 1)]

    tokens = n_batch * crops_all
    firsts = everywhere(chip_sum(jnp.concatenate(total_list + [row], axis=1)))

    row_parts, start = firsts, tokens
    for step_index in range(ITERS - 2):
        row = chip_sum(scale_pass(ids, row_parts, flips, start, sharp, images))
        row_parts, start = everywhere(row), 0
    firsts, _ = lax.optimization_barrier((firsts, row))
    total, *pushed = push(firsts, flips, crops_all, views, power_list, slices, parts)
    pieces = [pushed[0], along(pushed[1], "batch", 1)]
    before, _ = lax.optimization_barrier((row_parts, total))

    row = scale_pass(ids, before, flips, start, sharp, images, unit_c, blocks[:parts])
    last = everywhere(chip_sum(row))

    grad = None
    for part in range(parts):
        grad = pull(
            ids, before, last, flips, own, others, None if part else sharp, globs, unit_c,
            pieces[part], part, grad,
        )
    crop_loss = losses(mine, total, last, flips, images, n_batch * own, crops_all)
    return (crop_loss.reshape(crops_all), grad)


def solution(mesh):
    sizes = tuple(mesh.shape[a] for a in ("batch", "proto", "sub"))
    placed = (
        P(("groups", "batch", "proto", "sub"), None),
        P(("groups", "proto", "sub"), None),
        P(("groups", "batch")),
        P(("groups", "batch")),
    )
    return jax.shard_map(
        functools.partial(shards, sizes),
        mesh=mesh,
        in_specs=placed,
        out_specs=(P(("groups", "batch")), P("batch", ("groups", "proto", "sub"))),
        check_vma=False,
    )
```

```python
import functools
import math

import jax
import jax.numpy as jnp
from jax import lax
from jax.experimental import pallas as pl
from jax.experimental.pallas import tpu as pltpu
from jax.sharding import PartitionSpec as P

K = 32768
CROPS = 8
GLOBALS = 2
ITERS = 3
PAD = 16
LINES = 8
VMEM_LIMIT = 56 * 1024 * 1024

sharpen = 0.05
temper = 0.1

f32 = jnp.float32
bf16 = jnp.bfloat16


def params():
    return pltpu.CompilerParams(
        dimension_semantics=("arbitrary",), vmem_limit_bytes=VMEM_LIMIT
    )


def whole_spec(array):
    zeros = (0,) * array.ndim
    return pl.BlockSpec(array.shape, lambda *_: zeros)


def whole_out(shape):
    zeros = (0,) * len(shape)
    return pl.BlockSpec(shape, lambda *_: zeros)


def unit(wide):
    factor = lax.rsqrt(jnp.mean(wide * wide, axis=-1, keepdims=True) + 1e-06) / math.sqrt(
        wide.shape[-1]
    )
    return (wide * factor).astype(bf16)


def to_rows(lane_vector, width):
    return jnp.broadcast_to(lane_vector, (128, lane_vector.shape[1])).T[:, :width]


def fold(values):
    return values.reshape(values.shape[0] // 8, 8, values.shape[1]).sum(0)


def cost(flops, nbytes, trans=0):
    return pl.CostEstimate(flops=int(flops), bytes_accessed=int(nbytes), transcendentals=int(trans))


def crops_kernel(ids, emb_ref, image_ref, view_ref, out_ref):
    rows, width = emb_ref.shape
    out_ref[:rows, :] = unit(emb_ref[...].astype(f32))
    code = ((image_ref[...] - ids[0] * ids[3]) * 2 + view_ref[...]).astype(f32)
    code = jnp.concatenate([code, jnp.zeros((code.shape[0], width - code.shape[1]), f32)], axis=1)
    code = jnp.concatenate([code, jnp.zeros((PAD - code.shape[0], width), f32)], axis=0)
    out_ref[rows:, :] = code.astype(bf16)


def crops(ids, emb, image, view):
    rows, width = emb.shape
    shape = (rows + PAD, width)
    return pl.pallas_call(
        crops_kernel,
        out_shape=jax.ShapeDtypeStruct(shape, bf16),
        grid_spec=pltpu.PrefetchScalarGridSpec(
            num_scalar_prefetch=1,
            grid=(1,),
            in_specs=[whole_spec(emb), whole_spec(image), whole_spec(view)],
            out_specs=whole_out(shape),
        ),
        compiler_params=params(),
        name="unit_crops",
    )(ids, emb, image, view)


def protos_kernel(ids, c_ref, out_ref):
    out_ref[...] = unit(c_ref[...].astype(f32))


def protos(ids, prototypes, part, parts):
    width = prototypes.shape[1]
    count = prototypes.shape[0] // parts
    tile = min(1024, count)
    steps = count // tile
    return pl.pallas_call(
        protos_kernel,
        out_shape=jax.ShapeDtypeStruct((count, width), bf16),
        grid_spec=pltpu.PrefetchScalarGridSpec(
            num_scalar_prefetch=1,
            grid=(steps,),
            in_specs=[
                pl.BlockSpec((tile, width), lambda i, ids: ((part ^ ids[2]) * steps + i, 0))
            ],
            out_specs=pl.BlockSpec((tile, width), lambda i, ids: (i, 0)),
        ),
        compiler_params=params(),
        cost_estimate=cost(4 * count * width, 4 * count * width),
        name="unit_protos",
    )(ids, prototypes)


def image_masks(code, images):
    view = code - 2.0 * jnp.floor(code * 0.5)
    image = (code - view) * 0.5
    shape = (images, code.shape[1])
    row = lax.broadcasted_iota(jnp.int32, shape, 0).astype(f32)
    place = lax.broadcasted_iota(jnp.int32, shape, 1).astype(f32)
    mine = row == image
    glob = mine & (view > 0.5)
    first = jnp.min(jnp.where(glob, place, 1e9), axis=1, keepdims=True)
    one = glob & (place == first)
    two = glob & (place != first)
    return [m.astype(f32) for m in (mine, one, two)]


def code_line(lines):
    lines = lines.astype(f32)
    return jnp.concatenate([lines[j : j + 1, :] for j in range(LINES)], axis=1)


def block_copies(ids, blocks, rows, z_ref, code_ref, sems):
    m, n = len(blocks), len(blocks[0])
    lanes = code_ref.shape[2]
    copies = []
    for k in range(m):
        for j in range(n):
            at = pl.multiple_of(k * n * rows + (j ^ ids[1]) * rows, rows)
            copies.append((blocks[k][j].at[pl.ds(0, rows), :], z_ref.at[pl.ds(at, rows), :]))
        copies.append((blocks[k][0].at[pl.ds(rows, PAD), pl.ds(0, lanes)], code_ref.at[k]))
    return [pltpu.make_async_copy(a, b, sems.at[i]) for i, (a, b) in enumerate(copies)]


def load_blocks(*args):
    copies = block_copies(*args)
    for c in copies:
        c.start()
    for c in copies:
        c.wait()


def power_kernel(m, n, early, last, steps, images, ids, *refs):
    blocks = [refs[k * n : (k + 1) * n] for k in range(m)]
    refs = refs[m * n :]
    ready, c_ref, refs = refs[: 2 * early], refs[2 * early], refs[2 * early + 1 :]
    ready, carried = ready[:early], ready[early:]
    power_ref, total_ref, view_ref, other_ref, slice_ref, glob_ref = refs[:6]
    refs = refs[6:]
    if last:
        sharp_ref, *refs = refs
        z_ref, code_ref, acc_ref, sems, racc_ref = refs
    else:
        z_ref, code_ref, acc_ref, sems = refs
    rows = blocks[0][0].shape[0] - PAD
    each = n * rows
    own = GLOBALS * images
    width = z_ref.shape[1]
    step = pl.program_id(0)

    @pl.when(step == 0)
    def prepare():
        load_blocks(ids, blocks, rows, z_ref, code_ref, sems)
        span = other_ref.shape[1]
        feature = lax.broadcasted_iota(jnp.int32, (width, slice_ref.shape[1]), 0)
        column = lax.broadcasted_iota(jnp.int32, (width, slice_ref.shape[1]), 1)
        wanted = (ids[0] ^ (column // span)) * span + column % span
        chosen = jnp.where(feature == wanted, 1.0, 0.0).astype(bf16)
        base = 0
        for r in ready:
            glob_ref[base : base + r.shape[0], :] = r[...]
            base += r.shape[0]
        for k in range(m):
            at, to = slice(k * each, (k + 1) * each), slice(k * own, (k + 1) * own)
            code = code_line(code_ref[k])
            view_ref[:, at] = code - 2.0 * jnp.floor(code * 0.5)
            mine, one, two = image_masks(code, images)
            picks = jnp.concatenate([one, two], axis=0)
            rest = jnp.concatenate([mine, mine], axis=0) - picks
            z = z_ref[at, :]
            glob_ref[base + k * own : base + (k + 1) * own, :] = jnp.dot(
                picks.astype(bf16), z, preferred_element_type=f32
            ).astype(bf16)
            part = jnp.dot(z, chosen, preferred_element_type=f32).astype(bf16)
            slice_ref[at, :] = part
            other_ref[to, :] = jnp.dot(
                rest.astype(bf16), part[:, :span], preferred_element_type=f32
            )
        acc_ref[...] = jnp.zeros_like(acc_ref)
        if last:
            racc_ref[...] = jnp.zeros_like(racc_ref)

    scores = lax.dot_general(
        c_ref[...], z_ref[...], (((1,), (1,)), ((), ())), preferred_element_type=f32
    )
    power = jnp.exp(scores * (1.0 / temper))
    power_ref[...] = power.astype(bf16)
    acc_ref[...] += fold(power)
    if last:
        sharp = sharp_of(c_ref[...], glob_ref[...])
        sharp_ref[...] = sharp
        wide = sharp.astype(f32)
        col = 1.0 / jnp.sum(wide, axis=1, keepdims=True)
        racc_ref[...] += fold(wide * col.astype(bf16).astype(f32))

    @pl.when(step == steps - 1)
    def finish():
        base = 0
        for ref in carried:
            total_ref[:, : ref.shape[1]] = ref[...]
            base += ref.shape[1]
        total_ref[:, base : base + m * each] = jnp.sum(acc_ref[...], axis=0, keepdims=True)
        if last:
            total_ref[:, base + m * each :] = jnp.sum(racc_ref[...], axis=0, keepdims=True)


def powers(ids, blocks, ready, carried, last, unit_c, images, span, parts):
    count = unit_c.shape[0]
    m, n = len(blocks), len(blocks[0])
    rows, width = blocks[0][0].shape[0] - PAD, blocks[0][0].shape[1]
    crops_all = m * n * rows
    own = m * GLOBALS * images
    globs = own + sum(r.shape[0] for r in ready)
    sums = crops_all + sum(t.shape[1] for t in carried) + (globs if last else 0)
    tile = min(512, count, max(64, 2048 * 1024 // (crops_all + globs) // 64 * 64))
    while count % tile:
        tile -= 64
    steps = count // tile
    shapes = [
        ((count, crops_all), bf16),
        ((1, sums), f32),
        ((1, crops_all), f32),
        ((own, span), f32),
        ((crops_all, parts * span), bf16),
        ((globs, width), bf16),
    ]
    out_specs = [pl.BlockSpec((tile, crops_all), lambda i, ids: (i, 0))]
    out_specs += [whole_out(s) for s, _ in shapes[1:]]
    scratch = [
        pltpu.VMEM((crops_all, width), bf16),
        pltpu.VMEM((m, PAD, n * rows // LINES), bf16),
        pltpu.VMEM((8, crops_all), f32),
        pltpu.SemaphoreType.DMA((m * n + m,)),
    ]
    if last:
        shapes.append(((count, globs), bf16))
        out_specs.append(pl.BlockSpec((tile, globs), lambda i, ids: (i, 0)))
        scratch.append(pltpu.VMEM((8, globs), f32))
    columns = crops_all + (globs if last else 0)
    return pl.pallas_call(
        functools.partial(power_kernel, m, n, len(ready), last, steps, images),
        out_shape=[jax.ShapeDtypeStruct(s, d) for s, d in shapes],
        grid_spec=pltpu.PrefetchScalarGridSpec(
            num_scalar_prefetch=1,
            grid=(steps,),
            in_specs=[pl.BlockSpec(memory_space=pltpu.HBM)] * (m * n)
            + [whole_spec(r) for r in [*ready, *carried]]
            + [pl.BlockSpec((tile, width), lambda i, ids: (i, 0))],
            out_specs=out_specs,
            scratch_shapes=scratch,
        ),
        compiler_params=params(),
        cost_estimate=cost(
            2 * columns * count * width, 2 * count * (columns + width), columns * count
        ),
        name="softmax_powers",
    )(ids, *[b for block in blocks for b in block], *ready, *carried, unit_c)


def flip(row, block):
    pieces = [row[:, j * block : (j + 1) * block] for j in range(row.shape[1] // block)]
    return jnp.concatenate([pieces[j ^ 1] for j in range(len(pieces))], axis=1)


def row_sum(refs, flips, start, size, block):
    parts = [r[:, start : start + size] for r in refs]
    return sum(flip(p, block) if turn else p for p, turn in zip(parts, flips))


def sharp_of(c, z):
    scores = lax.dot_general(c, z, (((1,), (1,)), ((), ())), preferred_element_type=f32)
    return jnp.exp(scores * (1.0 / sharpen)).astype(bf16)


def scale_pass_kernel(flips, start, steps, images, final, ids, *refs):
    p = len(flips)
    parts, sharp_ref, refs = refs[:p], refs[p], refs[p + 1 :]
    if final:
        m, n = final
        c_ref, blocks, refs = refs[0], refs[1 : 1 + m * n], refs[1 + m * n :]
        blocks = [blocks[k * n : (k + 1) * n] for k in range(m)]
        out_ref, w_ref, acc_ref, v_ref, scaled_ref, z_ref, code_ref, sems = refs
        rows = blocks[0][0].shape[0] - PAD
    else:
        out_ref, w_ref, acc_ref = refs
    own = GLOBALS * images
    total = sharp_ref.shape[1]
    step = pl.program_id(0)

    @pl.when(step == 0)
    def prepare():
        if final:
            for c in block_copies(ids, blocks, rows, z_ref, code_ref, sems):
                c.start()
            v_ref[...] = jnp.zeros_like(v_ref)
        scale = 1.0 / row_sum(parts, flips, start, total, own)
        w_ref[...] = to_rows(scale, 128).astype(bf16)
        acc_ref[...] = jnp.zeros_like(acc_ref)

    chunk = min(256, sharp_ref.shape[0])
    for j in range(sharp_ref.shape[0] // chunk):
        at = slice(j * chunk, (j + 1) * chunk)
        sharp = sharp_ref[at, :]
        col = 1.0 / jnp.dot(sharp, w_ref[...], preferred_element_type=f32)
        narrow = col.astype(bf16).astype(f32)
        for lane in range(total // 128):
            span = slice(lane * 128, (lane + 1) * 128)
            acc_ref[:, span] += fold(sharp[:, span].astype(f32) * narrow)
        if final:
            scaled_ref[at, :] = (c_ref[at, :].astype(f32) * col[:, :1]).astype(bf16)
    if final:
        v_ref[...] += lax.dot_general(
            sharp_ref[:, : m * own],
            scaled_ref[...],
            (((0,), (0,)), ((), ())),
            preferred_element_type=f32,
        )

    @pl.when(step == steps - 1)
    def finish():
        out_ref[:, :total] = jnp.sum(acc_ref[...], axis=0, keepdims=True)
        if final:
            for c in block_copies(ids, blocks, rows, z_ref, code_ref, sems):
                c.wait()
            each = n * rows
            for k in range(m):
                at = slice(k * each, (k + 1) * each)
                mine, one, two = image_masks(code_line(code_ref[k]), images)
                hits = lax.dot_general(
                    v_ref[k * own : (k + 1) * own, :].astype(bf16),
                    z_ref[at, :],
                    (((1,), (1,)), ((), ())),
                    preferred_element_type=f32,
                )
                first = jnp.sum(hits[:images] * (mine - one), axis=0, keepdims=True)
                second = jnp.sum(hits[images:] * (mine - two), axis=0, keepdims=True)
                base = total + k * each
                out_ref[:, base : base + each] = first
                base += m * each
                out_ref[:, base : base + each] = second


def scale_pass(ids, row_parts, flips, start, sharp, images, unit_c=None, blocks=None):
    count, total = sharp.shape
    tile = min(count, max(64, 1024 * 1024 // total))
    steps = count // tile
    size = total
    scratch = [pltpu.VMEM((total, 128), bf16), pltpu.VMEM((8, total), f32)]
    args = [*row_parts, sharp]
    in_specs = [whole_spec(p) for p in row_parts]
    in_specs.append(pl.BlockSpec((tile, total), lambda i, ids: (i, 0)))
    final = None
    if unit_c is not None:
        m, n = final = len(blocks), len(blocks[0])
        rows, width = blocks[0][0].shape[0] - PAD, unit_c.shape[1]
        args += [unit_c] + [b for block in blocks for b in block]
        in_specs.append(pl.BlockSpec((tile, width), lambda i, ids: (i, 0)))
        in_specs += [pl.BlockSpec(memory_space=pltpu.HBM)] * (m * n)
        size += 2 * m * n * rows
        scratch += [
            pltpu.VMEM((m * GLOBALS * images, width), f32),
            pltpu.VMEM((tile, width), bf16),
            pltpu.VMEM((m * n * rows, width), bf16),
            pltpu.VMEM((m, PAD, n * rows // LINES), bf16),
            pltpu.SemaphoreType.DMA((m * n + m,)),
        ]
    return pl.pallas_call(
        functools.partial(scale_pass_kernel, flips, start, steps, images, final),
        out_shape=jax.ShapeDtypeStruct((1, size), f32),
        grid_spec=pltpu.PrefetchScalarGridSpec(
            num_scalar_prefetch=1,
            grid=(steps,),
            in_specs=in_specs,
            out_specs=whole_out((1, size)),
            scratch_shapes=scratch,
        ),
        compiler_params=params(),
        cost_estimate=cost(4 * total * count, 2 * total * count),
        name="sinkhorn_final" if final else "sinkhorn_pass",
    )(ids, *args)


def push_kernel(n, flips, block, cut, *refs):
    p = len(flips)
    totals, views, powers_in, slices = (
        refs[:p],
        refs[p : p + n],
        refs[p + n : p + 2 * n],
        refs[p + 2 * n : p + 3 * n],
    )
    sum_ref, near_ref, early_ref, late_ref, z_ref = refs[p + 3 * n :]
    bounds = [0]
    for s in slices:
        bounds.append(bounds[-1] + s.shape[0])
    spots = [slice(a, b) for a, b in zip(bounds, bounds[1:])]
    step = pl.program_id(0)

    @pl.when(step == 0)
    def prepare():
        total = row_sum(totals, flips, 0, bounds[-1], block)
        sum_ref[...] = total
        width = slices[0].shape[1]
        for j in range(n):
            at = spots[j]
            coef = (GLOBALS - views[j][...]) / total[:, at] * (1.0 / temper)
            tall = to_rows(coef, min(128, width))
            if width > 128:
                tall = jnp.concatenate([tall] * (width // 128), axis=1)
            z_ref[at, :] = (slices[j][...].astype(f32) * tall).astype(bf16)

    out = jnp.dot(powers_in[0][...], z_ref[spots[0], :], preferred_element_type=f32)
    for j in range(1, n):
        out += jnp.dot(powers_in[j][...], z_ref[spots[j], :], preferred_element_type=f32)
    span = near_ref.shape[1]
    near_ref[...] = out[:, :span]
    away = out[:, span:].astype(bf16)

    @pl.when(step < cut)
    def early():
        early_ref[...] = away

    @pl.when(step >= cut)
    def late():
        late_ref[...] = away


def push(totals, flips, block, views, power_list, slices):
    n = len(power_list)
    count = power_list[0].shape[0]
    rows = sum(p.shape[1] for p in power_list)
    width = slices[0].shape[1]
    span = width // 2
    tile = max(64, min(1024, 4096 * 1024 // rows, count // 2))
    steps = count // tile
    cut = steps // 2
    row = (1, rows)
    return pl.pallas_call(
        functools.partial(push_kernel, n, flips, block, cut),
        out_shape=[
            jax.ShapeDtypeStruct(row, f32),
            jax.ShapeDtypeStruct((count, span), f32),
            jax.ShapeDtypeStruct((cut * tile, span), bf16),
            jax.ShapeDtypeStruct((count - cut * tile, span), bf16),
        ],
        grid=(steps,),
        in_specs=[whole_spec(t) for t in totals]
        + [whole_spec(v) for v in views]
        + [pl.BlockSpec((tile, p.shape[1]), lambda i: (i, 0)) for p in power_list]
        + [whole_spec(s) for s in slices],
        out_specs=[
            whole_out(row),
            pl.BlockSpec((tile, span), lambda i: (i, 0)),
            pl.BlockSpec((tile, span), lambda i: (jnp.minimum(i, cut - 1), 0)),
            pl.BlockSpec((tile, span), lambda i: (jnp.maximum(i - cut, 0), 0)),
        ],
        scratch_shapes=[pltpu.VMEM((rows, width), bf16)],
        compiler_params=params(),
        cost_estimate=cost(2 * rows * count * width, 2 * rows * count),
        name="gradient_push",
    )(*totals, *views, *power_list, *slices)


def pull_kernel(flips, m, images, half, cut, ids, *refs):
    n = len(flips)
    before, last, others = refs[:n], refs[n : 2 * n], refs[2 * n : 2 * n + m]
    block_ref, sum_ref, glob_ref, sharp_ref, c_ref = refs[2 * n + m : 2 * n + m + 5]
    near_ref, early_ref, late_ref, out_ref, loss_ref, w_ref = refs[2 * n + m + 5 :]
    span = near_ref.shape[1]
    own = GLOBALS * images
    step = pl.program_id(0)

    @pl.when(step == 0)
    def prepare():
        total = w_ref.shape[0]
        weight = 1.0 / row_sum(before, flips, 0, total, own)
        scale = (1.0 / temper) / row_sum(last, flips, 0, total, own)
        tall = to_rows(scale, 128)
        base = 0
        for other in others:
            at = slice(base, base + other.shape[0])
            w_ref[at, :span] = (other[...] * tall[at, :span]).astype(bf16)
            base += other.shape[0]
        w_ref[:, span:] = to_rows(weight, span).astype(bf16)
        rows = block_ref.shape[0] - PAD
        size = loss_ref.shape[1]
        code = code_line(block_ref[rows:, : size // LINES])
        mine = image_masks(code, images)[0]
        pairs = (last[0].shape[1] - total) // 2
        value = 0.0
        for k in range(2):
            product = row_sum(last, flips, total + k * pairs, pairs, size)[:, :size]
            factor = tall[k * images : (k + 1) * images, :1]
            value += product * jnp.sum(mine * factor, axis=0, keepdims=True)
        view = code - 2.0 * jnp.floor(code * 0.5)
        logs = jnp.log(sum_ref[:, :size]) - math.log(K)
        loss_ref[...] = logs * (GLOBALS - view) - value

    def finish(sharp, pushed):
        both = jnp.dot(sharp, w_ref[...], preferred_element_type=f32)
        grad = pushed - both[:, :span] / both[:, span:]
        out_ref[...] = grad.T

    @pl.when(step < half)
    def kept():
        finish(sharp_ref[...], near_ref[...])

    @pl.when(step >= half)
    def fresh():
        pushed = jnp.where(step < half + cut, early_ref[...], late_ref[...])
        finish(sharp_of(c_ref[...], glob_ref[...]), pushed.astype(f32))


def pull(ids, before, last, flips, images, others, block, total, globs, sharp, unit_c, pieces):
    near, early, late = pieces
    n, m = len(before), len(others)
    count, columns = sharp.shape
    width, span = unit_c.shape[1], near.shape[1]
    tile = min(early.shape[0], max(128, 1024 * 1024 // columns))
    half, cut = count // tile, early.shape[0] // tile
    size = images * CROPS
    args = [*before, *last, *others, block, total, globs]
    in_specs = [whole_spec(a) for a in args] + [
        pl.BlockSpec((tile, columns), lambda i, ids: (jnp.minimum(i, half - 1), 0)),
        pl.BlockSpec((tile, width), lambda i, ids: (jnp.maximum(i - half, 0), 0)),
        pl.BlockSpec((tile, span), lambda i, ids: (jnp.minimum(i, half - 1), 0)),
        pl.BlockSpec(
            (tile, span), lambda i, ids: (jnp.minimum(jnp.maximum(i - half, 0), cut - 1), 0)
        ),
        pl.BlockSpec((tile, span), lambda i, ids: (jnp.maximum(i - half - cut, 0), 0)),
    ]
    return pl.pallas_call(
        functools.partial(pull_kernel, flips, m, images, half, cut),
        out_shape=[
            jax.ShapeDtypeStruct((span, 2 * count), f32),
            jax.ShapeDtypeStruct((1, size), f32),
        ],
        grid_spec=pltpu.PrefetchScalarGridSpec(
            num_scalar_prefetch=1,
            grid=(2 * half,),
            in_specs=in_specs,
            out_specs=[
                pl.BlockSpec(
                    (span, tile), lambda i, ids: (0, ((i // half) ^ ids[2]) * half + i % half)
                ),
                whole_out((1, size)),
            ],
            scratch_shapes=[pltpu.VMEM((columns, 2 * span), bf16)],
        ),
        compiler_params=params(),
        cost_estimate=cost(8 * columns * count * span, 2 * columns * count),
        name="gradient_pull",
    )(ids, *args, sharp, unit_c, near, early, late)


def swap(array, axes, sizes, offset):
    size = math.prod(sizes)
    return lax.ppermute(array, axes, [(i, i ^ offset) for i in range(size)])


def shards(sizes, embeddings, prototypes, crop_image, crop_view):
    n_batch, n_proto, n_sub = sizes
    n = n_proto * n_sub
    parts = 2
    width = embeddings.shape[1]
    crops_all = crop_image.shape[0]
    images = crop_image.shape[0] // CROPS
    count = prototypes.shape[0]
    half = count // parts
    span = width // n_batch
    own = GLOBALS * images

    batch = lax.axis_index("batch")
    place = lax.axis_index("proto") * n_sub + lax.axis_index("sub")
    ids = jnp.stack([batch, place, batch % parts, jnp.int32(images)]).astype(jnp.int32)

    lines = (LINES, crops_all // LINES)
    mine = crops(ids, embeddings, crop_image.reshape(lines), crop_view.reshape(lines))
    c_near = protos(ids, prototypes, 0, parts)
    c_far = protos(ids, prototypes, 1, parts)

    def along(array, axis, offset):
        return swap(array, axis, (sizes[("batch", "proto", "sub").index(axis)],), offset)

    def chips(block):
        return [block] + [along(block, "proto", j) for j in range(1, n_proto)]

    def cores(found):
        return [b if k == 0 else along(b, "sub", k) for b in found for k in range(n_sub)]

    moved = {0: mine}
    for k in range(1, n_batch):
        low = k & -k
        moved[k] = along(mine if k == low else moved[k ^ low], "batch", low)
    near = chips(mine)
    near, c_near = lax.optimization_barrier((near, c_near))
    near[0] = mine
    blocks = [cores(near)]

    power_list, views, others, slices = [], [], [], []

    def collect(found):
        power, total, *kept = found
        for store, new in zip((power_list, views, others, slices), [power, *kept]):
            store.append(new)
        return total, kept[3:]

    total, (globs,) = collect(powers(ids, blocks[:1], [], [], False, c_near, images, span, parts))
    moved[n_batch - 1], c_far = lax.optimization_barrier((moved[n_batch - 1], c_far))
    far = [chips(moved[k]) for k in range(1, n_batch)]
    far, total = lax.optimization_barrier((far, total))
    blocks += [cores(found) for found in far]
    for k in range(1, n_batch, 3):
        total, (globs, *rest) = collect(
            powers(
                ids, blocks[k : k + 3], [globs], [total], k + 3 >= n_batch, c_near, images, span,
                parts,
            )
        )
    (sharp,) = rest

    flips = (False, False, True, True) if n_proto == 2 else (False, True)

    def chip_sum(row):
        if n_proto != 2 or n_sub != 2:
            return lax.psum(row, ("proto", "sub"))
        return row + along(row, "sub", 1)

    def everywhere(row):
        if n_proto != 2 or n_sub != 2:
            return [row, along(row, "batch", 1)]
        pair = (n_batch, n_proto)
        return [row] + [swap(row, ("batch", "proto"), pair, j) for j in (1, n_proto, n_proto + 1)]

    tokens = n_batch * crops_all
    firsts = everywhere(chip_sum(total))
    total, near, early, late = push(firsts, flips, crops_all, views, power_list, slices)
    early = along(early, "batch", 1)
    row_parts, total = lax.optimization_barrier((firsts, total))

    start = tokens
    for step_index in range(ITERS - 2):
        row = chip_sum(scale_pass(ids, row_parts, flips, start, sharp, images))
        row_parts, start = everywhere(row), 0
    before = row_parts
    late, before[1] = lax.optimization_barrier((late, before[1]))
    late = along(late, "batch", 1)

    row = scale_pass(ids, before, flips, start, sharp, images, c_near, blocks[:parts])
    last = everywhere(chip_sum(row))

    grad, crop_loss = pull(
        ids, before, last, flips, images, others, mine, total, globs, sharp, c_far,
        (near, early, late),
    )
    return (crop_loss.reshape(crops_all), grad)


def solution(mesh):
    sizes = tuple(mesh.shape[a] for a in ("batch", "proto", "sub"))
    placed = (
        P(("groups", "batch", "proto", "sub"), None),
        P(("groups", "proto", "sub"), None),
        P(("groups", "batch")),
        P(("groups", "batch")),
    )
    return jax.shard_map(
        functools.partial(shards, sizes),
        mesh=mesh,
        in_specs=placed,
        out_specs=(P(("groups", "batch")), P("batch", ("groups", "proto", "sub"))),
        check_vma=False,
    )
```

```python
import functools
import math

import jax
import jax.numpy as jnp
from jax import lax
from jax.experimental import pallas as pl
from jax.experimental.pallas import tpu as pltpu
from jax.sharding import PartitionSpec as P

K = 32768
CROPS = 8
GLOBALS = 2
ITERS = 3
PAD = 16
LINES = 8
VMEM_LIMIT = 56 * 1024 * 1024

sharpen = 0.05
temper = 0.1

f32 = jnp.float32
bf16 = jnp.bfloat16


def params():
    return pltpu.CompilerParams(
        dimension_semantics=("arbitrary",), vmem_limit_bytes=VMEM_LIMIT
    )


def whole_spec(array):
    zeros = (0,) * array.ndim
    return pl.BlockSpec(array.shape, lambda *_: zeros)


def whole_out(shape):
    zeros = (0,) * len(shape)
    return pl.BlockSpec(shape, lambda *_: zeros)


def unit(wide):
    factor = lax.rsqrt(jnp.mean(wide * wide, axis=-1, keepdims=True) + 1e-06) / math.sqrt(
        wide.shape[-1]
    )
    return (wide * factor).astype(bf16)


def to_rows(lane_vector, width):
    return jnp.broadcast_to(lane_vector, (128, lane_vector.shape[1])).T[:, :width]


def fold(values):
    return values.reshape(values.shape[0] // 8, 8, values.shape[1]).sum(0)


def cost(flops, nbytes, trans=0):
    return pl.CostEstimate(flops=int(flops), bytes_accessed=int(nbytes), transcendentals=int(trans))


def crops_kernel(ids, emb_ref, image_ref, view_ref, out_ref):
    rows, width = emb_ref.shape
    out_ref[:rows, :] = unit(emb_ref[...].astype(f32))
    code = ((image_ref[...] - ids[0] * ids[3]) * 2 + view_ref[...]).astype(f32)
    code = jnp.concatenate([code, jnp.zeros((code.shape[0], width - code.shape[1]), f32)], axis=1)
    code = jnp.concatenate([code, jnp.zeros((PAD - code.shape[0], width), f32)], axis=0)
    out_ref[rows:, :] = code.astype(bf16)


def crops(ids, emb, image, view):
    rows, width = emb.shape
    shape = (rows + PAD, width)
    return pl.pallas_call(
        crops_kernel,
        out_shape=jax.ShapeDtypeStruct(shape, bf16),
        grid_spec=pltpu.PrefetchScalarGridSpec(
            num_scalar_prefetch=1,
            grid=(1,),
            in_specs=[whole_spec(emb), whole_spec(image), whole_spec(view)],
            out_specs=whole_out(shape),
        ),
        compiler_params=params(),
        name="unit_crops",
    )(ids, emb, image, view)


def protos_kernel(ids, c_ref, out_ref):
    out_ref[...] = unit(c_ref[...].astype(f32))


def protos(ids, prototypes, parts):
    count, width = prototypes.shape
    size = count // parts
    tile = min(2048, size)
    steps = size // tile
    return pl.pallas_call(
        protos_kernel,
        out_shape=jax.ShapeDtypeStruct((count, width), bf16),
        grid_spec=pltpu.PrefetchScalarGridSpec(
            num_scalar_prefetch=1,
            grid=(parts * steps,),
            in_specs=[
                pl.BlockSpec(
                    (tile, width),
                    lambda i, ids: (((i // steps) ^ ids[2]) * steps + i % steps, 0),
                )
            ],
            out_specs=pl.BlockSpec((tile, width), lambda i, ids: (i, 0)),
        ),
        compiler_params=params(),
        cost_estimate=cost(4 * count * width, 4 * count * width),
        name="unit_protos",
    )(ids, prototypes)


def image_masks(code, images):
    view = code - 2.0 * jnp.floor(code * 0.5)
    image = (code - view) * 0.5
    shape = (images, code.shape[1])
    row = lax.broadcasted_iota(jnp.int32, shape, 0).astype(f32)
    place = lax.broadcasted_iota(jnp.int32, shape, 1).astype(f32)
    mine = row == image
    glob = mine & (view > 0.5)
    first = jnp.min(jnp.where(glob, place, 1e9), axis=1, keepdims=True)
    one = glob & (place == first)
    two = glob & (place != first)
    return [m.astype(f32) for m in (mine, one, two)]


def code_line(lines):
    lines = lines.astype(f32)
    return jnp.concatenate([lines[j : j + 1, :] for j in range(LINES)], axis=1)


def block_copies(ids, blocks, rows, z_ref, code_ref, sems):
    m, n = len(blocks), len(blocks[0])
    lanes = code_ref.shape[2]
    copies = []
    for k in range(m):
        for j in range(n):
            at = pl.multiple_of(k * n * rows + (j ^ ids[1]) * rows, rows)
            copies.append((blocks[k][j].at[pl.ds(0, rows), :], z_ref.at[pl.ds(at, rows), :]))
        copies.append((blocks[k][0].at[pl.ds(rows, PAD), pl.ds(0, lanes)], code_ref.at[k]))
    return [pltpu.make_async_copy(a, b, sems.at[i]) for i, (a, b) in enumerate(copies)]


def load_blocks(*args):
    copies = block_copies(*args)
    for c in copies:
        c.start()
    for c in copies:
        c.wait()


def power_kernel(m, n, early, last, steps, images, ids, *refs):
    blocks = [refs[k * n : (k + 1) * n] for k in range(m)]
    refs = refs[m * n :]
    ready, c_ref, refs = refs[: 2 * early], refs[2 * early], refs[2 * early + 1 :]
    ready, carried = ready[:early], ready[early:]
    power_ref, total_ref, view_ref, other_ref, slice_ref, glob_ref = refs[:6]
    refs = refs[6:]
    if last:
        sharp_ref, *refs = refs
        z_ref, code_ref, acc_ref, sems, racc_ref = refs
    else:
        z_ref, code_ref, acc_ref, sems = refs
    rows = blocks[0][0].shape[0] - PAD
    each = n * rows
    own = GLOBALS * images
    width = z_ref.shape[1]
    step = pl.program_id(0)

    @pl.when(step == 0)
    def prepare():
        load_blocks(ids, blocks, rows, z_ref, code_ref, sems)
        span = other_ref.shape[1]
        feature = lax.broadcasted_iota(jnp.int32, (width, slice_ref.shape[1]), 0)
        column = lax.broadcasted_iota(jnp.int32, (width, slice_ref.shape[1]), 1)
        wanted = (ids[0] ^ (column // span)) * span + column % span
        chosen = jnp.where(feature == wanted, 1.0, 0.0).astype(bf16)
        base = 0
        for r in ready:
            glob_ref[base : base + r.shape[0], :] = r[...]
            base += r.shape[0]
        for k in range(m):
            at, to = slice(k * each, (k + 1) * each), slice(k * own, (k + 1) * own)
            code = code_line(code_ref[k])
            view_ref[:, at] = code - 2.0 * jnp.floor(code * 0.5)
            mine, one, two = image_masks(code, images)
            picks = jnp.concatenate([one, two], axis=0)
            rest = jnp.concatenate([mine, mine], axis=0) - picks
            z = z_ref[at, :]
            glob_ref[base + k * own : base + (k + 1) * own, :] = jnp.dot(
                picks.astype(bf16), z, preferred_element_type=f32
            ).astype(bf16)
            part = jnp.dot(z, chosen, preferred_element_type=f32).astype(bf16)
            slice_ref[at, :] = part
            other_ref[to, :] = jnp.dot(
                rest.astype(bf16), part[:, :span], preferred_element_type=f32
            )
        acc_ref[...] = jnp.zeros_like(acc_ref)
        if last:
            racc_ref[...] = jnp.zeros_like(racc_ref)

    scores = lax.dot_general(
        c_ref[...], z_ref[...], (((1,), (1,)), ((), ())), preferred_element_type=f32
    )
    power = jnp.exp(scores * (1.0 / temper))
    power_ref[...] = power.astype(bf16)
    acc_ref[...] += fold(power)
    if last:
        sharp = sharp_of(c_ref[...], glob_ref[...])
        sharp_ref[...] = sharp
        wide = sharp.astype(f32)
        col = 1.0 / jnp.sum(wide, axis=1, keepdims=True)
        racc_ref[...] += fold(wide * col.astype(bf16).astype(f32))

    @pl.when(step == steps - 1)
    def finish():
        base = 0
        for ref in carried:
            total_ref[:, : ref.shape[1]] = ref[...]
            base += ref.shape[1]
        total_ref[:, base : base + m * each] = jnp.sum(acc_ref[...], axis=0, keepdims=True)
        if last:
            total_ref[:, base + m * each :] = jnp.sum(racc_ref[...], axis=0, keepdims=True)


def powers(ids, blocks, ready, carried, last, unit_c, count, images, span, parts):
    m, n = len(blocks), len(blocks[0])
    rows, width = blocks[0][0].shape[0] - PAD, blocks[0][0].shape[1]
    crops_all = m * n * rows
    own = m * GLOBALS * images
    globs = own + sum(r.shape[0] for r in ready)
    sums = crops_all + sum(t.shape[1] for t in carried) + (globs if last else 0)
    tile = min(512, count, max(64, 2048 * 1024 // (crops_all + globs) // 64 * 64))
    while count % tile:
        tile -= 64
    steps = count // tile
    shapes = [
        ((count, crops_all), bf16),
        ((1, sums), f32),
        ((1, crops_all), f32),
        ((own, span), f32),
        ((crops_all, parts * span), bf16),
        ((globs, width), bf16),
    ]
    out_specs = [pl.BlockSpec((tile, crops_all), lambda i, ids: (i, 0))]
    out_specs += [whole_out(s) for s, _ in shapes[1:]]
    scratch = [
        pltpu.VMEM((crops_all, width), bf16),
        pltpu.VMEM((m, PAD, n * rows // LINES), bf16),
        pltpu.VMEM((8, crops_all), f32),
        pltpu.SemaphoreType.DMA((m * n + m,)),
    ]
    if last:
        shapes.append(((count, globs), bf16))
        out_specs.append(pl.BlockSpec((tile, globs), lambda i, ids: (i, 0)))
        scratch.append(pltpu.VMEM((8, globs), f32))
    columns = crops_all + (globs if last else 0)
    return pl.pallas_call(
        functools.partial(power_kernel, m, n, len(ready), last, steps, images),
        out_shape=[jax.ShapeDtypeStruct(s, d) for s, d in shapes],
        grid_spec=pltpu.PrefetchScalarGridSpec(
            num_scalar_prefetch=1,
            grid=(steps,),
            in_specs=[pl.BlockSpec(memory_space=pltpu.HBM)] * (m * n)
            + [whole_spec(r) for r in [*ready, *carried]]
            + [pl.BlockSpec((tile, width), lambda i, ids: (i, 0))],
            out_specs=out_specs,
            scratch_shapes=scratch,
        ),
        compiler_params=params(),
        cost_estimate=cost(
            2 * columns * count * width, 2 * count * (columns + width), columns * count
        ),
        name="softmax_powers",
    )(ids, *[b for block in blocks for b in block], *ready, *carried, unit_c)


def flip(row, block):
    pieces = [row[:, j * block : (j + 1) * block] for j in range(row.shape[1] // block)]
    return jnp.concatenate([pieces[j ^ 1] for j in range(len(pieces))], axis=1)


def row_sum(refs, flips, start, size, block):
    parts = [r[:, start : start + size] for r in refs]
    return sum(flip(p, block) if turn else p for p, turn in zip(parts, flips))


def sharp_of(c, z):
    scores = lax.dot_general(c, z, (((1,), (1,)), ((), ())), preferred_element_type=f32)
    return jnp.exp(scores * (1.0 / sharpen)).astype(bf16)


def scale_pass_kernel(flips, start, steps, images, final, ids, *refs):
    p = len(flips)
    parts, sharp_ref, refs = refs[:p], refs[p], refs[p + 1 :]
    if final:
        m, n = final
        c_ref, blocks, refs = refs[0], refs[1 : 1 + m * n], refs[1 + m * n :]
        blocks = [blocks[k * n : (k + 1) * n] for k in range(m)]
        out_ref, w_ref, acc_ref, v_ref, scaled_ref, z_ref, code_ref, sems = refs
        rows = blocks[0][0].shape[0] - PAD
    else:
        out_ref, w_ref, acc_ref = refs
    own = GLOBALS * images
    total = sharp_ref.shape[1]
    step = pl.program_id(0)

    @pl.when(step == 0)
    def prepare():
        if final:
            for c in block_copies(ids, blocks, rows, z_ref, code_ref, sems):
                c.start()
            v_ref[...] = jnp.zeros_like(v_ref)
        scale = 1.0 / row_sum(parts, flips, start, total, own)
        w_ref[...] = to_rows(scale, 128).astype(bf16)
        acc_ref[...] = jnp.zeros_like(acc_ref)

    chunk = min(256, sharp_ref.shape[0])
    for j in range(sharp_ref.shape[0] // chunk):
        at = slice(j * chunk, (j + 1) * chunk)
        sharp = sharp_ref[at, :]
        col = 1.0 / jnp.dot(sharp, w_ref[...], preferred_element_type=f32)
        narrow = col.astype(bf16).astype(f32)
        for lane in range(total // 128):
            span = slice(lane * 128, (lane + 1) * 128)
            acc_ref[:, span] += fold(sharp[:, span].astype(f32) * narrow)
        if final:
            scaled_ref[at, :] = (c_ref[at, :].astype(f32) * col[:, :1]).astype(bf16)
    if final:
        v_ref[...] += lax.dot_general(
            sharp_ref[:, : m * own],
            scaled_ref[...],
            (((0,), (0,)), ((), ())),
            preferred_element_type=f32,
        )

    @pl.when(step == steps - 1)
    def finish():
        out_ref[:, :total] = jnp.sum(acc_ref[...], axis=0, keepdims=True)
        if final:
            for c in block_copies(ids, blocks, rows, z_ref, code_ref, sems):
                c.wait()
            each = n * rows
            for k in range(m):
                at = slice(k * each, (k + 1) * each)
                mine, one, two = image_masks(code_line(code_ref[k]), images)
                hits = lax.dot_general(
                    v_ref[k * own : (k + 1) * own, :].astype(bf16),
                    z_ref[at, :],
                    (((1,), (1,)), ((), ())),
                    preferred_element_type=f32,
                )
                first = jnp.sum(hits[:images] * (mine - one), axis=0, keepdims=True)
                second = jnp.sum(hits[images:] * (mine - two), axis=0, keepdims=True)
                base = total + k * each
                out_ref[:, base : base + each] = first
                base += m * each
                out_ref[:, base : base + each] = second


def scale_pass(ids, row_parts, flips, start, sharp, images, unit_c=None, blocks=None):
    count, total = sharp.shape
    tile = min(count, max(64, 1024 * 1024 // total))
    steps = count // tile
    size = total
    scratch = [pltpu.VMEM((total, 128), bf16), pltpu.VMEM((8, total), f32)]
    args = [*row_parts, sharp]
    in_specs = [whole_spec(p) for p in row_parts]
    in_specs.append(pl.BlockSpec((tile, total), lambda i, ids: (i, 0)))
    final = None
    if unit_c is not None:
        m, n = final = len(blocks), len(blocks[0])
        rows, width = blocks[0][0].shape[0] - PAD, unit_c.shape[1]
        args += [unit_c] + [b for block in blocks for b in block]
        in_specs.append(pl.BlockSpec((tile, width), lambda i, ids: (i, 0)))
        in_specs += [pl.BlockSpec(memory_space=pltpu.HBM)] * (m * n)
        size += 2 * m * n * rows
        scratch += [
            pltpu.VMEM((m * GLOBALS * images, width), f32),
            pltpu.VMEM((tile, width), bf16),
            pltpu.VMEM((m * n * rows, width), bf16),
            pltpu.VMEM((m, PAD, n * rows // LINES), bf16),
            pltpu.SemaphoreType.DMA((m * n + m,)),
        ]
    return pl.pallas_call(
        functools.partial(scale_pass_kernel, flips, start, steps, images, final),
        out_shape=jax.ShapeDtypeStruct((1, size), f32),
        grid_spec=pltpu.PrefetchScalarGridSpec(
            num_scalar_prefetch=1,
            grid=(steps,),
            in_specs=in_specs,
            out_specs=whole_out((1, size)),
            scratch_shapes=scratch,
        ),
        compiler_params=params(),
        cost_estimate=cost(4 * total * count, 2 * total * count),
        name="sinkhorn_final" if final else "sinkhorn_pass",
    )(ids, *args)


def push_kernel(n, flips, block, cut, *refs):
    p = len(flips)
    totals, views, powers_in, slices = (
        refs[:p],
        refs[p : p + n],
        refs[p + n : p + 2 * n],
        refs[p + 2 * n : p + 3 * n],
    )
    sum_ref, near_ref, early_ref, late_ref, z_ref = refs[p + 3 * n :]
    bounds = [0]
    for s in slices:
        bounds.append(bounds[-1] + s.shape[0])
    spots = [slice(a, b) for a, b in zip(bounds, bounds[1:])]
    step = pl.program_id(0)

    @pl.when(step == 0)
    def prepare():
        total = row_sum(totals, flips, 0, bounds[-1], block)
        sum_ref[...] = total
        width = slices[0].shape[1]
        for j in range(n):
            at = spots[j]
            coef = (GLOBALS - views[j][...]) / total[:, at] * (1.0 / temper)
            tall = to_rows(coef, min(128, width))
            if width > 128:
                tall = jnp.concatenate([tall] * (width // 128), axis=1)
            z_ref[at, :] = (slices[j][...].astype(f32) * tall).astype(bf16)

    out = jnp.dot(powers_in[0][...], z_ref[spots[0], :], preferred_element_type=f32)
    for j in range(1, n):
        out += jnp.dot(powers_in[j][...], z_ref[spots[j], :], preferred_element_type=f32)
    span = near_ref.shape[1]
    near_ref[...] = out[:, :span]
    away = out[:, span:].astype(bf16)

    @pl.when(step < cut)
    def early():
        early_ref[...] = away

    @pl.when(step >= cut)
    def late():
        late_ref[...] = away


def push(totals, flips, block, views, power_list, slices):
    n = len(power_list)
    count = power_list[0].shape[0]
    rows = sum(p.shape[1] for p in power_list)
    width = slices[0].shape[1]
    span = width // 2
    tile = max(64, min(1024, 4096 * 1024 // rows, count // 2))
    steps = count // tile
    cut = steps // 2
    row = (1, rows)
    return pl.pallas_call(
        functools.partial(push_kernel, n, flips, block, cut),
        out_shape=[
            jax.ShapeDtypeStruct(row, f32),
            jax.ShapeDtypeStruct((count, span), f32),
            jax.ShapeDtypeStruct((cut * tile, span), bf16),
            jax.ShapeDtypeStruct((count - cut * tile, span), bf16),
        ],
        grid=(steps,),
        in_specs=[whole_spec(t) for t in totals]
        + [whole_spec(v) for v in views]
        + [pl.BlockSpec((tile, p.shape[1]), lambda i: (i, 0)) for p in power_list]
        + [whole_spec(s) for s in slices],
        out_specs=[
            whole_out(row),
            pl.BlockSpec((tile, span), lambda i: (i, 0)),
            pl.BlockSpec((tile, span), lambda i: (jnp.minimum(i, cut - 1), 0)),
            pl.BlockSpec((tile, span), lambda i: (jnp.maximum(i - cut, 0), 0)),
        ],
        scratch_shapes=[pltpu.VMEM((rows, width), bf16)],
        compiler_params=params(),
        cost_estimate=cost(2 * rows * count * width, 2 * rows * count),
        name="gradient_push",
    )(*totals, *views, *power_list, *slices)


def pull_kernel(flips, m, images, half, cut, ids, *refs):
    n = len(flips)
    before, last, others = refs[:n], refs[n : 2 * n], refs[2 * n : 2 * n + m]
    block_ref, sum_ref, glob_ref, sharp_ref, c_ref = refs[2 * n + m : 2 * n + m + 5]
    near_ref, early_ref, late_ref, out_ref, loss_ref, w_ref = refs[2 * n + m + 5 :]
    span = near_ref.shape[1]
    own = GLOBALS * images
    step = pl.program_id(0)

    @pl.when(step == 0)
    def prepare():
        total = w_ref.shape[0]
        weight = 1.0 / row_sum(before, flips, 0, total, own)
        scale = (1.0 / temper) / row_sum(last, flips, 0, total, own)
        tall = to_rows(scale, 128)
        base = 0
        for other in others:
            at = slice(base, base + other.shape[0])
            w_ref[at, :span] = (other[...] * tall[at, :span]).astype(bf16)
            base += other.shape[0]
        w_ref[:, span:] = to_rows(weight, span).astype(bf16)
        rows = block_ref.shape[0] - PAD
        size = loss_ref.shape[1]
        code = code_line(block_ref[rows:, : size // LINES])
        mine = image_masks(code, images)[0]
        pairs = (last[0].shape[1] - total) // 2
        value = 0.0
        for k in range(2):
            product = row_sum(last, flips, total + k * pairs, pairs, size)[:, :size]
            factor = tall[k * images : (k + 1) * images, :1]
            value += product * jnp.sum(mine * factor, axis=0, keepdims=True)
        view = code - 2.0 * jnp.floor(code * 0.5)
        logs = jnp.log(sum_ref[:, :size]) - math.log(K)
        loss_ref[...] = logs * (GLOBALS - view) - value

    def finish(sharp, pushed):
        both = jnp.dot(sharp, w_ref[...], preferred_element_type=f32)
        grad = pushed - both[:, :span] / both[:, span:]
        out_ref[...] = grad.T

    @pl.when(step < half)
    def kept():
        finish(sharp_ref[...], near_ref[...])

    @pl.when(step >= half)
    def fresh():
        pushed = jnp.where(step < half + cut, early_ref[...], late_ref[...])
        finish(sharp_of(c_ref[...], glob_ref[...]), pushed.astype(f32))


def pull(ids, before, last, flips, images, others, block, total, globs, sharp, unit_c, pieces):
    near, early, late = pieces
    n, m = len(before), len(others)
    count, columns = sharp.shape
    width, span = unit_c.shape[1], near.shape[1]
    tile = min(early.shape[0], max(128, 1024 * 1024 // columns))
    half, cut = count // tile, early.shape[0] // tile
    size = images * CROPS
    args = [*before, *last, *others, block, total, globs]
    in_specs = [whole_spec(a) for a in args] + [
        pl.BlockSpec((tile, columns), lambda i, ids: (jnp.minimum(i, half - 1), 0)),
        pl.BlockSpec((tile, width), lambda i, ids: (jnp.maximum(i, half), 0)),
        pl.BlockSpec((tile, span), lambda i, ids: (jnp.minimum(i, half - 1), 0)),
        pl.BlockSpec(
            (tile, span), lambda i, ids: (jnp.minimum(jnp.maximum(i - half, 0), cut - 1), 0)
        ),
        pl.BlockSpec((tile, span), lambda i, ids: (jnp.maximum(i - half - cut, 0), 0)),
    ]
    return pl.pallas_call(
        functools.partial(pull_kernel, flips, m, images, half, cut),
        out_shape=[
            jax.ShapeDtypeStruct((span, 2 * count), f32),
            jax.ShapeDtypeStruct((1, size), f32),
        ],
        grid_spec=pltpu.PrefetchScalarGridSpec(
            num_scalar_prefetch=1,
            grid=(2 * half,),
            in_specs=in_specs,
            out_specs=[
                pl.BlockSpec(
                    (span, tile), lambda i, ids: (0, ((i // half) ^ ids[2]) * half + i % half)
                ),
                whole_out((1, size)),
            ],
            scratch_shapes=[pltpu.VMEM((columns, 2 * span), bf16)],
        ),
        compiler_params=params(),
        cost_estimate=cost(8 * columns * count * span, 2 * columns * count),
        name="gradient_pull",
    )(ids, *args, sharp, unit_c, near, early, late)


def swap(array, axes, sizes, offset):
    size = math.prod(sizes)
    return lax.ppermute(array, axes, [(i, i ^ offset) for i in range(size)])


def shards(sizes, embeddings, prototypes, crop_image, crop_view):
    n_batch, n_proto, n_sub = sizes
    n = n_proto * n_sub
    parts = 2
    width = embeddings.shape[1]
    crops_all = crop_image.shape[0]
    images = crop_image.shape[0] // CROPS
    count = prototypes.shape[0]
    half = count // parts
    span = width // n_batch
    own = GLOBALS * images

    batch = lax.axis_index("batch")
    place = lax.axis_index("proto") * n_sub + lax.axis_index("sub")
    ids = jnp.stack([batch, place, batch % parts, jnp.int32(images)]).astype(jnp.int32)

    lines = (LINES, crops_all // LINES)
    mine = crops(ids, embeddings, crop_image.reshape(lines), crop_view.reshape(lines))
    unit_c = protos(ids, prototypes, parts)

    def along(array, axis, offset):
        return swap(array, axis, (sizes[("batch", "proto", "sub").index(axis)],), offset)

    def chips(block):
        return [block] + [along(block, "proto", j) for j in range(1, n_proto)]

    def cores(found):
        return [b if k == 0 else along(b, "sub", k) for b in found for k in range(n_sub)]

    def pass_on(k):
        low = k & -k
        return along(mine if k == low else moved[k ^ low], "batch", low)

    moved = {0: mine}
    for k in range(1, n_batch - 1):
        moved[k] = pass_on(k)
    near = chips(mine)
    near, first, unit_c = lax.optimization_barrier(
        (near, [moved[k] for k in range(1, n_batch - 1)], unit_c)
    )
    near[0] = mine
    moved = dict(enumerate([mine, *first]))
    moved[n_batch - 1] = pass_on(n_batch - 1)
    blocks = [cores(near)]

    power_list, views, others, slices = [], [], [], []

    def collect(found):
        power, total, *kept = found
        for store, new in zip((power_list, views, others, slices), [power, *kept]):
            store.append(new)
        return total, kept[3:]

    total, (globs,) = collect(powers(ids, blocks[:1], [], [], False, unit_c, half, images, span, parts))
    far = [chips(moved[k]) for k in range(1, n_batch - 1)]
    far, final, total = lax.optimization_barrier((far, moved[n_batch - 1], total))
    far.append(chips(final))
    blocks += [cores(found) for found in far]
    for k in range(1, n_batch, 3):
        total, (globs, *rest) = collect(
            powers(
                ids, blocks[k : k + 3], [globs], [total], k + 3 >= n_batch, unit_c, half, images,
                span, parts,
            )
        )
    (sharp,) = rest

    flips = (False, False, True, True) if n_proto == 2 else (False, True)

    def chip_sum(row):
        if n_proto != 2 or n_sub != 2:
            return lax.psum(row, ("proto", "sub"))
        return row + along(row, "sub", 1)

    def everywhere(row):
        if n_proto != 2 or n_sub != 2:
            return [row, along(row, "batch", 1)]
        pair = (n_batch, n_proto)
        return [row] + [swap(row, ("batch", "proto"), pair, j) for j in (1, n_proto, n_proto + 1)]

    tokens = n_batch * crops_all
    firsts = everywhere(chip_sum(total))
    total, near, early, late = push(firsts, flips, crops_all, views, power_list, slices)
    early = along(early, "batch", 1)
    row_parts, total = lax.optimization_barrier((firsts, total))

    start = tokens
    for step_index in range(ITERS - 2):
        row = chip_sum(scale_pass(ids, row_parts, flips, start, sharp, images))
        row, early = lax.optimization_barrier((row, early))
        row_parts, start = everywhere(row), 0
    before, late = lax.optimization_barrier((row_parts, late))
    late = along(late, "batch", 1)

    row = scale_pass(ids, before, flips, start, sharp, images, unit_c, blocks[:parts])
    row, late = lax.optimization_barrier((chip_sum(row), late))
    last = everywhere(row)

    grad, crop_loss = pull(
        ids, before, last, flips, images, others, mine, total, globs, sharp, unit_c,
        (near, early, late),
    )
    return (crop_loss.reshape(crops_all), grad)


def solution(mesh):
    sizes = tuple(mesh.shape[a] for a in ("batch", "proto", "sub"))
    placed = (
        P(("groups", "batch", "proto", "sub"), None),
        P(("groups", "proto", "sub"), None),
        P(("groups", "batch")),
        P(("groups", "batch")),
    )
    return jax.shard_map(
        functools.partial(shards, sizes),
        mesh=mesh,
        in_specs=placed,
        out_specs=(P(("groups", "batch")), P("batch", ("groups", "proto", "sub"))),
        check_vma=False,
    )
```

```python
import functools
import math

import jax
import jax.numpy as jnp
from jax import lax
from jax.experimental import pallas as pl
from jax.experimental.pallas import tpu as pltpu
from jax.sharding import PartitionSpec as P

K = 32768
CROPS = 8
GLOBALS = 2
ITERS = 3
PAD = 16
TILE = 1024
KEPT = 1
LINES = 8
VMEM_LIMIT = 20 * 1024 * 1024

sharpen = 0.05
temper = 0.1

f32 = jnp.float32
bf16 = jnp.bfloat16


def params():
    return pltpu.CompilerParams(
        dimension_semantics=("arbitrary",), vmem_limit_bytes=VMEM_LIMIT
    )


def whole_spec(array):
    zeros = (0,) * array.ndim
    return pl.BlockSpec(array.shape, lambda *_: zeros)


def whole_out(shape):
    zeros = (0,) * len(shape)
    return pl.BlockSpec(shape, lambda *_: zeros)


def unit(wide):
    factor = lax.rsqrt(jnp.mean(wide * wide, axis=-1, keepdims=True) + 1e-06) / math.sqrt(
        wide.shape[-1]
    )
    return (wide * factor).astype(bf16)


def to_rows(lane_vector, width):
    return jnp.broadcast_to(lane_vector, (128, lane_vector.shape[1])).T[:, :width]


def fold(values):
    return values.reshape(values.shape[0] // 8, 8, values.shape[1]).sum(0)


def hbm(array):
    return pltpu.with_memory_space_constraint(array, pltpu.HBM)


def vmem(array):
    return pltpu.with_memory_space_constraint(array, pltpu.VMEM)


def cost(flops, nbytes, trans=0):
    return pl.CostEstimate(flops=int(flops), bytes_accessed=int(nbytes), transcendentals=int(trans))


def crops_kernel(ids, emb_in, image_in, view_in, out_ref, emb_ref, image_ref, view_ref, sems):
    pairs = [(emb_in, emb_ref), (image_in, image_ref), (view_in, view_ref)]
    copies = [pltpu.make_async_copy(a, b, sems.at[k]) for k, (a, b) in enumerate(pairs)]
    for c in copies:
        c.start()
    for c in copies:
        c.wait()
    rows, width = emb_ref.shape
    out_ref[:rows, :] = unit(emb_ref[...].astype(f32))
    code = ((image_ref[...] - ids[0] * ids[3]) * 2 + view_ref[...]).astype(f32)
    code = jnp.concatenate([code, jnp.zeros((code.shape[0], width - code.shape[1]), f32)], axis=1)
    code = jnp.concatenate([code, jnp.zeros((PAD - code.shape[0], width), f32)], axis=0)
    out_ref[rows:, :] = code.astype(bf16)


def crops(ids, emb, image, view):
    rows, width = emb.shape
    shape = (rows + PAD, width)
    return pl.pallas_call(
        crops_kernel,
        out_shape=jax.ShapeDtypeStruct(shape, bf16),
        grid_spec=pltpu.PrefetchScalarGridSpec(
            num_scalar_prefetch=1,
            grid=(1,),
            in_specs=[pl.BlockSpec(memory_space=pltpu.HBM)] * 3,
            out_specs=whole_out(shape),
            scratch_shapes=[
                pltpu.VMEM(emb.shape, emb.dtype),
                pltpu.VMEM(image.shape, image.dtype),
                pltpu.VMEM(view.shape, view.dtype),
                pltpu.SemaphoreType.DMA((3,)),
            ],
        ),
        compiler_params=params(),
        name="unit_crops",
    )(ids, hbm(emb), hbm(image), hbm(view))


def protos_kernel(ids, c_ref, out_ref):
    out_ref[...] = unit(c_ref[...].astype(f32))


def protos(ids, prototypes, parts):
    count, width = prototypes.shape
    size = count // parts
    tile = min(2048, size)
    steps = size // tile
    return pl.pallas_call(
        protos_kernel,
        out_shape=pltpu.VMEM((count, width), bf16),
        grid_spec=pltpu.PrefetchScalarGridSpec(
            num_scalar_prefetch=1,
            grid=(parts * steps,),
            in_specs=[
                pl.BlockSpec(
                    (tile, width),
                    lambda i, ids: (((i // steps) ^ ids[2]) * steps + i % steps, 0),
                )
            ],
            out_specs=pl.BlockSpec((tile, width), lambda i, ids: (i, 0)),
        ),
        compiler_params=params(),
        cost_estimate=cost(4 * count * width, 4 * count * width),
        name="unit_protos",
    )(ids, hbm(prototypes))


def image_masks(code, images):
    view = code - 2.0 * jnp.floor(code * 0.5)
    image = (code - view) * 0.5
    shape = (images, code.shape[1])
    row = lax.broadcasted_iota(jnp.int32, shape, 0).astype(f32)
    place = lax.broadcasted_iota(jnp.int32, shape, 1).astype(f32)
    mine = row == image
    glob = mine & (view > 0.5)
    first = jnp.min(jnp.where(glob, place, 1e9), axis=1, keepdims=True)
    one = glob & (place == first)
    two = glob & (place != first)
    return [m.astype(f32) for m in (mine, one, two)]


def code_line(lines):
    lines = lines.astype(f32)
    return jnp.concatenate([lines[j : j + 1, :] for j in range(LINES)], axis=1)


def block_copies(ids, blocks, rows, z_ref, code_ref, sems):
    m, n = len(blocks), len(blocks[0])
    lanes = code_ref.shape[2]
    copies = []
    for k in range(m):
        for j in range(n):
            at = pl.multiple_of(k * n * rows + (j ^ ids[1]) * rows, rows)
            copies.append((blocks[k][j].at[pl.ds(0, rows), :], z_ref.at[pl.ds(at, rows), :]))
        copies.append((blocks[k][0].at[pl.ds(rows, PAD), pl.ds(0, lanes)], code_ref.at[k]))
    return [pltpu.make_async_copy(a, b, sems.at[i]) for i, (a, b) in enumerate(copies)]


def load_blocks(*args):
    copies = block_copies(*args)
    for c in copies:
        c.start()
    for c in copies:
        c.wait()


def power_kernel(m, n, early, last, steps, images, ids, *refs):
    blocks = [refs[k * n : (k + 1) * n] for k in range(m)]
    refs = refs[m * n :]
    ready, c_ref, refs = refs[: 2 * early], refs[2 * early], refs[2 * early + 1 :]
    ready, carried = ready[:early], ready[early:]
    power_refs, refs = refs[:m], refs[m:]
    total_ref, view_ref, other_ref, slice_ref, glob_ref = refs[:5]
    refs = refs[5:]
    if last:
        sharp_ref, *refs = refs
        z_ref, code_ref, acc_ref, sems, racc_ref = refs
    else:
        z_ref, code_ref, acc_ref, sems = refs
    rows = blocks[0][0].shape[0] - PAD
    each = n * rows
    own = GLOBALS * images
    width = z_ref.shape[1]
    step = pl.program_id(0)

    @pl.when(step == 0)
    def prepare():
        load_blocks(ids, blocks, rows, z_ref, code_ref, sems)
        span = other_ref.shape[1]
        feature = lax.broadcasted_iota(jnp.int32, (width, slice_ref.shape[1]), 0)
        column = lax.broadcasted_iota(jnp.int32, (width, slice_ref.shape[1]), 1)
        wanted = (ids[0] ^ (column // span)) * span + column % span
        chosen = jnp.where(feature == wanted, 1.0, 0.0).astype(bf16)
        base = 0
        for r in ready:
            glob_ref[base : base + r.shape[0], :] = r[...]
            base += r.shape[0]
        for k in range(m):
            at, to = slice(k * each, (k + 1) * each), slice(k * own, (k + 1) * own)
            code = code_line(code_ref[k])
            view_ref[:, at] = code - 2.0 * jnp.floor(code * 0.5)
            mine, one, two = image_masks(code, images)
            picks = jnp.concatenate([one, two], axis=0)
            rest = jnp.concatenate([mine, mine], axis=0) - picks
            z = z_ref[at, :]
            glob_ref[base + k * own : base + (k + 1) * own, :] = jnp.dot(
                picks.astype(bf16), z, preferred_element_type=f32
            ).astype(bf16)
            part = jnp.dot(z, chosen, preferred_element_type=f32).astype(bf16)
            slice_ref[at, :] = part
            other_ref[to, :] = jnp.dot(
                rest.astype(bf16), part[:, :span], preferred_element_type=f32
            )
        acc_ref[...] = jnp.zeros_like(acc_ref)
        if last:
            racc_ref[...] = jnp.zeros_like(racc_ref)

    for k, power_ref in enumerate(power_refs):
        at = slice(k * each, (k + 1) * each)
        scores = lax.dot_general(
            c_ref[...], z_ref[at, :], (((1,), (1,)), ((), ())), preferred_element_type=f32
        )
        power = jnp.exp(scores * (1.0 / temper))
        power_ref[...] = power.astype(bf16)
        acc_ref[:, at] += fold(power)
    if last:
        sharp = sharp_of(c_ref[...], glob_ref[...])
        sharp_ref[...] = sharp
        wide = sharp.astype(f32)
        col = 1.0 / jnp.sum(wide, axis=1, keepdims=True)
        racc_ref[...] += fold(wide * col.astype(bf16).astype(f32))

    @pl.when(step == steps - 1)
    def finish():
        base = 0
        for ref in carried:
            total_ref[:, : ref.shape[1]] = ref[...]
            base += ref.shape[1]
        total_ref[:, base : base + m * each] = jnp.sum(acc_ref[...], axis=0, keepdims=True)
        if last:
            total_ref[:, base + m * each :] = jnp.sum(racc_ref[...], axis=0, keepdims=True)


def powers(ids, blocks, ready, carried, last, unit_c, count, images, span, parts, place):
    m, n = len(blocks), len(blocks[0])
    rows, width = blocks[0][0].shape[0] - PAD, blocks[0][0].shape[1]
    crops_all = m * n * rows
    own = m * GLOBALS * images
    globs = own + sum(r.shape[0] for r in ready)
    sums = crops_all + sum(t.shape[1] for t in carried) + (globs if last else 0)
    tile = min(TILE, count, max(64, 2048 * 1024 // (crops_all + globs) // 64 * 64))
    while count % tile:
        tile -= 64
    steps = count // tile
    shapes = [
        *[((count, n * rows), bf16)] * m,
        ((1, sums), f32),
        ((1, crops_all), f32),
        ((own, span), f32),
        ((crops_all, parts * span), bf16),
        ((globs, width), bf16),
    ]
    out_specs = [pl.BlockSpec((tile, n * rows), lambda i, ids: (i, 0))] * m
    out_specs += [whole_out(s) for s, _ in shapes[m:]]
    scratch = [
        pltpu.VMEM((crops_all, width), bf16),
        pltpu.VMEM((m, PAD, n * rows // LINES), bf16),
        pltpu.VMEM((8, crops_all), f32),
        pltpu.SemaphoreType.DMA((m * n + m,)),
    ]
    if last:
        shapes.append(((count, globs), bf16))
        out_specs.append(pl.BlockSpec((tile, globs), lambda i, ids: (i, 0)))
        scratch.append(pltpu.VMEM((8, globs), f32))
    columns = crops_all + (globs if last else 0)
    return pl.pallas_call(
        functools.partial(power_kernel, m, n, len(ready), last, steps, images),
        out_shape=[place(s, d) for s, d in shapes[:m]]
        + [jax.ShapeDtypeStruct(s, d) for s, d in shapes[m : m + 5]]
        + [pltpu.VMEM(s, d) for s, d in shapes[m + 5 :]],
        grid_spec=pltpu.PrefetchScalarGridSpec(
            num_scalar_prefetch=1,
            grid=(steps,),
            in_specs=[pl.BlockSpec(memory_space=pltpu.HBM)] * (m * n)
            + [whole_spec(r) for r in [*ready, *carried]]
            + [pl.BlockSpec((tile, width), lambda i, ids: (i, 0))],
            out_specs=out_specs,
            scratch_shapes=scratch,
        ),
        compiler_params=params(),
        cost_estimate=cost(
            2 * columns * count * width, 2 * count * (columns + width), columns * count
        ),
        name="softmax_powers",
    )(ids, *[b for block in blocks for b in block], *ready, *carried, vmem(unit_c))


def flip(row, block):
    pieces = [row[:, j * block : (j + 1) * block] for j in range(row.shape[1] // block)]
    return jnp.concatenate([pieces[j ^ 1] for j in range(len(pieces))], axis=1)


def row_sum(refs, flips, start, size, block):
    parts = [r[:, start : start + size] for r in refs]
    return sum(flip(p, block) if turn else p for p, turn in zip(parts, flips))


def sharp_of(c, z):
    scores = lax.dot_general(c, z, (((1,), (1,)), ((), ())), preferred_element_type=f32)
    return jnp.exp(scores * (1.0 / sharpen)).astype(bf16)


def scale_pass_kernel(flips, start, steps, images, final, ids, *refs):
    p = len(flips)
    parts, sharp_ref, refs = refs[:p], refs[p], refs[p + 1 :]
    if final:
        m, n = final
        c_ref, blocks, refs = refs[0], refs[1 : 1 + m * n], refs[1 + m * n :]
        blocks = [blocks[k * n : (k + 1) * n] for k in range(m)]
        out_ref, w_ref, acc_ref, v_ref, scaled_ref, z_ref, code_ref, sems = refs
        rows = blocks[0][0].shape[0] - PAD
    else:
        out_ref, w_ref, acc_ref = refs
    own = GLOBALS * images
    total = sharp_ref.shape[1]
    step = pl.program_id(0)

    @pl.when(step == 0)
    def prepare():
        if final:
            for c in block_copies(ids, blocks, rows, z_ref, code_ref, sems):
                c.start()
            v_ref[...] = jnp.zeros_like(v_ref)
        scale = 1.0 / row_sum(parts, flips, start, total, own)
        w_ref[...] = to_rows(scale, 128).astype(bf16)
        acc_ref[...] = jnp.zeros_like(acc_ref)

    chunk = min(256, sharp_ref.shape[0])
    for j in range(sharp_ref.shape[0] // chunk):
        at = slice(j * chunk, (j + 1) * chunk)
        sharp = sharp_ref[at, :]
        col = 1.0 / jnp.dot(sharp, w_ref[...], preferred_element_type=f32)
        narrow = col.astype(bf16).astype(f32)
        for lane in range(total // 128):
            span = slice(lane * 128, (lane + 1) * 128)
            acc_ref[:, span] += fold(sharp[:, span].astype(f32) * narrow)
        if final:
            scaled_ref[at, :] = (c_ref[at, :].astype(f32) * col[:, :1]).astype(bf16)
    if final:
        v_ref[...] += lax.dot_general(
            sharp_ref[:, : m * own],
            scaled_ref[...],
            (((0,), (0,)), ((), ())),
            preferred_element_type=f32,
        )

    @pl.when(step == steps - 1)
    def finish():
        out_ref[:, :total] = jnp.sum(acc_ref[...], axis=0, keepdims=True)
        if final:
            for c in block_copies(ids, blocks, rows, z_ref, code_ref, sems):
                c.wait()
            each = n * rows
            for k in range(m):
                at = slice(k * each, (k + 1) * each)
                mine, one, two = image_masks(code_line(code_ref[k]), images)
                hits = lax.dot_general(
                    v_ref[k * own : (k + 1) * own, :].astype(bf16),
                    z_ref[at, :],
                    (((1,), (1,)), ((), ())),
                    preferred_element_type=f32,
                )
                first = jnp.sum(hits[:images] * (mine - one), axis=0, keepdims=True)
                second = jnp.sum(hits[images:] * (mine - two), axis=0, keepdims=True)
                base = total + k * each
                out_ref[:, base : base + each] = first
                base += m * each
                out_ref[:, base : base + each] = second


def scale_pass(ids, row_parts, flips, start, sharp, images, unit_c=None, blocks=None):
    count, total = sharp.shape
    tile = min(count, max(64, 1024 * 1024 // total))
    steps = count // tile
    size = total
    scratch = [pltpu.VMEM((total, 128), bf16), pltpu.VMEM((8, total), f32)]
    args = [*row_parts, vmem(sharp)]
    in_specs = [whole_spec(p) for p in row_parts]
    in_specs.append(pl.BlockSpec((tile, total), lambda i, ids: (i, 0)))
    final = None
    if unit_c is not None:
        m, n = final = len(blocks), len(blocks[0])
        rows, width = blocks[0][0].shape[0] - PAD, unit_c.shape[1]
        args += [vmem(unit_c)] + [b for block in blocks for b in block]
        in_specs.append(pl.BlockSpec((tile, width), lambda i, ids: (i, 0)))
        in_specs += [pl.BlockSpec(memory_space=pltpu.HBM)] * (m * n)
        size += 2 * m * n * rows
        scratch += [
            pltpu.VMEM((m * GLOBALS * images, width), f32),
            pltpu.VMEM((tile, width), bf16),
            pltpu.VMEM((m * n * rows, width), bf16),
            pltpu.VMEM((m, PAD, n * rows // LINES), bf16),
            pltpu.SemaphoreType.DMA((m * n + m,)),
        ]
    return pl.pallas_call(
        functools.partial(scale_pass_kernel, flips, start, steps, images, final),
        out_shape=jax.ShapeDtypeStruct((1, size), f32),
        grid_spec=pltpu.PrefetchScalarGridSpec(
            num_scalar_prefetch=1,
            grid=(steps,),
            in_specs=in_specs,
            out_specs=whole_out((1, size)),
            scratch_shapes=scratch,
        ),
        compiler_params=params(),
        cost_estimate=cost(4 * total * count, 2 * total * count),
        name="sinkhorn_final" if final else "sinkhorn_pass",
    )(ids, *args)


def push_kernel(n, m, flips, block, cuts, *refs):
    p = len(flips)
    totals, refs = refs[:p], refs[p:]
    views, slices, powers_in, refs = refs[:m], refs[m : 2 * m], refs[2 * m : 2 * m + n], refs[2 * m + n :]
    sum_ref, near_ref, *aways, z_ref = refs
    step = pl.program_id(0)

    @pl.when(step == 0)
    def prepare():
        total = row_sum(totals, flips, 0, sum_ref.shape[1], block)
        sum_ref[...] = total
        width = slices[0].shape[1]
        base = 0
        for j in range(m):
            at = slice(base, base + slices[j].shape[0])
            base = at.stop
            coef = (GLOBALS - views[j][...]) / total[:, at] * (1.0 / temper)
            tall = to_rows(coef, min(128, width))
            if width > 128:
                tall = jnp.concatenate([tall] * (width // 128), axis=1)
            z_ref[at, :] = (slices[j][...].astype(f32) * tall).astype(bf16)

    out = 0.0
    for j in range(n):
        at = slice(j * block, (j + 1) * block)
        out += jnp.dot(powers_in[j][...], z_ref[at, :], preferred_element_type=f32)
    span = near_ref.shape[1]
    near_ref[...] = out[:, :span]
    away = out[:, span:].astype(bf16)
    for k, ref in enumerate(aways):

        @pl.when((step >= cuts[k]) & (step < cuts[k + 1]))
        def store(ref=ref):
            ref[...] = away


def piece_spec(shape, first, count):
    return pl.BlockSpec(shape, lambda i, *_: (jnp.clip(i - first, 0, count - 1), 0))


def push(totals, flips, block, views, power_list, slices, places):
    power_list = [pltpu.with_memory_space_constraint(p, q) for p, q in zip(power_list, places)]
    n, m = len(power_list), len(slices)
    count = power_list[0].shape[0]
    rows = n * block
    width = slices[0].shape[1]
    span = width // 2
    tile = max(64, min(1024, 4096 * 1024 // rows, count // 4))
    steps = count // tile
    cuts = (0, steps // 4, steps // 4 * 3, steps)
    sizes = [b - a for a, b in zip(cuts, cuts[1:])]
    row = (1, rows)
    tiles = pl.BlockSpec((tile, span), lambda i: (i, 0))
    return pl.pallas_call(
        functools.partial(push_kernel, n, m, flips, block, cuts),
        out_shape=[jax.ShapeDtypeStruct(row, f32), jax.ShapeDtypeStruct((count, span), f32)]
        + [jax.ShapeDtypeStruct((size * tile, span), bf16) for size in sizes],
        grid=(steps,),
        in_specs=[whole_spec(t) for t in [*totals, *views, *slices]]
        + [pl.BlockSpec((tile, block), lambda i: (i, 0)) for _ in power_list],
        out_specs=[whole_out(row), tiles]
        + [piece_spec((tile, span), a, size) for a, size in zip(cuts, sizes)],
        scratch_shapes=[pltpu.VMEM((rows, width), bf16)],
        compiler_params=params(),
        cost_estimate=cost(2 * rows * count * width, 2 * rows * count),
        name="gradient_push",
    )(*totals, *views, *slices, *power_list)


def pull_kernel(flips, m, images, kept, cuts, ids, *refs):
    n = len(flips)
    before, last, others = refs[:n], refs[n : 2 * n], refs[2 * n : 2 * n + m]
    glob_ref, c_ref, refs = refs[2 * n + m], refs[2 * n + m + 1], refs[2 * n + m + 2 :]
    pieces, refs = refs[: len(cuts) - 1], refs[len(cuts) - 1 :]
    if kept:
        block_ref, sum_ref, sharp_ref, near_ref, out_ref, loss_ref, w_ref = refs
    else:
        _, out_ref, w_ref = refs
    span = out_ref.shape[0]
    own = GLOBALS * images
    step = pl.program_id(0)

    @pl.when(step == 0)
    def prepare():
        total = w_ref.shape[0]
        weight = 1.0 / row_sum(before, flips, 0, total, own)
        scale = (1.0 / temper) / row_sum(last, flips, 0, total, own)
        tall = to_rows(scale, 128)
        base = 0
        for other in others:
            at = slice(base, base + other.shape[0])
            w_ref[at, :span] = (other[...] * tall[at, :span]).astype(bf16)
            base += other.shape[0]
        w_ref[:, span:] = to_rows(weight, span).astype(bf16)
        if kept:
            rows = block_ref.shape[0] - PAD
            size = loss_ref.shape[1]
            code = code_line(block_ref[rows:, : size // LINES])
            mine = image_masks(code, images)[0]
            pairs = (last[0].shape[1] - total) // 2
            value = 0.0
            for k in range(2):
                product = row_sum(last, flips, total + k * pairs, pairs, size)[:, :size]
                factor = tall[k * images : (k + 1) * images, :1]
                value += product * jnp.sum(mine * factor, axis=0, keepdims=True)
            view = code - 2.0 * jnp.floor(code * 0.5)
            logs = jnp.log(sum_ref[:, :size]) - math.log(K)
            loss_ref[...] = logs * (GLOBALS - view) - value

    def finish(sharp, pushed):
        both = jnp.dot(sharp, w_ref[...], preferred_element_type=f32)
        grad = pushed - both[:, :span] / both[:, span:]
        out_ref[...] = grad.T

    if kept:

        @pl.when(step < kept)
        def stored():
            finish(sharp_ref[...], near_ref[...])

    @pl.when(step >= kept)
    def fresh():
        pushed = pieces[0][...]
        for k, piece in enumerate(pieces[1:], 1):
            pushed = jnp.where(step < kept + cuts[k], pushed, piece[...])
        finish(sharp_of(c_ref[...], glob_ref[...]), pushed.astype(f32))


def pull(ids, before, last, flips, images, others, globs, unit_c, pieces, first, own=None, grad=None):
    n, m = len(before), len(others)
    total = globs.shape[0]
    width, span = unit_c.shape[1], pieces[0].shape[1]
    half = unit_c.shape[0] // 2
    tile = min(pieces[0].shape[0], max(128, 1024 * 1024 // total))
    steps = half // tile
    kept = steps if own else 0
    cuts = [0]
    for piece in pieces:
        cuts.append(cuts[-1] + piece.shape[0] // tile)
    start = steps + first // tile
    size = images * CROPS
    args = [*before, *last, *others, globs, vmem(unit_c), *pieces]
    in_specs = [whole_spec(a) for a in args[: 2 * n + m + 1]]
    in_specs.append(
        pl.BlockSpec((tile, width), lambda i, ids: (start + jnp.maximum(i - kept, 0), 0))
    )
    in_specs += [
        piece_spec((tile, span), kept + a, b - a) for a, b in zip(cuts, cuts[1:])
    ]

    def spot(i, ids):
        place = jnp.where(i < kept, i, start + i - kept)
        return (0, ((place // steps) ^ ids[2]) * steps + place % steps)

    out_shape = [jax.ShapeDtypeStruct((span, 2 * half), f32)]
    out_specs = [pl.BlockSpec((span, tile), spot)]
    aliases = {}
    if own:
        block, sums, sharp, near = own
        args += [block, sums, vmem(sharp), near]
        in_specs += [
            whole_spec(block),
            whole_spec(sums),
            piece_spec((tile, total), 0, kept),
            piece_spec((tile, span), 0, kept),
        ]
        out_shape.append(jax.ShapeDtypeStruct((1, size), f32))
        out_specs.append(whole_out((1, size)))
    else:
        aliases = {len(args) + 1: 0}
        args.append(grad)
        in_specs.append(pl.BlockSpec(memory_space=pl.ANY))
    return pl.pallas_call(
        functools.partial(pull_kernel, flips, m, images, kept, tuple(cuts)),
        out_shape=out_shape,
        grid_spec=pltpu.PrefetchScalarGridSpec(
            num_scalar_prefetch=1,
            grid=(kept + cuts[-1],),
            in_specs=in_specs,
            out_specs=out_specs,
            scratch_shapes=[pltpu.VMEM((total, 2 * span), bf16)],
        ),
        input_output_aliases=aliases,
        compiler_params=params(),
        cost_estimate=cost(
            (kept + cuts[-1]) * tile * total * (4 * span + width), 2 * total * half
        ),
        name="gradient_pull",
    )(ids, *args)


def swap(array, axes, sizes, offset):
    size = math.prod(sizes)
    return lax.ppermute(array, axes, [(i, i ^ offset) for i in range(size)])


def shards(sizes, embeddings, prototypes, crop_image, crop_view):
    n_batch, n_proto, n_sub = sizes
    n = n_proto * n_sub
    parts = 2
    width = embeddings.shape[1]
    crops_all = crop_image.shape[0]
    images = crop_image.shape[0] // CROPS
    count = prototypes.shape[0]
    half = count // parts
    span = width // n_batch
    own = GLOBALS * images

    batch = lax.axis_index("batch")
    place = lax.axis_index("proto") * n_sub + lax.axis_index("sub")
    ids = jnp.stack([batch, place, batch % parts, jnp.int32(images)]).astype(jnp.int32)

    lines = (LINES, crops_all // LINES)
    mine = crops(ids, embeddings, crop_image.reshape(lines), crop_view.reshape(lines))
    unit_c = protos(ids, prototypes, parts)

    def along(array, axis, offset):
        return swap(array, axis, (sizes[("batch", "proto", "sub").index(axis)],), offset)

    def chips(block):
        return [block] + [along(block, "proto", j) for j in range(1, n_proto)]

    def cores(found):
        return [b if k == 0 else along(b, "sub", k) for b in found for k in range(n_sub)]

    def pass_on(k):
        low = k & -k
        return along(mine if k == low else moved[k ^ low], "batch", low)

    moved = {0: mine}
    for k in range(1, n_batch - 1):
        moved[k] = pass_on(k)
    near = chips(mine)
    near, first, unit_c = lax.optimization_barrier(
        (near, [moved[k] for k in range(1, n_batch - 1)], unit_c)
    )
    near[0] = mine
    moved = dict(enumerate([mine, *first]))
    moved[n_batch - 1] = pass_on(n_batch - 1)
    blocks = [cores(near)]

    places = [pltpu.HBM] * (n_batch - KEPT) + [pltpu.VMEM] * KEPT
    power_list, views, others, slices = [], [], [], []

    def collect(found, m):
        power_list.extend(found[:m])
        total, *kept = found[m:]
        for store, new in zip((views, others, slices), kept):
            store.append(new)
        return total, kept[3:]

    total, (globs,) = collect(
        powers(ids, blocks[:1], [], [], False, unit_c, half, images, span, parts, places[0]), 1
    )
    far = [chips(moved[k])[1:] for k in range(1, n_batch - 1)]
    far, moved[n_batch - 1], total = lax.optimization_barrier((far, moved[n_batch - 1], total))
    far.append(chips(moved[n_batch - 1])[1:])
    for k, found in enumerate(far, 1):
        found, total = lax.optimization_barrier((found, total))
        blocks.append(cores([moved[k], *found]))
        last = k + 1 == n_batch
        total, (globs, *rest) = collect(
            powers(
                ids, blocks[k:], [globs], [total], last, unit_c, half, images, span, parts,
                places[k],
            ),
            1,
        )
    (sharp,) = rest

    flips = (False, False, True, True) if n_proto == 2 else (False, True)

    def chip_sum(row):
        if n_proto != 2 or n_sub != 2:
            return lax.psum(row, ("proto", "sub"))
        return row + along(row, "sub", 1)

    def everywhere(row):
        if n_proto != 2 or n_sub != 2:
            return [row, along(row, "batch", 1)]
        pair = (n_batch, n_proto)
        return [row] + [swap(row, ("batch", "proto"), pair, j) for j in (1, n_proto, n_proto + 1)]

    tokens = n_batch * crops_all
    firsts = everywhere(chip_sum(total))
    total, near, early, middle, late = push(
        firsts, flips, crops_all, views, power_list, slices, places
    )
    early = along(early, "batch", 1)
    row_parts, total = lax.optimization_barrier((firsts, total))

    start = tokens
    for step_index in range(ITERS - 2):
        row = chip_sum(scale_pass(ids, row_parts, flips, start, sharp, images))
        row, early = lax.optimization_barrier((row, early))
        row_parts, start = everywhere(row), 0
    before, middle = lax.optimization_barrier((row_parts, middle))
    middle = along(middle, "batch", 1)

    row = scale_pass(ids, before, flips, start, sharp, images, unit_c, blocks[:parts])
    row, middle = lax.optimization_barrier((chip_sum(row), middle))
    last, late = lax.optimization_barrier((everywhere(row), late))
    late = along(late, "batch", 1)

    shared = (ids, before, last, flips, images, others, globs, unit_c)
    grad, crop_loss = pull(*shared, [early, middle], 0, own=(mine, total, sharp, near))
    (grad,) = pull(*shared, [late], early.shape[0] + middle.shape[0], grad=grad)
    return (crop_loss.reshape(crops_all), grad)


def solution(mesh):
    sizes = tuple(mesh.shape[a] for a in ("batch", "proto", "sub"))
    placed = (
        P(("groups", "batch", "proto", "sub"), None),
        P(("groups", "proto", "sub"), None),
        P(("groups", "batch")),
        P(("groups", "batch")),
    )
    return jax.shard_map(
        functools.partial(shards, sizes),
        mesh=mesh,
        in_specs=placed,
        out_specs=(P(("groups", "batch")), P("batch", ("groups", "proto", "sub"))),
        check_vma=False,
    )
```

```python
import functools
import math

import jax
import jax.numpy as jnp
from jax import lax
from jax.experimental import pallas as pl
from jax.experimental.pallas import tpu as pltpu
from jax.sharding import PartitionSpec as P

K = 32768
CROPS = 8
GLOBALS = 2
ITERS = 3
PAD = 16
TILE = 1024
PROTO_TILE = 1024
KEPT = 2
LINES = 8
MIB = 1024 * 1024
SMALL, LARGE = 16, 44

sharpen = 0.05
temper = 0.1

f32 = jnp.float32
bf16 = jnp.bfloat16


def params(globs=0):
    return pltpu.CompilerParams(
        dimension_semantics=("arbitrary",),
        vmem_limit_bytes=(SMALL if globs <= 1024 else LARGE) * MIB,
    )


def whole_spec(array):
    zeros = (0,) * array.ndim
    return pl.BlockSpec(array.shape, lambda *_: zeros)


def whole_out(shape):
    zeros = (0,) * len(shape)
    return pl.BlockSpec(shape, lambda *_: zeros)


def piece_spec(shape, first, count):
    return pl.BlockSpec(shape, lambda i, *_: (jnp.clip(i - first, 0, count - 1), 0))


def unit(wide):
    factor = lax.rsqrt(jnp.mean(wide * wide, axis=-1, keepdims=True) + 1e-06) / math.sqrt(
        wide.shape[-1]
    )
    return (wide * factor).astype(bf16)


def to_rows(lane_vector, width):
    return jnp.broadcast_to(lane_vector, (128, lane_vector.shape[1])).T[:, :width]


def fold(values):
    return values.reshape(values.shape[0] // 8, 8, values.shape[1]).sum(0)


def hbm(array):
    return pltpu.with_memory_space_constraint(array, pltpu.HBM)


def vmem(array):
    return pltpu.with_memory_space_constraint(array, pltpu.VMEM)


def cost(flops, nbytes, trans=0):
    return pl.CostEstimate(flops=int(flops), bytes_accessed=int(nbytes), transcendentals=int(trans))


def crops_kernel(ids, emb_in, image_in, view_in, out_ref, emb_ref, image_ref, view_ref, sems):
    pairs = [(emb_in, emb_ref), (image_in, image_ref), (view_in, view_ref)]
    copies = [pltpu.make_async_copy(a, b, sems.at[k]) for k, (a, b) in enumerate(pairs)]
    for c in copies:
        c.start()
    for c in copies:
        c.wait()
    rows, width = emb_ref.shape
    out_ref[:rows, :] = unit(emb_ref[...].astype(f32))
    code = ((image_ref[...] - ids[0] * ids[3]) * 2 + view_ref[...]).astype(f32)
    code = jnp.concatenate([code, jnp.zeros((code.shape[0], width - code.shape[1]), f32)], axis=1)
    code = jnp.concatenate([code, jnp.zeros((PAD - code.shape[0], width), f32)], axis=0)
    out_ref[rows:, :] = code.astype(bf16)


def crops(ids, emb, image, view):
    rows, width = emb.shape
    shape = (rows + PAD, width)
    return pl.pallas_call(
        crops_kernel,
        out_shape=jax.ShapeDtypeStruct(shape, bf16),
        grid_spec=pltpu.PrefetchScalarGridSpec(
            num_scalar_prefetch=1,
            grid=(1,),
            in_specs=[pl.BlockSpec(memory_space=pltpu.HBM)] * 3,
            out_specs=whole_out(shape),
            scratch_shapes=[
                pltpu.VMEM(emb.shape, emb.dtype),
                pltpu.VMEM(image.shape, image.dtype),
                pltpu.VMEM(view.shape, view.dtype),
                pltpu.SemaphoreType.DMA((3,)),
            ],
        ),
        compiler_params=params(),
        name="unit_crops",
    )(ids, hbm(emb), hbm(image), hbm(view))


def protos_kernel(steps, ids, c_ref, near_ref, far_ref):
    out = unit(c_ref[...].astype(f32))

    @pl.when(pl.program_id(0) < steps)
    def near():
        near_ref[...] = out

    @pl.when(pl.program_id(0) >= steps)
    def far():
        far_ref[...] = out


def protos(ids, prototypes):
    count, width = prototypes.shape
    size = count // 2
    tile = min(PROTO_TILE, size)
    steps = size // tile
    return pl.pallas_call(
        functools.partial(protos_kernel, steps),
        out_shape=[pltpu.VMEM((size, width), bf16), pltpu.VMEM((size, width), bf16)],
        grid_spec=pltpu.PrefetchScalarGridSpec(
            num_scalar_prefetch=1,
            grid=(2 * steps,),
            in_specs=[
                pl.BlockSpec(
                    (tile, width),
                    lambda i, ids: (((i // steps) ^ ids[2]) * steps + i % steps, 0),
                )
            ],
            out_specs=[piece_spec((tile, width), 0, steps), piece_spec((tile, width), steps, steps)],
        ),
        compiler_params=params(),
        cost_estimate=cost(4 * count * width, 4 * count * width),
        name="unit_protos",
    )(ids, hbm(prototypes))


def image_masks(code, images):
    view = code - 2.0 * jnp.floor(code * 0.5)
    image = (code - view) * 0.5
    shape = (images, code.shape[1])
    row = lax.broadcasted_iota(jnp.int32, shape, 0).astype(f32)
    place = lax.broadcasted_iota(jnp.int32, shape, 1).astype(f32)
    mine = row == image
    glob = mine & (view > 0.5)
    first = jnp.min(jnp.where(glob, place, 1e9), axis=1, keepdims=True)
    one = glob & (place == first)
    two = glob & (place != first)
    return [m.astype(f32) for m in (mine, one, two)]


def code_line(lines):
    lines = lines.astype(f32)
    return jnp.concatenate([lines[j : j + 1, :] for j in range(LINES)], axis=1)


def block_copies(ids, blocks, rows, z_ref, code_ref, sems):
    m, n = len(blocks), len(blocks[0])
    lanes = code_ref.shape[2]
    copies = []
    for k in range(m):
        for j in range(n):
            at = pl.multiple_of(k * n * rows + (j ^ ids[1]) * rows, rows)
            copies.append((blocks[k][j].at[pl.ds(0, rows), :], z_ref.at[pl.ds(at, rows), :]))
        copies.append((blocks[k][0].at[pl.ds(rows, PAD), pl.ds(0, lanes)], code_ref.at[k]))
    return [pltpu.make_async_copy(a, b, sems.at[i]) for i, (a, b) in enumerate(copies)]


def power_kernel(m, n, early, last, steps, images, ids, *refs):
    blocks = [refs[k * n : (k + 1) * n] for k in range(m)]
    refs = refs[m * n :]
    ready, c_ref, refs = refs[: 2 * early], refs[2 * early], refs[2 * early + 1 :]
    ready, carried = ready[:early], ready[early:]
    power_refs, refs = refs[:m], refs[m:]
    total_ref, view_ref, other_ref, slice_ref, glob_ref = refs[:5]
    refs = refs[5:]
    if last:
        sharp_ref, *refs = refs
        z_ref, code_ref, acc_ref, sems, racc_ref = refs
    else:
        z_ref, code_ref, acc_ref, sems = refs
    rows = blocks[0][0].shape[0] - PAD
    each = n * rows
    own = GLOBALS * images
    width = z_ref.shape[1]
    step = pl.program_id(0)

    @pl.when(step == 0)
    def prepare():
        copies = block_copies(ids, blocks, rows, z_ref, code_ref, sems)
        for c in copies:
            c.start()
        span = other_ref.shape[1]
        if span % 128:
            feature = lax.broadcasted_iota(jnp.int32, (width, slice_ref.shape[1]), 0)
            column = lax.broadcasted_iota(jnp.int32, (width, slice_ref.shape[1]), 1)
            wanted = (ids[0] ^ (column // span)) * span + column % span
            chosen = jnp.where(feature == wanted, 1.0, 0.0).astype(bf16)
        base = 0
        for r in ready:
            glob_ref[base : base + r.shape[0], :] = r[...]
            base += r.shape[0]
        for k in range(m):
            at, to = slice(k * each, (k + 1) * each), slice(k * own, (k + 1) * own)
            loads = copies[k * (n + 1) : (k + 1) * (n + 1)]
            loads[n].wait()
            code = code_line(code_ref[k])
            view_ref[:, at] = code - 2.0 * jnp.floor(code * 0.5)
            mine, one, two = image_masks(code, images)
            picks = jnp.concatenate([one, two], axis=0)
            rest = jnp.concatenate([mine, mine], axis=0) - picks
            for c in loads[:n]:
                c.wait()
            z = z_ref[at, :]
            glob_ref[base + k * own : base + (k + 1) * own, :] = jnp.dot(
                picks.astype(bf16), z, preferred_element_type=f32
            ).astype(bf16)
            if span % 128:
                part = jnp.dot(z, chosen, preferred_element_type=f32).astype(bf16)
            else:
                spots = [pl.multiple_of((ids[0] ^ k) * span, span) for k in range(2)]
                part = jnp.concatenate([z_ref[at, pl.ds(p, span)] for p in spots], axis=1)
            slice_ref[at, :] = part
            other_ref[to, :] = jnp.dot(
                rest.astype(bf16), part[:, :span], preferred_element_type=f32
            )
        acc_ref[...] = jnp.zeros_like(acc_ref)
        if last:
            racc_ref[...] = jnp.zeros_like(racc_ref)

    for k, power_ref in enumerate(power_refs):
        at = slice(k * each, (k + 1) * each)
        scores = lax.dot_general(
            c_ref[...], z_ref[at, :], (((1,), (1,)), ((), ())), preferred_element_type=f32
        )
        power = jnp.exp(scores * (1.0 / temper))
        power_ref[...] = power.astype(bf16)
        acc_ref[:, at] += fold(power)
    if last:
        sharp = sharp_of(c_ref[...], glob_ref[...])
        sharp_ref[...] = sharp
        wide = sharp.astype(f32)
        col = 1.0 / jnp.sum(wide, axis=1, keepdims=True)
        racc_ref[...] += fold(wide * col.astype(bf16).astype(f32))

    @pl.when(step == steps - 1)
    def finish():
        base = 0
        for ref in carried:
            total_ref[:, : ref.shape[1]] = ref[...]
            base += ref.shape[1]
        total_ref[:, base : base + m * each] = jnp.sum(acc_ref[...], axis=0, keepdims=True)
        if last:
            total_ref[:, base + m * each :] = jnp.sum(racc_ref[...], axis=0, keepdims=True)


def powers(ids, blocks, ready, carried, last, unit_c, count, images, span, parts, place):
    m, n = len(blocks), len(blocks[0])
    rows, width = blocks[0][0].shape[0] - PAD, blocks[0][0].shape[1]
    crops_all = m * n * rows
    own = m * GLOBALS * images
    globs = own + sum(r.shape[0] for r in ready)
    sums = crops_all + sum(t.shape[1] for t in carried) + (globs if last else 0)
    tile = min(TILE, count, max(64, 2048 * 1024 // (crops_all + globs) // 64 * 64))
    while count % tile:
        tile -= 64
    steps = count // tile
    shapes = [
        *[((count, n * rows), bf16)] * m,
        ((1, sums), f32),
        ((1, crops_all), f32),
        ((own, span), f32),
        ((crops_all, parts * span), bf16),
        ((globs, width), bf16),
    ]
    out_specs = [pl.BlockSpec((tile, n * rows), lambda i, ids: (i, 0))] * m
    out_specs += [whole_out(s) for s, _ in shapes[m:]]
    scratch = [
        pltpu.VMEM((crops_all, width), bf16),
        pltpu.VMEM((m, PAD, n * rows // LINES), bf16),
        pltpu.VMEM((8, crops_all), f32),
        pltpu.SemaphoreType.DMA((m * n + m,)),
    ]
    if last:
        shapes.append(((count, globs), bf16))
        out_specs.append(pl.BlockSpec((tile, globs), lambda i, ids: (i, 0)))
        scratch.append(pltpu.VMEM((8, globs), f32))
    columns = crops_all + (globs if last else 0)
    return pl.pallas_call(
        functools.partial(power_kernel, m, n, len(ready), last, steps, images),
        out_shape=[place(s, d) for s, d in shapes[:m]]
        + [jax.ShapeDtypeStruct(s, d) for s, d in shapes[m : m + 5]]
        + [pltpu.VMEM(s, d) for s, d in shapes[m + 5 :]],
        grid_spec=pltpu.PrefetchScalarGridSpec(
            num_scalar_prefetch=1,
            grid=(steps,),
            in_specs=[pl.BlockSpec(memory_space=pltpu.HBM)] * (m * n)
            + [whole_spec(r) for r in [*ready, *carried]]
            + [pl.BlockSpec((tile, width), lambda i, ids: (i, 0))],
            out_specs=out_specs,
            scratch_shapes=scratch,
        ),
        compiler_params=params(globs),
        cost_estimate=cost(
            2 * columns * count * width, 2 * count * (columns + width), columns * count
        ),
        name="softmax_powers",
    )(ids, *[b for block in blocks for b in block], *ready, *carried, vmem(unit_c))


def flip(row, block):
    pieces = [row[:, j * block : (j + 1) * block] for j in range(row.shape[1] // block)]
    return jnp.concatenate([pieces[j ^ 1] for j in range(len(pieces))], axis=1)


def row_sum(refs, flips, start, size, block):
    parts = [r[:, start : start + size] for r in refs]
    return sum(flip(p, block) if turn else p for p, turn in zip(parts, flips))


def sharp_of(c, z):
    scores = lax.dot_general(c, z, (((1,), (1,)), ((), ())), preferred_element_type=f32)
    return jnp.exp(scores * (1.0 / sharpen)).astype(bf16)


def scale_pass_kernel(flips, start, steps, images, final, ids, *refs):
    p = len(flips)
    parts, sharp_ref, refs = refs[:p], refs[p], refs[p + 1 :]
    if final:
        m, n = final
        c_ref, blocks, refs = refs[0], refs[1 : 1 + m * n], refs[1 + m * n :]
        blocks = [blocks[k * n : (k + 1) * n] for k in range(m)]
        out_ref, w_ref, acc_ref, v_ref, scaled_ref, z_ref, code_ref, sems = refs
        rows = blocks[0][0].shape[0] - PAD
    else:
        out_ref, w_ref, acc_ref = refs
    own = GLOBALS * images
    total = sharp_ref.shape[1]
    step = pl.program_id(0)

    @pl.when(step == 0)
    def prepare():
        if final:
            for c in block_copies(ids, blocks, rows, z_ref, code_ref, sems):
                c.start()
            v_ref[...] = jnp.zeros_like(v_ref)
        scale = 1.0 / row_sum(parts, flips, start, total, own)
        w_ref[...] = to_rows(scale, 128).astype(bf16)
        acc_ref[...] = jnp.zeros_like(acc_ref)

    chunk = min(256, sharp_ref.shape[0])
    for j in range(sharp_ref.shape[0] // chunk):
        at = slice(j * chunk, (j + 1) * chunk)
        sharp = sharp_ref[at, :]
        col = 1.0 / jnp.dot(sharp, w_ref[...], preferred_element_type=f32)
        narrow = col.astype(bf16).astype(f32)
        for lane in range(total // 128):
            span = slice(lane * 128, (lane + 1) * 128)
            acc_ref[:, span] += fold(sharp[:, span].astype(f32) * narrow)
        if final:
            scaled_ref[at, :] = (c_ref[at, :].astype(f32) * col[:, :1]).astype(bf16)
    if final:
        v_ref[...] += lax.dot_general(
            sharp_ref[:, : m * own],
            scaled_ref[...],
            (((0,), (0,)), ((), ())),
            preferred_element_type=f32,
        )

    @pl.when(step == steps - 1)
    def finish():
        out_ref[:, :total] = jnp.sum(acc_ref[...], axis=0, keepdims=True)
        if final:
            for c in block_copies(ids, blocks, rows, z_ref, code_ref, sems):
                c.wait()
            each = n * rows
            for k in range(m):
                at = slice(k * each, (k + 1) * each)
                mine, one, two = image_masks(code_line(code_ref[k]), images)
                hits = lax.dot_general(
                    v_ref[k * own : (k + 1) * own, :].astype(bf16),
                    z_ref[at, :],
                    (((1,), (1,)), ((), ())),
                    preferred_element_type=f32,
                )
                first = jnp.sum(hits[:images] * (mine - one), axis=0, keepdims=True)
                second = jnp.sum(hits[images:] * (mine - two), axis=0, keepdims=True)
                base = total + k * each
                out_ref[:, base : base + each] = first
                base += m * each
                out_ref[:, base : base + each] = second


def scale_pass(ids, row_parts, flips, start, sharp, images, unit_c=None, blocks=None):
    count, total = sharp.shape
    tile = min(count, max(64, 1024 * 1024 // total))
    steps = count // tile
    size = total
    scratch = [pltpu.VMEM((total, 128), bf16), pltpu.VMEM((8, total), f32)]
    args = [*row_parts, vmem(sharp)]
    in_specs = [whole_spec(p) for p in row_parts]
    in_specs.append(pl.BlockSpec((tile, total), lambda i, ids: (i, 0)))
    final = None
    if unit_c is not None:
        m, n = final = len(blocks), len(blocks[0])
        rows, width = blocks[0][0].shape[0] - PAD, unit_c.shape[1]
        args += [vmem(unit_c)] + [b for block in blocks for b in block]
        in_specs.append(pl.BlockSpec((tile, width), lambda i, ids: (i, 0)))
        in_specs += [pl.BlockSpec(memory_space=pltpu.HBM)] * (m * n)
        size += 2 * m * n * rows
        scratch += [
            pltpu.VMEM((m * GLOBALS * images, width), f32),
            pltpu.VMEM((tile, width), bf16),
            pltpu.VMEM((m * n * rows, width), bf16),
            pltpu.VMEM((m, PAD, n * rows // LINES), bf16),
            pltpu.SemaphoreType.DMA((m * n + m,)),
        ]
    return pl.pallas_call(
        functools.partial(scale_pass_kernel, flips, start, steps, images, final),
        out_shape=jax.ShapeDtypeStruct((1, size), f32),
        grid_spec=pltpu.PrefetchScalarGridSpec(
            num_scalar_prefetch=1,
            grid=(steps,),
            in_specs=in_specs,
            out_specs=whole_out((1, size)),
            scratch_shapes=scratch,
        ),
        compiler_params=params(total),
        cost_estimate=cost(4 * total * count, 2 * total * count),
        name="sinkhorn_final" if final else "sinkhorn_pass",
    )(ids, *args)


def push_kernel(n, m, flips, block, cuts, *refs):
    p = len(flips)
    totals, refs = refs[:p], refs[p:]
    views, slices, powers_in, refs = refs[:m], refs[m : 2 * m], refs[2 * m : 2 * m + n], refs[2 * m + n :]
    sum_ref, near_ref, *aways, z_ref = refs
    step = pl.program_id(0)

    @pl.when(step == 0)
    def prepare():
        total = row_sum(totals, flips, 0, sum_ref.shape[1], block)
        sum_ref[...] = total
        width = slices[0].shape[1]
        base = 0
        for j in range(m):
            at = slice(base, base + slices[j].shape[0])
            base = at.stop
            coef = (GLOBALS - views[j][...]) / total[:, at] * (1.0 / temper)
            tall = to_rows(coef, min(128, width))
            if width > 128:
                tall = jnp.concatenate([tall] * (width // 128), axis=1)
            z_ref[at, :] = (slices[j][...].astype(f32) * tall).astype(bf16)

    out = 0.0
    for j in range(n):
        at = slice(j * block, (j + 1) * block)
        out += jnp.dot(powers_in[j][...], z_ref[at, :], preferred_element_type=f32)
    span = near_ref.shape[1]
    near_ref[...] = out[:, :span]
    away = out[:, span:].astype(bf16)
    for k, ref in enumerate(aways):

        @pl.when((step >= cuts[k]) & (step < cuts[k + 1]))
        def store(ref=ref):
            ref[...] = away


def push(totals, flips, block, views, power_list, slices, places):
    power_list = [pltpu.with_memory_space_constraint(p, q) for p, q in zip(power_list, places)]
    n, m = len(power_list), len(slices)
    count = power_list[0].shape[0]
    rows = n * block
    width = slices[0].shape[1]
    span = width // 2
    tile = max(64, min(1024, 4096 * 1024 // rows, count // 4))
    steps = count // tile
    cuts = (0, steps // 4, steps // 4 * 3, steps)
    sizes = [b - a for a, b in zip(cuts, cuts[1:])]
    row = (1, rows)
    tiles = pl.BlockSpec((tile, span), lambda i: (i, 0))
    return pl.pallas_call(
        functools.partial(push_kernel, n, m, flips, block, cuts),
        out_shape=[jax.ShapeDtypeStruct(row, f32), jax.ShapeDtypeStruct((count, span), f32)]
        + [jax.ShapeDtypeStruct((size * tile, span), bf16) for size in sizes],
        grid=(steps,),
        in_specs=[whole_spec(t) for t in [*totals, *views, *slices]]
        + [pl.BlockSpec((tile, block), lambda i: (i, 0)) for _ in power_list],
        out_specs=[whole_out(row), tiles]
        + [piece_spec((tile, span), a, size) for a, size in zip(cuts, sizes)],
        scratch_shapes=[pltpu.VMEM((rows, width), bf16)],
        compiler_params=params(rows // 4),
        cost_estimate=cost(2 * rows * count * width, 2 * rows * count),
        name="gradient_push",
    )(*totals, *views, *slices, *power_list)


def pull_kernel(flips, m, images, kept, cuts, ids, *refs):
    n = len(flips)
    before, last, others = refs[:n], refs[n : 2 * n], refs[2 * n : 2 * n + m]
    glob_ref, c_ref, refs = refs[2 * n + m], refs[2 * n + m + 1], refs[2 * n + m + 2 :]
    pieces, refs = refs[: len(cuts) - 1], refs[len(cuts) - 1 :]
    if kept:
        block_ref, sum_ref, sharp_ref, near_ref, out_ref, loss_ref, w_ref = refs
    else:
        _, out_ref, w_ref = refs
    span = out_ref.shape[0]
    own = GLOBALS * images
    step = pl.program_id(0)

    @pl.when(step == 0)
    def prepare():
        total = w_ref.shape[0]
        weight = 1.0 / row_sum(before, flips, 0, total, own)
        scale = (1.0 / temper) / row_sum(last, flips, 0, total, own)
        tall = to_rows(scale, 128)
        base = 0
        for other in others:
            at = slice(base, base + other.shape[0])
            w_ref[at, :span] = (other[...] * tall[at, :span]).astype(bf16)
            base += other.shape[0]
        w_ref[:, span:] = to_rows(weight, span).astype(bf16)
        if kept:
            rows = block_ref.shape[0] - PAD
            size = loss_ref.shape[1]
            code = code_line(block_ref[rows:, : size // LINES])
            mine = image_masks(code, images)[0]
            pairs = (last[0].shape[1] - total) // 2
            value = 0.0
            for k in range(2):
                product = row_sum(last, flips, total + k * pairs, pairs, size)[:, :size]
                factor = tall[k * images : (k + 1) * images, :1]
                value += product * jnp.sum(mine * factor, axis=0, keepdims=True)
            view = code - 2.0 * jnp.floor(code * 0.5)
            logs = jnp.log(sum_ref[:, :size]) - math.log(K)
            loss_ref[...] = logs * (GLOBALS - view) - value

    def finish(sharp, pushed):
        both = jnp.dot(sharp, w_ref[...], preferred_element_type=f32)
        grad = pushed - both[:, :span] / both[:, span:]
        out_ref[...] = grad.T

    if kept:

        @pl.when(step < kept)
        def stored():
            finish(sharp_ref[...], near_ref[...])

    @pl.when(step >= kept)
    def fresh():
        pushed = pieces[0][...]
        for k, piece in enumerate(pieces[1:], 1):
            pushed = jnp.where(step < kept + cuts[k], pushed, piece[...])
        finish(sharp_of(c_ref[...], glob_ref[...]), pushed.astype(f32))


def pull(ids, before, last, flips, images, others, globs, unit_c, pieces, first, own=None, grad=None):
    n, m = len(before), len(others)
    total = globs.shape[0]
    width, span = unit_c.shape[1], pieces[0].shape[1]
    half = unit_c.shape[0]
    tile = min(pieces[0].shape[0], max(128, 1024 * 1024 // total))
    steps = half // tile
    kept = steps if own else 0
    cuts = [0]
    for piece in pieces:
        cuts.append(cuts[-1] + piece.shape[0] // tile)
    start = steps + first // tile
    size = images * CROPS
    args = [*before, *last, *others, globs, vmem(unit_c), *pieces]
    in_specs = [whole_spec(a) for a in args[: 2 * n + m + 1]]
    in_specs.append(
        pl.BlockSpec((tile, width), lambda i, ids: (start - steps + jnp.maximum(i - kept, 0), 0))
    )
    in_specs += [
        piece_spec((tile, span), kept + a, b - a) for a, b in zip(cuts, cuts[1:])
    ]

    def spot(i, ids):
        place = jnp.where(i < kept, i, start + i - kept)
        return (0, ((place // steps) ^ ids[2]) * steps + place % steps)

    out_shape = [jax.ShapeDtypeStruct((span, 2 * half), f32)]
    out_specs = [pl.BlockSpec((span, tile), spot)]
    aliases = {}
    if own:
        block, sums, sharp, near = own
        args += [block, sums, vmem(sharp), near]
        in_specs += [
            whole_spec(block),
            whole_spec(sums),
            piece_spec((tile, total), 0, kept),
            piece_spec((tile, span), 0, kept),
        ]
        out_shape.append(jax.ShapeDtypeStruct((1, size), f32))
        out_specs.append(whole_out((1, size)))
    else:
        aliases = {len(args) + 1: 0}
        args.append(grad)
        in_specs.append(pl.BlockSpec(memory_space=pl.ANY))
    return pl.pallas_call(
        functools.partial(pull_kernel, flips, m, images, kept, tuple(cuts)),
        out_shape=out_shape,
        grid_spec=pltpu.PrefetchScalarGridSpec(
            num_scalar_prefetch=1,
            grid=(kept + cuts[-1],),
            in_specs=in_specs,
            out_specs=out_specs,
            scratch_shapes=[pltpu.VMEM((total, 2 * span), bf16)],
        ),
        input_output_aliases=aliases,
        compiler_params=params(total),
        cost_estimate=cost(
            (kept + cuts[-1]) * tile * total * (4 * span + width), 2 * total * half
        ),
        name="gradient_pull",
    )(ids, *args)


def swap(array, axes, sizes, offset):
    size = math.prod(sizes)
    return lax.ppermute(array, axes, [(i, i ^ offset) for i in range(size)])


def shards(sizes, embeddings, prototypes, crop_image, crop_view):
    n_batch, n_proto, n_sub = sizes
    n = n_proto * n_sub
    parts = 2
    width = embeddings.shape[1]
    crops_all = crop_image.shape[0]
    images = crop_image.shape[0] // CROPS
    count = prototypes.shape[0]
    half = count // parts
    span = width // n_batch
    own = GLOBALS * images

    batch = lax.axis_index("batch")
    place = lax.axis_index("proto") * n_sub + lax.axis_index("sub")
    ids = jnp.stack([batch, place, batch % parts, jnp.int32(images)]).astype(jnp.int32)

    lines = (LINES, crops_all // LINES)
    mine = crops(ids, embeddings, crop_image.reshape(lines), crop_view.reshape(lines))
    c_near, c_far = protos(ids, prototypes)

    def along(array, axis, offset):
        return swap(array, axis, (sizes[("batch", "proto", "sub").index(axis)],), offset)

    def chips(block):
        return [block] + [along(block, "proto", j) for j in range(1, n_proto)]

    def cores(found):
        return [b if k == 0 else along(b, "sub", k) for b in found for k in range(n_sub)]

    def pass_on(k):
        low = k & -k
        return along(mine if k == low else moved[k ^ low], "batch", low)

    moved = {0: mine}
    for k in range(1, n_batch - 1):
        moved[k] = pass_on(k)
    near = chips(mine)
    near, first, c_near, c_far = lax.optimization_barrier(
        (near, [moved[k] for k in range(1, n_batch - 1)], c_near, c_far)
    )
    near[0] = mine
    moved = dict(enumerate([mine, *first]))
    moved[n_batch - 1] = pass_on(n_batch - 1)
    blocks = [cores(near)]

    places = [pltpu.HBM] * (n_batch - KEPT) + [pltpu.VMEM] * KEPT
    power_list, views, others, slices = [], [], [], []

    def collect(found, m):
        power_list.extend(found[:m])
        total, *kept = found[m:]
        for store, new in zip((views, others, slices), kept):
            store.append(new)
        return total, kept[3:]

    total, (globs,) = collect(
        powers(ids, blocks[:1], [], [], False, c_near, half, images, span, parts, places[0]), 1
    )
    far = [chips(moved[k])[1:] for k in range(1, n_batch - 1)]
    moved[n_batch - 1], total = lax.optimization_barrier((moved[n_batch - 1], total))
    far.append(chips(moved[n_batch - 1])[1:])
    for k, found in enumerate(far, 1):
        found, total = lax.optimization_barrier((found, total))
        blocks.append(cores([moved[k], *found]))
        last = k + 1 == n_batch
        total, (globs, *rest) = collect(
            powers(
                ids, blocks[k:], [globs], [total], last, c_near, half, images, span, parts,
                places[k],
            ),
            1,
        )
    (sharp,) = rest

    flips = (False, False, True, True) if n_proto == 2 else (False, True)

    def chip_sum(row):
        if n_proto != 2 or n_sub != 2:
            return lax.psum(row, ("proto", "sub"))
        return row + along(row, "sub", 1)

    def everywhere(row):
        if n_proto != 2 or n_sub != 2:
            return [row, along(row, "batch", 1)]
        pair = (n_batch, n_proto)
        return [row] + [swap(row, ("batch", "proto"), pair, j) for j in (1, n_proto, n_proto + 1)]

    tokens = n_batch * crops_all
    firsts = everywhere(chip_sum(total))
    total, near, early, middle, late = push(
        firsts, flips, crops_all, views, power_list, slices, places
    )
    early = along(early, "batch", 1)
    row_parts, total = lax.optimization_barrier((firsts, total))

    start = tokens
    for step_index in range(ITERS - 2):
        row = chip_sum(scale_pass(ids, row_parts, flips, start, sharp, images))
        row, early = lax.optimization_barrier((row, early))
        row_parts, start = everywhere(row), 0
    before, middle = lax.optimization_barrier((row_parts, middle))
    middle = along(middle, "batch", 1)

    row = scale_pass(ids, before, flips, start, sharp, images, c_near, blocks[:parts])
    row, middle = lax.optimization_barrier((chip_sum(row), middle))
    last, late = lax.optimization_barrier((everywhere(row), late))
    late = along(late, "batch", 1)

    shared = (ids, before, last, flips, images, others, globs, c_far)
    grad, crop_loss = pull(*shared, [early, middle], 0, own=(mine, total, sharp, near))
    (grad,) = pull(*shared, [late], early.shape[0] + middle.shape[0], grad=grad)
    return (crop_loss.reshape(crops_all), grad)


def solution(mesh):
    sizes = tuple(mesh.shape[a] for a in ("batch", "proto", "sub"))
    placed = (
        P(("groups", "batch", "proto", "sub"), None),
        P(("groups", "proto", "sub"), None),
        P(("groups", "batch")),
        P(("groups", "batch")),
    )
    return jax.shard_map(
        functools.partial(shards, sizes),
        mesh=mesh,
        in_specs=placed,
        out_specs=(P(("groups", "batch")), P("batch", ("groups", "proto", "sub"))),
        check_vma=False,
    )
```

```python
import functools
import math

import jax
import jax.numpy as jnp
from jax import lax
from jax.experimental import pallas as pl
from jax.experimental.pallas import tpu as pltpu
from jax.sharding import PartitionSpec as P

K = 32768
CROPS = 8
GLOBALS = 2
ITERS = 3
PAD = 16
TILE = 1024
PROTO_TILE = 1024
KEPT = 2
LINES = 8
MIB = 1024 * 1024
SMALL, LARGE = 16, 44

sharpen = 0.05
temper = 0.1

f32 = jnp.float32
bf16 = jnp.bfloat16


def params(globs=0):
    return pltpu.CompilerParams(
        dimension_semantics=("arbitrary",),
        vmem_limit_bytes=(SMALL if globs <= 1024 else LARGE) * MIB,
    )


def whole_spec(array):
    zeros = (0,) * array.ndim
    return pl.BlockSpec(array.shape, lambda *_: zeros)


def whole_out(shape):
    zeros = (0,) * len(shape)
    return pl.BlockSpec(shape, lambda *_: zeros)


def piece_spec(shape, first, count):
    return pl.BlockSpec(shape, lambda i, *_: (jnp.clip(i - first, 0, count - 1), 0))


def unit(wide):
    factor = lax.rsqrt(jnp.mean(wide * wide, axis=-1, keepdims=True) + 1e-06) / math.sqrt(
        wide.shape[-1]
    )
    return (wide * factor).astype(bf16)


def to_rows(lane_vector, width):
    return jnp.broadcast_to(lane_vector, (128, lane_vector.shape[1])).T[:, :width]


def fold(values):
    return values.reshape(values.shape[0] // 8, 8, values.shape[1]).sum(0)


def hbm(array):
    return pltpu.with_memory_space_constraint(array, pltpu.HBM)


def vmem(array):
    return pltpu.with_memory_space_constraint(array, pltpu.VMEM)


def cost(flops, nbytes, trans=0):
    return pl.CostEstimate(flops=int(flops), bytes_accessed=int(nbytes), transcendentals=int(trans))


def crops_kernel(ids, emb_in, image_in, view_in, out_ref, emb_ref, image_ref, view_ref, sems):
    pairs = [(emb_in, emb_ref), (image_in, image_ref), (view_in, view_ref)]
    copies = [pltpu.make_async_copy(a, b, sems.at[k]) for k, (a, b) in enumerate(pairs)]
    for c in copies:
        c.start()
    for c in copies:
        c.wait()
    rows, width = emb_ref.shape
    out_ref[:rows, :] = unit(emb_ref[...].astype(f32))
    code = ((image_ref[...] - ids[0] * ids[3]) * 2 + view_ref[...]).astype(f32)
    code = jnp.concatenate([code, jnp.zeros((code.shape[0], width - code.shape[1]), f32)], axis=1)
    code = jnp.concatenate([code, jnp.zeros((PAD - code.shape[0], width), f32)], axis=0)
    out_ref[rows:, :] = code.astype(bf16)


def crops(ids, emb, image, view):
    rows, width = emb.shape
    shape = (rows + PAD, width)
    return pl.pallas_call(
        crops_kernel,
        out_shape=jax.ShapeDtypeStruct(shape, bf16),
        grid_spec=pltpu.PrefetchScalarGridSpec(
            num_scalar_prefetch=1,
            grid=(1,),
            in_specs=[pl.BlockSpec(memory_space=pltpu.HBM)] * 3,
            out_specs=whole_out(shape),
            scratch_shapes=[
                pltpu.VMEM(emb.shape, emb.dtype),
                pltpu.VMEM(image.shape, image.dtype),
                pltpu.VMEM(view.shape, view.dtype),
                pltpu.SemaphoreType.DMA((3,)),
            ],
        ),
        compiler_params=params(),
        name="unit_crops",
    )(ids, hbm(emb), hbm(image), hbm(view))


def protos_kernel(steps, ids, c_ref, near_ref, far_ref):
    out = unit(c_ref[...].astype(f32))

    @pl.when(pl.program_id(0) < steps)
    def near():
        near_ref[...] = out

    @pl.when(pl.program_id(0) >= steps)
    def far():
        far_ref[...] = out


def protos(ids, prototypes):
    count, width = prototypes.shape
    size = count // 2
    tile = min(PROTO_TILE, size)
    steps = size // tile
    return pl.pallas_call(
        functools.partial(protos_kernel, steps),
        out_shape=[pltpu.VMEM((size, width), bf16), pltpu.VMEM((size, width), bf16)],
        grid_spec=pltpu.PrefetchScalarGridSpec(
            num_scalar_prefetch=1,
            grid=(2 * steps,),
            in_specs=[
                pl.BlockSpec(
                    (tile, width),
                    lambda i, ids: (((i // steps) ^ ids[2]) * steps + i % steps, 0),
                )
            ],
            out_specs=[piece_spec((tile, width), 0, steps), piece_spec((tile, width), steps, steps)],
        ),
        compiler_params=params(),
        cost_estimate=cost(4 * count * width, 4 * count * width),
        name="unit_protos",
    )(ids, hbm(prototypes))


def image_masks(code, images):
    view = code - 2.0 * jnp.floor(code * 0.5)
    image = (code - view) * 0.5
    shape = (images, code.shape[1])
    row = lax.broadcasted_iota(jnp.int32, shape, 0).astype(f32)
    place = lax.broadcasted_iota(jnp.int32, shape, 1).astype(f32)
    mine = row == image
    glob = mine & (view > 0.5)
    first = jnp.min(jnp.where(glob, place, 1e9), axis=1, keepdims=True)
    one = glob & (place == first)
    two = glob & (place != first)
    return [m.astype(f32) for m in (mine, one, two)]


def code_line(lines):
    lines = lines.astype(f32)
    return jnp.concatenate([lines[j : j + 1, :] for j in range(LINES)], axis=1)


def block_copies(ids, blocks, rows, z_ref, code_ref, sems):
    m, n = len(blocks), len(blocks[0])
    lanes = code_ref.shape[2]
    copies = []
    for k in range(m):
        for j in range(n):
            at = pl.multiple_of(k * n * rows + (j ^ ids[1]) * rows, rows)
            copies.append((blocks[k][j].at[pl.ds(0, rows), :], z_ref.at[pl.ds(at, rows), :]))
        copies.append((blocks[k][0].at[pl.ds(rows, PAD), pl.ds(0, lanes)], code_ref.at[k]))
    return [pltpu.make_async_copy(a, b, sems.at[i]) for i, (a, b) in enumerate(copies)]


def power_kernel(m, n, early, last, steps, images, ids, *refs):
    blocks = [refs[k * n : (k + 1) * n] for k in range(m)]
    refs = refs[m * n :]
    ready, c_ref, refs = refs[: 2 * early], refs[2 * early], refs[2 * early + 1 :]
    ready, carried = ready[:early], ready[early:]
    power_refs, refs = refs[:m], refs[m:]
    total_ref, view_ref, other_ref, slice_ref, glob_ref = refs[:5]
    refs = refs[5:]
    if last:
        sharp_ref, *refs = refs
        z_ref, code_ref, acc_ref, sems, racc_ref = refs
    else:
        z_ref, code_ref, acc_ref, sems = refs
    rows = blocks[0][0].shape[0] - PAD
    each = n * rows
    own = GLOBALS * images
    width = z_ref.shape[1]
    step = pl.program_id(0)

    @pl.when(step == 0)
    def prepare():
        copies = block_copies(ids, blocks, rows, z_ref, code_ref, sems)
        for c in copies:
            c.start()
        span = other_ref.shape[1]
        if span % 128:
            feature = lax.broadcasted_iota(jnp.int32, (width, slice_ref.shape[1]), 0)
            column = lax.broadcasted_iota(jnp.int32, (width, slice_ref.shape[1]), 1)
            wanted = (ids[0] ^ (column // span)) * span + column % span
            chosen = jnp.where(feature == wanted, 1.0, 0.0).astype(bf16)
        base = 0
        for r in ready:
            glob_ref[base : base + r.shape[0], :] = r[...]
            base += r.shape[0]
        for k in range(m):
            at, to = slice(k * each, (k + 1) * each), slice(k * own, (k + 1) * own)
            loads = copies[k * (n + 1) : (k + 1) * (n + 1)]
            loads[n].wait()
            code = code_line(code_ref[k])
            view_ref[:, at] = code - 2.0 * jnp.floor(code * 0.5)
            mine, one, two = image_masks(code, images)
            picks = jnp.concatenate([one, two], axis=0)
            rest = jnp.concatenate([mine, mine], axis=0) - picks
            for c in loads[:n]:
                c.wait()
            z = z_ref[at, :]
            glob_ref[base + k * own : base + (k + 1) * own, :] = jnp.dot(
                picks.astype(bf16), z, preferred_element_type=f32
            ).astype(bf16)
            if span % 128:
                part = jnp.dot(z, chosen, preferred_element_type=f32).astype(bf16)
            else:
                spots = [pl.multiple_of((ids[0] ^ k) * span, span) for k in range(2)]
                part = jnp.concatenate([z_ref[at, pl.ds(p, span)] for p in spots], axis=1)
            slice_ref[at, :] = part
            other_ref[to, :] = jnp.dot(
                rest.astype(bf16), part[:, :span], preferred_element_type=f32
            )
        acc_ref[...] = jnp.zeros_like(acc_ref)
        if last:
            racc_ref[...] = jnp.zeros_like(racc_ref)

    chunk = min(256, c_ref.shape[0])
    for part in range(c_ref.shape[0] // chunk):
        at = slice(part * chunk, (part + 1) * chunk)
        if last:
            sharp = sharp_of(c_ref[at, :], glob_ref[...])
            sharp_ref[at, :] = sharp
            wide = sharp.astype(f32)
            col = 1.0 / jnp.sum(wide, axis=1, keepdims=True)
            racc_ref[...] += fold(wide * col.astype(bf16).astype(f32))
        for k, power_ref in enumerate(power_refs):
            to = slice(k * each, (k + 1) * each)
            scores = lax.dot_general(
                c_ref[at, :], z_ref[to, :], (((1,), (1,)), ((), ())), preferred_element_type=f32
            )
            power = jnp.exp(scores * (1.0 / temper))
            power_ref[at, :] = power.astype(bf16)
            acc_ref[:, to] += fold(power)

    @pl.when(step == steps - 1)
    def finish():
        base = 0
        for ref in carried:
            total_ref[:, : ref.shape[1]] = ref[...]
            base += ref.shape[1]
        total_ref[:, base : base + m * each] = jnp.sum(acc_ref[...], axis=0, keepdims=True)
        if last:
            total_ref[:, base + m * each :] = jnp.sum(racc_ref[...], axis=0, keepdims=True)


def powers(ids, blocks, ready, carried, last, unit_c, count, images, span, parts, place):
    m, n = len(blocks), len(blocks[0])
    rows, width = blocks[0][0].shape[0] - PAD, blocks[0][0].shape[1]
    crops_all = m * n * rows
    own = m * GLOBALS * images
    globs = own + sum(r.shape[0] for r in ready)
    sums = crops_all + sum(t.shape[1] for t in carried) + (globs if last else 0)
    tile = min(TILE, count, max(64, 2048 * 1024 // (crops_all + globs) // 64 * 64))
    while count % tile:
        tile -= 64
    steps = count // tile
    shapes = [
        *[((count, n * rows), bf16)] * m,
        ((1, sums), f32),
        ((1, crops_all), f32),
        ((own, span), f32),
        ((crops_all, parts * span), bf16),
        ((globs, width), bf16),
    ]
    out_specs = [pl.BlockSpec((tile, n * rows), lambda i, ids: (i, 0))] * m
    out_specs += [whole_out(s) for s, _ in shapes[m:]]
    scratch = [
        pltpu.VMEM((crops_all, width), bf16),
        pltpu.VMEM((m, PAD, n * rows // LINES), bf16),
        pltpu.VMEM((8, crops_all), f32),
        pltpu.SemaphoreType.DMA((m * n + m,)),
    ]
    if last:
        shapes.append(((count, globs), bf16))
        out_specs.append(pl.BlockSpec((tile, globs), lambda i, ids: (i, 0)))
        scratch.append(pltpu.VMEM((8, globs), f32))
    columns = crops_all + (globs if last else 0)
    return pl.pallas_call(
        functools.partial(power_kernel, m, n, len(ready), last, steps, images),
        out_shape=[place(s, d) for s, d in shapes[:m]]
        + [jax.ShapeDtypeStruct(s, d) for s, d in shapes[m : m + 5]]
        + [pltpu.VMEM(s, d) for s, d in shapes[m + 5 :]],
        grid_spec=pltpu.PrefetchScalarGridSpec(
            num_scalar_prefetch=1,
            grid=(steps,),
            in_specs=[pl.BlockSpec(memory_space=pltpu.HBM)] * (m * n)
            + [whole_spec(r) for r in [*ready, *carried]]
            + [pl.BlockSpec((tile, width), lambda i, ids: (i, 0))],
            out_specs=out_specs,
            scratch_shapes=scratch,
        ),
        compiler_params=params(globs),
        cost_estimate=cost(
            2 * columns * count * width, 2 * count * (columns + width), columns * count
        ),
        name="softmax_powers",
    )(ids, *[b for block in blocks for b in block], *ready, *carried, vmem(unit_c))


def flip(row, block):
    pieces = [row[:, j * block : (j + 1) * block] for j in range(row.shape[1] // block)]
    return jnp.concatenate([pieces[j ^ 1] for j in range(len(pieces))], axis=1)


def row_sum(refs, flips, start, size, block):
    parts = [r[:, start : start + size] for r in refs]
    return sum(flip(p, block) if turn else p for p, turn in zip(parts, flips))


def sharp_of(c, z):
    scores = lax.dot_general(c, z, (((1,), (1,)), ((), ())), preferred_element_type=f32)
    return jnp.exp(scores * (1.0 / sharpen)).astype(bf16)


def scale_pass_kernel(flips, start, steps, images, final, ids, *refs):
    p = len(flips)
    parts, sharp_ref, refs = refs[:p], refs[p], refs[p + 1 :]
    if final:
        m, n = final
        c_ref, blocks, refs = refs[0], refs[1 : 1 + m * n], refs[1 + m * n :]
        blocks = [blocks[k * n : (k + 1) * n] for k in range(m)]
        out_ref, w_ref, acc_ref, v_ref, scaled_ref, z_ref, code_ref, sems = refs
        rows = blocks[0][0].shape[0] - PAD
    else:
        out_ref, w_ref, acc_ref = refs
    own = GLOBALS * images
    total = sharp_ref.shape[1]
    step = pl.program_id(0)

    @pl.when(step == 0)
    def prepare():
        if final:
            for c in block_copies(ids, blocks, rows, z_ref, code_ref, sems):
                c.start()
            v_ref[...] = jnp.zeros_like(v_ref)
        scale = 1.0 / row_sum(parts, flips, start, total, own)
        w_ref[...] = to_rows(scale, 128).astype(bf16)
        acc_ref[...] = jnp.zeros_like(acc_ref)

    chunk = min(256, sharp_ref.shape[0])
    for j in range(sharp_ref.shape[0] // chunk):
        at = slice(j * chunk, (j + 1) * chunk)
        sharp = sharp_ref[at, :]
        col = 1.0 / jnp.dot(sharp, w_ref[...], preferred_element_type=f32)
        narrow = col.astype(bf16).astype(f32)
        for lane in range(total // 128):
            span = slice(lane * 128, (lane + 1) * 128)
            acc_ref[:, span] += fold(sharp[:, span].astype(f32) * narrow)
        if final:
            scaled_ref[at, :] = (c_ref[at, :].astype(f32) * col[:, :1]).astype(bf16)
    if final:
        v_ref[...] += lax.dot_general(
            sharp_ref[:, : m * own],
            scaled_ref[...],
            (((0,), (0,)), ((), ())),
            preferred_element_type=f32,
        )

    @pl.when(step == steps - 1)
    def finish():
        out_ref[:, :total] = jnp.sum(acc_ref[...], axis=0, keepdims=True)
        if final:
            for c in block_copies(ids, blocks, rows, z_ref, code_ref, sems):
                c.wait()
            each = n * rows
            for k in range(m):
                at = slice(k * each, (k + 1) * each)
                mine, one, two = image_masks(code_line(code_ref[k]), images)
                hits = lax.dot_general(
                    v_ref[k * own : (k + 1) * own, :].astype(bf16),
                    z_ref[at, :],
                    (((1,), (1,)), ((), ())),
                    preferred_element_type=f32,
                )
                first = jnp.sum(hits[:images] * (mine - one), axis=0, keepdims=True)
                second = jnp.sum(hits[images:] * (mine - two), axis=0, keepdims=True)
                base = total + k * each
                out_ref[:, base : base + each] = first
                base += m * each
                out_ref[:, base : base + each] = second


def scale_pass(ids, row_parts, flips, start, sharp, images, unit_c=None, blocks=None):
    count, total = sharp.shape
    tile = min(count, max(64, 1024 * 1024 // total))
    steps = count // tile
    size = total
    scratch = [pltpu.VMEM((total, 128), bf16), pltpu.VMEM((8, total), f32)]
    args = [*row_parts, vmem(sharp)]
    in_specs = [whole_spec(p) for p in row_parts]
    in_specs.append(pl.BlockSpec((tile, total), lambda i, ids: (i, 0)))
    final = None
    if unit_c is not None:
        m, n = final = len(blocks), len(blocks[0])
        rows, width = blocks[0][0].shape[0] - PAD, unit_c.shape[1]
        args += [vmem(unit_c)] + [b for block in blocks for b in block]
        in_specs.append(pl.BlockSpec((tile, width), lambda i, ids: (i, 0)))
        in_specs += [pl.BlockSpec(memory_space=pltpu.HBM)] * (m * n)
        size += 2 * m * n * rows
        scratch += [
            pltpu.VMEM((m * GLOBALS * images, width), f32),
            pltpu.VMEM((tile, width), bf16),
            pltpu.VMEM((m * n * rows, width), bf16),
            pltpu.VMEM((m, PAD, n * rows // LINES), bf16),
            pltpu.SemaphoreType.DMA((m * n + m,)),
        ]
    return pl.pallas_call(
        functools.partial(scale_pass_kernel, flips, start, steps, images, final),
        out_shape=jax.ShapeDtypeStruct((1, size), f32),
        grid_spec=pltpu.PrefetchScalarGridSpec(
            num_scalar_prefetch=1,
            grid=(steps,),
            in_specs=in_specs,
            out_specs=whole_out((1, size)),
            scratch_shapes=scratch,
        ),
        compiler_params=params(total),
        cost_estimate=cost(4 * total * count, 2 * total * count),
        name="sinkhorn_final" if final else "sinkhorn_pass",
    )(ids, *args)


def push_kernel(n, m, flips, block, cuts, *refs):
    p = len(flips)
    totals, refs = refs[:p], refs[p:]
    views, slices, powers_in, refs = refs[:m], refs[m : 2 * m], refs[2 * m : 2 * m + n], refs[2 * m + n :]
    sum_ref, near_ref, *aways, z_ref = refs
    step = pl.program_id(0)

    @pl.when(step == 0)
    def prepare():
        total = row_sum(totals, flips, 0, sum_ref.shape[1], block)
        sum_ref[...] = total
        width = slices[0].shape[1]
        base = 0
        for j in range(m):
            at = slice(base, base + slices[j].shape[0])
            base = at.stop
            coef = (GLOBALS - views[j][...]) / total[:, at] * (1.0 / temper)
            tall = to_rows(coef, min(128, width))
            if width > 128:
                tall = jnp.concatenate([tall] * (width // 128), axis=1)
            z_ref[at, :] = (slices[j][...].astype(f32) * tall).astype(bf16)

    out = 0.0
    for j in range(n):
        at = slice(j * block, (j + 1) * block)
        out += jnp.dot(powers_in[j][...], z_ref[at, :], preferred_element_type=f32)
    span = near_ref.shape[1]
    near_ref[...] = out[:, :span]
    away = out[:, span:].astype(bf16)
    for k, ref in enumerate(aways):

        @pl.when((step >= cuts[k]) & (step < cuts[k + 1]))
        def store(ref=ref):
            ref[...] = away


def push(totals, flips, block, views, power_list, slices, places):
    power_list = [pltpu.with_memory_space_constraint(p, q) for p, q in zip(power_list, places)]
    n, m = len(power_list), len(slices)
    count = power_list[0].shape[0]
    rows = n * block
    width = slices[0].shape[1]
    span = width // 2
    tile = max(64, min(1024, 4096 * 1024 // rows, count // 4))
    steps = count // tile
    cuts = (0, steps // 4, steps // 4 * 3, steps)
    sizes = [b - a for a, b in zip(cuts, cuts[1:])]
    row = (1, rows)
    tiles = pl.BlockSpec((tile, span), lambda i: (i, 0))
    return pl.pallas_call(
        functools.partial(push_kernel, n, m, flips, block, cuts),
        out_shape=[jax.ShapeDtypeStruct(row, f32), jax.ShapeDtypeStruct((count, span), f32)]
        + [jax.ShapeDtypeStruct((size * tile, span), bf16) for size in sizes],
        grid=(steps,),
        in_specs=[whole_spec(t) for t in [*totals, *views, *slices]]
        + [pl.BlockSpec((tile, block), lambda i: (i, 0)) for _ in power_list],
        out_specs=[whole_out(row), tiles]
        + [piece_spec((tile, span), a, size) for a, size in zip(cuts, sizes)],
        scratch_shapes=[pltpu.VMEM((rows, width), bf16)],
        compiler_params=params(rows // 4),
        cost_estimate=cost(2 * rows * count * width, 2 * rows * count),
        name="gradient_push",
    )(*totals, *views, *slices, *power_list)


def pull_kernel(flips, m, images, kept, cuts, ids, *refs):
    n = len(flips)
    before, last, others = refs[:n], refs[n : 2 * n], refs[2 * n : 2 * n + m]
    glob_ref, c_ref, refs = refs[2 * n + m], refs[2 * n + m + 1], refs[2 * n + m + 2 :]
    pieces, refs = refs[: len(cuts) - 1], refs[len(cuts) - 1 :]
    if kept:
        block_ref, sum_ref, sharp_ref, near_ref, out_ref, loss_ref, w_ref = refs
    else:
        _, out_ref, w_ref = refs
    span = out_ref.shape[0]
    own = GLOBALS * images
    step = pl.program_id(0)

    @pl.when(step == 0)
    def prepare():
        total = w_ref.shape[0]
        weight = 1.0 / row_sum(before, flips, 0, total, own)
        scale = (1.0 / temper) / row_sum(last, flips, 0, total, own)
        tall = to_rows(scale, 128)
        base = 0
        for other in others:
            at = slice(base, base + other.shape[0])
            w_ref[at, :span] = (other[...] * tall[at, :span]).astype(bf16)
            base += other.shape[0]
        w_ref[:, span:] = to_rows(weight, span).astype(bf16)
        if kept:
            rows = block_ref.shape[0] - PAD
            size = loss_ref.shape[1]
            code = code_line(block_ref[rows:, : size // LINES])
            mine = image_masks(code, images)[0]
            pairs = (last[0].shape[1] - total) // 2
            value = 0.0
            for k in range(2):
                product = row_sum(last, flips, total + k * pairs, pairs, size)[:, :size]
                factor = tall[k * images : (k + 1) * images, :1]
                value += product * jnp.sum(mine * factor, axis=0, keepdims=True)
            view = code - 2.0 * jnp.floor(code * 0.5)
            logs = jnp.log(sum_ref[:, :size]) - math.log(K)
            loss_ref[...] = logs * (GLOBALS - view) - value

    def finish(sharp, pushed):
        both = jnp.dot(sharp, w_ref[...], preferred_element_type=f32)
        grad = pushed - both[:, :span] / both[:, span:]
        out_ref[...] = grad.T

    if kept:

        @pl.when(step < kept)
        def stored():
            finish(sharp_ref[...], near_ref[...])

    @pl.when(step >= kept)
    def fresh():
        pushed = pieces[0][...]
        for k, piece in enumerate(pieces[1:], 1):
            pushed = jnp.where(step < kept + cuts[k], pushed, piece[...])
        finish(sharp_of(c_ref[...], glob_ref[...]), pushed.astype(f32))


def pull(ids, before, last, flips, images, others, globs, unit_c, pieces, first, own=None, grad=None):
    n, m = len(before), len(others)
    total = globs.shape[0]
    width, span = unit_c.shape[1], pieces[0].shape[1]
    half = unit_c.shape[0]
    tile = min(pieces[0].shape[0], max(128, 1024 * 1024 // total))
    steps = half // tile
    kept = steps if own else 0
    cuts = [0]
    for piece in pieces:
        cuts.append(cuts[-1] + piece.shape[0] // tile)
    start = steps + first // tile
    size = images * CROPS
    args = [*before, *last, *others, globs, vmem(unit_c), *pieces]
    in_specs = [whole_spec(a) for a in args[: 2 * n + m + 1]]
    in_specs.append(
        pl.BlockSpec((tile, width), lambda i, ids: (start - steps + jnp.maximum(i - kept, 0), 0))
    )
    in_specs += [
        piece_spec((tile, span), kept + a, b - a) for a, b in zip(cuts, cuts[1:])
    ]

    def spot(i, ids):
        place = jnp.where(i < kept, i, start + i - kept)
        return (0, ((place // steps) ^ ids[2]) * steps + place % steps)

    out_shape = [jax.ShapeDtypeStruct((span, 2 * half), f32)]
    out_specs = [pl.BlockSpec((span, tile), spot)]
    aliases = {}
    if own:
        block, sums, sharp, near = own
        args += [block, sums, vmem(sharp), near]
        in_specs += [
            whole_spec(block),
            whole_spec(sums),
            piece_spec((tile, total), 0, kept),
            piece_spec((tile, span), 0, kept),
        ]
        out_shape.append(jax.ShapeDtypeStruct((1, size), f32))
        out_specs.append(whole_out((1, size)))
    else:
        aliases = {len(args) + 1: 0}
        args.append(grad)
        in_specs.append(pl.BlockSpec(memory_space=pl.ANY))
    return pl.pallas_call(
        functools.partial(pull_kernel, flips, m, images, kept, tuple(cuts)),
        out_shape=out_shape,
        grid_spec=pltpu.PrefetchScalarGridSpec(
            num_scalar_prefetch=1,
            grid=(kept + cuts[-1],),
            in_specs=in_specs,
            out_specs=out_specs,
            scratch_shapes=[pltpu.VMEM((total, 2 * span), bf16)],
        ),
        input_output_aliases=aliases,
        compiler_params=params(total),
        cost_estimate=cost(
            (kept + cuts[-1]) * tile * total * (4 * span + width), 2 * total * half
        ),
        name="gradient_pull",
    )(ids, *args)


def swap(array, axes, sizes, offset):
    size = math.prod(sizes)
    return lax.ppermute(array, axes, [(i, i ^ offset) for i in range(size)])


def shards(sizes, embeddings, prototypes, crop_image, crop_view):
    n_batch, n_proto, n_sub = sizes
    n = n_proto * n_sub
    parts = 2
    width = embeddings.shape[1]
    crops_all = crop_image.shape[0]
    images = crop_image.shape[0] // CROPS
    count = prototypes.shape[0]
    half = count // parts
    span = width // n_batch
    own = GLOBALS * images

    batch = lax.axis_index("batch")
    place = lax.axis_index("proto") * n_sub + lax.axis_index("sub")
    ids = jnp.stack([batch, place, batch % parts, jnp.int32(images)]).astype(jnp.int32)

    lines = (LINES, crops_all // LINES)
    mine = crops(ids, embeddings, crop_image.reshape(lines), crop_view.reshape(lines))
    c_near, c_far = protos(ids, prototypes)

    def along(array, axis, offset):
        return swap(array, axis, (sizes[("batch", "proto", "sub").index(axis)],), offset)

    def chips(block):
        return [block] + [along(block, "proto", j) for j in range(1, n_proto)]

    def cores(found):
        return [b if k == 0 else along(b, "sub", k) for b in found for k in range(n_sub)]

    def pass_on(k):
        low = k & -k
        return along(mine if k == low else moved[k ^ low], "batch", low)

    moved = {0: mine}
    for k in range(1, n_batch - 1):
        moved[k] = pass_on(k)
    near = chips(mine)
    near, first, c_near, c_far = lax.optimization_barrier(
        (near, [moved[k] for k in range(1, n_batch - 1)], c_near, c_far)
    )
    near[0] = mine
    moved = dict(enumerate([mine, *first]))
    moved[n_batch - 1] = pass_on(n_batch - 1)
    blocks = [cores(near)]

    places = [pltpu.HBM] * (n_batch - KEPT) + [pltpu.VMEM] * KEPT
    power_list, views, others, slices = [], [], [], []

    def collect(found, m):
        power_list.extend(found[:m])
        total, *kept = found[m:]
        for store, new in zip((views, others, slices), kept):
            store.append(new)
        return total, kept[3:]

    total, (globs,) = collect(
        powers(ids, blocks[:1], [], [], False, c_near, half, images, span, parts, places[0]), 1
    )
    far = [chips(moved[k])[1:] for k in range(1, n_batch - 1)]
    moved[n_batch - 1], total = lax.optimization_barrier((moved[n_batch - 1], total))
    far.append(chips(moved[n_batch - 1])[1:])
    for k, found in enumerate(far, 1):
        found, total = lax.optimization_barrier((found, total))
        blocks.append(cores([moved[k], *found]))
        last = k + 1 == n_batch
        total, (globs, *rest) = collect(
            powers(
                ids, blocks[k:], [globs], [total], last, c_near, half, images, span, parts,
                places[k],
            ),
            1,
        )
    (sharp,) = rest

    flips = (False, False, True, True) if n_proto == 2 else (False, True)

    def chip_sum(row):
        if n_proto != 2 or n_sub != 2:
            return lax.psum(row, ("proto", "sub"))
        return row + along(row, "sub", 1)

    def everywhere(row):
        if n_proto != 2 or n_sub != 2:
            return [row, along(row, "batch", 1)]
        pair = (n_batch, n_proto)
        return [row] + [swap(row, ("batch", "proto"), pair, j) for j in (1, n_proto, n_proto + 1)]

    tokens = n_batch * crops_all
    firsts = everywhere(chip_sum(total))
    total, near, early, middle, late = push(
        firsts, flips, crops_all, views, power_list, slices, places
    )
    early = along(early, "batch", 1)
    row_parts, total = lax.optimization_barrier((firsts, total))

    start = tokens
    for step_index in range(ITERS - 2):
        row = chip_sum(scale_pass(ids, row_parts, flips, start, sharp, images))
        row, early = lax.optimization_barrier((row, early))
        row_parts, start = everywhere(row), 0
    before, middle = lax.optimization_barrier((row_parts, middle))
    middle = along(middle, "batch", 1)

    row = scale_pass(ids, before, flips, start, sharp, images, c_near, blocks[:parts])
    row, middle = lax.optimization_barrier((chip_sum(row), middle))
    last, late = lax.optimization_barrier((everywhere(row), late))
    late = along(late, "batch", 1)

    shared = (ids, before, last, flips, images, others, globs, c_far)
    grad, crop_loss = pull(*shared, [early, middle], 0, own=(mine, total, sharp, near))
    (grad,) = pull(*shared, [late], early.shape[0] + middle.shape[0], grad=grad)
    return (crop_loss.reshape(crops_all), grad)


def solution(mesh):
    sizes = tuple(mesh.shape[a] for a in ("batch", "proto", "sub"))
    placed = (
        P(("groups", "batch", "proto", "sub"), None),
        P(("groups", "proto", "sub"), None),
        P(("groups", "batch")),
        P(("groups", "batch")),
    )
    return jax.shard_map(
        functools.partial(shards, sizes),
        mesh=mesh,
        in_specs=placed,
        out_specs=(P(("groups", "batch")), P("batch", ("groups", "proto", "sub"))),
        check_vma=False,
    )
```
